128 devices in a mesh: dp: 32 (over x, y, core), pipe: 4 (over z).
Axes of the slice: x: 4, y: 4, z: 4, core: 2. Of those that a mesh axis runs over, the one named last changes fastest.
Arguments:
- student_in: bfloat16 [4096, 8192], P('dp', 'pipe'), may hold values from -6 to 6
- value_weight: bfloat16 [4, 8192, 512], P('pipe'), may hold values from -0.0625 to 0.0625
- folded_out: bfloat16 [4, 512, 8192], P('pipe'), may hold values from -0.25 to 0.25
- norm_gain: bfloat16 [4, 8192], P('pipe'), may hold values from 0.5 to 1.5
- proj: bfloat16 [8192, 16384], P('pipe', 'dp'), may hold values from -0.0625 to 0.0625
- teacher_codes: bfloat16 [4096, 16384], P('dp'), may hold values from -12 to 12
- teacher_scales: bfloat16 [4096], P('dp'), may hold values from 0.5 to 3
- perm: int32 [4096], replicated, may hold values from 0 to 4095, each once
Outputs:
- grad_proj: bfloat16 [8192, 16384], P('pipe', 'dp')
- loss: float32 [], replicated
The draws below stay inside these ranges and needn't reach their ends.
Inputs may be any that keep to these rules, and one draw needn't show every extreme that they name: perm names every store row exactly once.
All inputs are finite; a program needn't handle non-finite values.
Results may differ from the reference program's by a relative error of at most 0.018.
Values may be sent and summed in bfloat16 or wider, within the bound.
A program may use at most 192 MiB of HBM per device.

```python
import math
import jax
import jax.numpy as jnp
from jax import lax

D = 8192
DT = 16384
HEAD = 512
TOKENS = 4096
LAYERS = 4


def column_ramp(low, ratio):
    column = jnp.arange(DT, dtype=jnp.float32) / (DT - 1)
    return low * jnp.exp(jnp.log(ratio) * column)


def draw_teacher_codes(key, part):
    key = jax.random.fold_in(key, 11)
    base = jnp.clip(jax.random.normal(key, (TOKENS, DT), jnp.float32), -6.0, 6.0)
    ramp = column_ramp(0.5, 4.0)
    return (base * ramp[None, :]).astype(jnp.bfloat16)


def levels(stream_key, shape, cuts, smallest, largest):
    def one(position, blocks):
        heights = jax.random.uniform(jax.random.fold_in(jax.random.fold_in(stream_key, 6), position), (blocks,), jnp.float32, smallest / len(cuts), largest / len(cuts))
        return jnp.repeat(jnp.exp(heights), shape[position] // blocks).reshape((-1,) + (1,) * (len(shape) - position - 1))

    level = one(*cuts[0])
    for cut in cuts[1:]:
        level = level * one(*cut)
    return level


def gaussian(own_key, extent, scale, reach, pieces=(), kind=jnp.bfloat16):
    drawn = jax.random.normal(own_key, extent, jnp.float32) * scale
    if len(pieces) > 0:
        drawn = levels(own_key, extent, pieces, -0.22, 0.18) * drawn
    return jnp.clip(drawn, min=-reach, max=reach).astype(kind)


def setup_inputs(seed: int = 0) -> dict:
    keys = jax.random.split(jax.random.key(seed), 9)
    return {
        "student_in": gaussian(keys[0], (TOKENS, D), 1.0, 6.0, ((0, 32), (1, 4))),
        "value_weight": gaussian(keys[1], (LAYERS, D, HEAD), D ** -0.5, 0.0625, ((0, 4),)),
        "folded_out": gaussian(keys[2], (LAYERS, HEAD, D), HEAD ** -0.5, 0.25, ((0, 4),)),
        "norm_gain": jnp.clip(1.0 + 0.1 * jax.random.normal(keys[3], (LAYERS, D), jnp.float32), 0.5, 1.5).astype(jnp.bfloat16),
        "proj": gaussian(keys[4], (D, DT), D ** -0.5, 0.0625, ((0, 4), (1, 32))),
        "teacher_codes": draw_teacher_codes(jax.random.fold_in(keys[8], 71), 0),
        "teacher_scales": jnp.clip(jnp.exp(math.log(3.0) - 1.7917595 * jax.random.uniform(keys[6], (TOKENS,), jnp.float32) ** levels(keys[6], (TOKENS,), ((0, 32),), -0.2, 0.2)), 0.5, 3.0).astype(jnp.bfloat16),
        "perm": jax.random.permutation(keys[7], TOKENS).astype(jnp.int32),
    }


def norm_rows(hidden, gain):
    values = hidden.astype(jnp.float32)
    scale = lax.rsqrt(lax.optimization_barrier(jnp.mean(values * values, axis=-1, keepdims=True)) + 1e-05)
    return (values * scale * gain.astype(jnp.float32)).astype(jnp.bfloat16)

def reference(student_in, value_weight, folded_out, norm_gain, proj, teacher_codes, teacher_scales, perm):
    hidden = student_in
    for layer in range(LAYERS):
        normed = norm_rows(hidden, norm_gain[layer])
        values = jnp.dot(normed, value_weight[layer], preferred_element_type=jnp.float32).astype(jnp.bfloat16)
        branch = jnp.dot(values, folded_out[layer], preferred_element_type=jnp.float32)
        hidden = (hidden.astype(jnp.float32) + branch).astype(jnp.bfloat16)
    output = jnp.dot(hidden, proj, preferred_element_type=jnp.float32)
    target = teacher_codes[perm].astype(jnp.float32) * teacher_scales[perm].astype(jnp.float32)[:, None]
    diff = output - target
    loss = 0.5 * jnp.sum(diff * diff) / (TOKENS * DT)
    grad_rows = (diff * (1.0 / math.sqrt(TOKENS))).astype(jnp.bfloat16)
    grad_proj = lax.dot_general(hidden, grad_rows, (((0,), (0,)), ((), ())), preferred_element_type=jnp.float32)
    return (grad_proj.astype(jnp.bfloat16), loss)
```

```python
import functools
import math

import jax
import jax.numpy as jnp
from jax import lax
from jax.experimental import pallas as pl
from jax.experimental.pallas import tpu as pltpu
from jax.sharding import PartitionSpec as P

MESH = pl.DeviceIdType.MESH
SIDE = 4
CHIPS = SIDE * SIDE


def place(dp):
    core = lax.rem(dp, 2)
    chip = dp // 2
    return chip // SIDE, lax.rem(chip, SIDE), core


def cycle_position(x, y, core):
    return SIDE * (y + core * (x - y)) + lax.rem(x + y, SIDE)


def cycle_device(position, core):
    major = position // SIDE
    minor = lax.rem(lax.rem(position, SIDE) - major + SIDE, SIDE)
    x = minor + core * (major - minor)
    y = major + core * (minor - major)
    return (x * SIDE + y) * 2 + core


def wide_kernel(
    inv_root,
    h_ref,
    proj_ref,
    target_ref,
    grad_ref,
    loss_ref,
    held,
    total,
    y_own,
    y_keep,
    out1,
    in1,
    out2,
    in2,
    rows_g,
    own_sem,
    ring_send,
    ring_recv,
    side_send,
    side_recv,
    sum1_send,
    sum1_recv,
    sum2_send,
    sum2_recv,
    rows1_send,
    rows1_recv,
    rows2_send,
    rows2_recv,
):
    dp = lax.axis_index("dp")
    z = lax.axis_index("pipe")
    x, y, core = place(dp)
    here = cycle_position(x, y, core)
    after = cycle_device(lax.rem(here + 1, CHIPS), core)
    before = cycle_device(lax.rem(here + CHIPS - 1, CHIPS), core)
    sibling = dp + 1 - 2 * core
    za = z + 1 - 2 * lax.rem(z, 2)
    zb = 3 - z
    steps = CHIPS
    part = h_ref.shape[0] // 2
    block = 4 * part
    half = block // 2
    zpair = (za, zb)
    ring = (after, before)

    barrier = pltpu.get_barrier_semaphore()
    for device in ((after, z), (before, z), (sibling, z), (dp, za), (dp, zb)):
        pl.semaphore_signal(barrier, inc=1, device_id=device, device_id_type=MESH)
    pl.semaphore_wait(barrier, 5)

    mine = pl.multiple_of(core * 2 * part, 2 * part)
    theirs = pl.multiple_of((1 - core) * 2 * part, 2 * part)

    def own_copy():
        return pltpu.make_async_copy(h_ref, held.at[0, pl.ds(mine, 2 * part)], own_sem)

    def ring_copy(s, way):
        rows = pl.ds(pl.multiple_of(mine + way * part, part), part)
        return pltpu.make_async_remote_copy(
            src_ref=held.at[s, rows],
            dst_ref=held.at[s + 1, rows],
            send_sem=ring_send.at[s, way],
            recv_sem=ring_recv.at[s + 1, way],
            device_id=(ring[way], z),
            device_id_type=MESH,
        )

    def ring_arrival(s, way):
        rows = pl.ds(pl.multiple_of(mine + way * part, part), part)
        return pltpu.make_async_remote_copy(
            src_ref=held.at[s, rows],
            dst_ref=held.at[s, rows],
            send_sem=ring_send.at[s, way],
            recv_sem=ring_recv.at[s, way],
            device_id=(ring[way], z),
            device_id_type=MESH,
        )

    def side_copy(s, way, start):
        rows = pl.ds(pl.multiple_of(start + way * part, part), part)
        return pltpu.make_async_remote_copy(
            src_ref=held.at[s, rows],
            dst_ref=held.at[s, rows],
            send_sem=side_send.at[s, way],
            recv_sem=side_recv.at[s, way],
            device_id=(sibling, z),
            device_id_type=MESH,
        )

    def sum1_copy(s, k):
        return pltpu.make_async_remote_copy(
            src_ref=out1.at[s, k],
            dst_ref=in1.at[s, k],
            send_sem=sum1_send.at[s, k],
            recv_sem=sum1_recv.at[s, k],
            device_id=(dp, zpair[k]),
            device_id_type=MESH,
        )

    def sum2_copy(s, k):
        return pltpu.make_async_remote_copy(
            src_ref=out2.at[s, k],
            dst_ref=in2.at[s, k],
            send_sem=sum2_send.at[s, k],
            recv_sem=sum2_recv.at[s, k],
            device_id=(dp, zpair[1 - k]),
            device_id_type=MESH,
        )

    def rows1_copy(s, k, quarter):
        return pltpu.make_async_remote_copy(
            src_ref=rows_g.at[s, quarter],
            dst_ref=rows_g.at[s, quarter],
            send_sem=rows1_send.at[s, k],
            recv_sem=rows1_recv.at[s, k],
            device_id=(dp, zpair[k]),
            device_id_type=MESH,
        )

    def rows2_copy(s, k, quarter):
        rows = pl.ds(k * half, half)
        return pltpu.make_async_remote_copy(
            src_ref=rows_g.at[s, quarter, rows],
            dst_ref=rows_g.at[s, quarter, rows],
            send_sem=rows2_send.at[s, k],
            recv_sem=rows2_recv.at[s, k],
            device_id=(dp, zpair[k]),
            device_id_type=MESH,
        )

    loss_ref[...] = jnp.zeros_like(loss_ref)
    total[...] = jnp.zeros_like(total)
    own_copy().start()
    own_copy().wait()

    def body(i, carry):
        @pl.when(i < steps)
        def _():
            @pl.when(i > 0)
            def _():
                for way in range(2):
                    ring_arrival(i, way).wait_recv()

            @pl.when(i < steps - 1)
            def _():
                for way in range(2):
                    ring_copy(i, way).start()

            for way in range(2):
                side_copy(i, way, mine).start()

        @pl.when(jnp.logical_and(i >= 1, i < steps + 1))
        def _():
            s = i - 1
            slot = lax.rem(s, 2)
            for k in range(2):
                rows = pl.ds(k * half, half)
                sum1_copy(s, k).wait_recv()
                passed = y_own[slot, zpair[1 - k], rows, :] + in1[s, k, 1].astype(jnp.float32)
                out2[s, k] = passed.astype(jnp.bfloat16)
                sum2_copy(s, k).start()
                y_keep[slot, rows, :] = y_own[slot, z, rows, :] + in1[s, k, 0].astype(jnp.float32)

        @pl.when(jnp.logical_and(i >= 2, i < steps + 2))
        def _():
            s = i - 2
            slot = lax.rem(s, 2)
            for k in range(2):
                sum2_copy(s, k).wait_recv()
            for chunk in range(4):
                ring_core, way = chunk // 2, chunk % 2
                at = cycle_position(x, y, ring_core)
                origin = cycle_device(lax.rem(at + (CHIPS - s if way == 0 else s), CHIPS), ring_core)
                token = pl.multiple_of((origin * 2 + way) * part, part)
                rows = pl.ds(chunk * part, part)
                inside = pl.ds((chunk % 2) * part, part)
                diff = (
                    y_keep[slot, rows, :]
                    + in2[s, chunk // 2, inside, :].astype(jnp.float32)
                    - target_ref[pl.ds(token, part), :]
                )
                rows_g[s, z, rows, :] = (diff * inv_root).astype(jnp.bfloat16)
                loss_ref[...] += jnp.sum((diff * diff).reshape(part // 8, 8, diff.shape[1]), axis=0)
            for k in range(2):
                rows1_copy(s, k, z).start()

        @pl.when(jnp.logical_and(i >= 3, i < steps + 3))
        def _():
            s = i - 3
            for k in range(2):
                rows1_copy(s, k, zpair[k]).wait_recv()
            for k in range(2):
                rows2_copy(s, k, zpair[1 - k]).start()

        @pl.when(i < steps)
        def _():
            slot = lax.rem(i, 2)
            for way in range(2):
                side_copy(i, way, theirs).wait_recv()
            for n in range(2):
                part_y = jnp.dot(
                    held[i], proj_ref[:, n * 256 : (n + 1) * 256], preferred_element_type=jnp.float32
                )
                y_own[slot, 2 * n] = part_y[:, :128]
                y_own[slot, 2 * n + 1] = part_y[:, 128:]
            for k in range(2):
                rows = pl.ds(k * half, half)
                other = 3 - zpair[k] if k == 0 else zpair[k] + 1 - 2 * lax.rem(zpair[k], 2)
                out1[i, k, 0] = y_own[slot, zpair[k], rows, :].astype(jnp.bfloat16)
                out1[i, k, 1] = y_own[slot, other, rows, :].astype(jnp.bfloat16)
                sum1_copy(i, k).start()

        @pl.when(i >= 4)
        def _():
            s = i - 4
            for k in range(2):
                rows2_copy(s, k, 3 - zpair[k] if k == 0 else zpair[k] + 1 - 2 * lax.rem(zpair[k], 2)).wait_recv()
            rows = jnp.concatenate([rows_g[s, q] for q in range(4)], axis=1)
            for f in range(8):
                features = slice(f * 256, (f + 1) * 256)
                total[features, :] += lax.dot_general(
                    held[s, :, features], rows, (((0,), (0,)), ((), ())), preferred_element_type=jnp.float32
                )

        return carry

    lax.fori_loop(0, steps + 4, body, 0)

    def finish(s, carry):
        @pl.when(s < steps - 1)
        def _():
            for way in range(2):
                ring_copy(s, way).wait_send()

        for k in range(2):
            side_copy(s, k, mine).wait_send()
            sum1_copy(s, k).wait_send()
            sum2_copy(s, k).wait_send()
            rows1_copy(s, k, z).wait_send()
            rows2_copy(s, k, zpair[1 - k]).wait_send()
        return carry

    lax.fori_loop(0, steps, finish, 0)
    grad_ref[...] = total[...].astype(jnp.bfloat16)


def wide(hidden, proj, target, inv_root):
    rows, features = hidden.shape
    columns = proj.shape[1]
    quarter = columns // 4
    block = 2 * rows
    half = block // 2
    pairs = pltpu.SemaphoreType.DMA((CHIPS, 2))
    vmem = pl.BlockSpec(memory_space=pltpu.VMEM)
    return pl.pallas_call(
        functools.partial(wide_kernel, inv_root),
        out_shape=(
            jax.ShapeDtypeStruct((features, columns), jnp.bfloat16),
            jax.ShapeDtypeStruct((8, quarter), jnp.float32),
        ),
        in_specs=[vmem] * 3,
        out_specs=(vmem, vmem),
        scratch_shapes=[
            pltpu.VMEM((CHIPS, block, features), jnp.bfloat16),
            pltpu.VMEM((features, columns), jnp.float32),
            pltpu.VMEM((2, 4, block, quarter), jnp.float32),
            pltpu.VMEM((2, block, quarter), jnp.float32),
            pltpu.VMEM((CHIPS, 2, 2, half, quarter), jnp.bfloat16),
            pltpu.VMEM((CHIPS, 2, 2, half, quarter), jnp.bfloat16),
            pltpu.VMEM((CHIPS, 2, half, quarter), jnp.bfloat16),
            pltpu.VMEM((CHIPS, 2, half, quarter), jnp.bfloat16),
            pltpu.VMEM((CHIPS, 4, block, quarter), jnp.bfloat16),
            pltpu.SemaphoreType.DMA,
        ]
        + [pairs] * 12,
        compiler_params=pltpu.CompilerParams(
            collective_id=0, has_side_effects=True, vmem_limit_bytes=56 * 1024 * 1024
        ),
    )(hidden, proj, target)


def shards(
    student_in, value_weight, folded_out, norm_gain, proj, teacher_codes, teacher_scales, perm
):
    sections = lax.axis_size("pipe")
    section = lax.axis_index("pipe")
    n_ranks = lax.axis_size("dp")
    rank = lax.axis_index("dp")
    rows, features = student_in.shape
    width = features * sections
    head = value_weight.shape[2]
    tokens = rows * n_ranks
    columns = proj.shape[1]
    total_cols = columns * n_ranks

    scaled = value_weight[0].astype(jnp.float32) * norm_gain[0].astype(jnp.float32)[:, None]
    w_value = scaled.astype(jnp.bfloat16).reshape(sections, n_ranks, features // n_ranks, head)
    w_value = lax.dynamic_index_in_dim(w_value, rank, 1, keepdims=False)
    w_value = lax.all_to_all(w_value, "pipe", split_axis=0, concat_axis=0, tiled=True)
    w_value = lax.all_gather(w_value, "dp", axis=1, tiled=True)
    w_out = lax.dynamic_slice_in_dim(folded_out[0], rank * (head // n_ranks), head // n_ranks, 0)
    w_out = w_out.reshape(head // n_ranks, sections, features).transpose(1, 0, 2)
    w_out = lax.all_to_all(w_out, "pipe", split_axis=0, concat_axis=0, tiled=True)
    w_out = lax.all_gather(w_out, "dp", axis=1, tiled=True)

    codes = teacher_codes.reshape(rows, n_ranks, sections, columns // sections)
    codes = lax.dynamic_index_in_dim(codes, section, 2, keepdims=False)
    codes = lax.all_to_all(codes, "dp", split_axis=1, concat_axis=0, tiled=True).reshape(tokens, -1)
    scales = lax.all_gather(teacher_scales, "dp", axis=0, tiled=True)
    target = codes[perm].astype(jnp.float32) * scales[perm].astype(jnp.float32)[:, None]

    hidden = student_in
    for layer in range(sections):
        wide_rows = hidden.astype(jnp.float32)
        squares = jnp.sum(wide_rows * wide_rows, axis=1, keepdims=True)
        products = jnp.dot(hidden, w_value[layer], preferred_element_type=jnp.float32)
        both = lax.psum(jnp.concatenate([products, jnp.broadcast_to(squares, (rows, 128))], axis=1), "pipe")
        scale = lax.rsqrt(both[:, head : head + 1] / width + 1e-05)
        values = (both[:, :head] * scale).astype(jnp.bfloat16)
        branch = jnp.dot(values, w_out[layer], preferred_element_type=jnp.float32)
        hidden = (wide_rows + branch).astype(jnp.bfloat16)

    grad_proj, squared = wide(hidden, proj, target, 1.0 / math.sqrt(tokens))
    loss = 0.5 * lax.psum(jnp.sum(squared), ("dp", "pipe")) / (tokens * total_cols)
    return (grad_proj, loss)


def solution(mesh):
    return jax.shard_map(
        shards,
        mesh=mesh,
        in_specs=(
            P("dp", "pipe"),
            P("pipe", None, None),
            P("pipe", None, None),
            P("pipe", None),
            P("pipe", "dp"),
            P("dp", None),
            P("dp"),
            P(),
        ),
        out_specs=(P("pipe", "dp"), P()),
        check_vma=False,
    )
```

```python
import functools
import math

import jax
import jax.numpy as jnp
from jax import lax
from jax.experimental import pallas as pl
from jax.experimental.pallas import tpu as pltpu
from jax.sharding import PartitionSpec as P

MESH = pl.DeviceIdType.MESH
SIDE = 4
CHIPS = SIDE * SIDE
RANKS = 2 * CHIPS
LANES = 128


def place(dp):
    core = lax.rem(dp, 2)
    chip = dp // 2
    return chip // SIDE, lax.rem(chip, SIDE), core


def cycle_position(x, y, core):
    return SIDE * (y + core * (x - y)) + lax.rem(x + y, SIDE)


def cycle_device(position, core):
    major = position // SIDE
    minor = lax.rem(lax.rem(position, SIDE) - major + SIDE, SIDE)
    x = minor + core * (major - minor)
    y = major + core * (minor - major)
    return (x * SIDE + y) * 2 + core


def layers_kernel(
    eps,
    h_ref,
    value_ref,
    out_ref,
    gain_ref,
    codes_ref,
    scale_ref,
    hidden_ref,
    store_ref,
    w_value,
    w_out,
    gains,
    products,
    normed,
    values,
    out1,
    in1,
    out2,
    in2,
    stage,
    staged,
    own_sem,
    first_send,
    ring_send,
    ring_recv,
    side_send,
    side_recv,
    gain_send,
    gain_recv,
    sum1_send,
    sum1_recv,
    sum2_send,
    sum2_recv,
    stage_sem,
    code_send,
    code_recv,
):
    dp = lax.axis_index("dp")
    z = lax.axis_index("pipe")
    x, y, core = place(dp)
    here = cycle_position(x, y, core)
    after = cycle_device(lax.rem(here + 1, CHIPS), core)
    before = cycle_device(lax.rem(here + CHIPS - 1, CHIPS), core)
    sibling = dp + 1 - 2 * core
    zpair = (z + 1 - 2 * lax.rem(z, 2), 3 - z)
    ring = (after, before)
    rows, features = h_ref.shape
    head = value_ref.shape[1]
    half = rows // 2
    weights = (w_value, w_out)
    depth = (features // RANKS, head // RANKS)
    width = 4 * features

    barrier = pltpu.get_barrier_semaphore()

    def greet(j, carry):
        pl.semaphore_signal(
            barrier, inc=1, device_id=(lax.rem(dp + j, RANKS), z), device_id_type=MESH
        )
        return carry

    lax.fori_loop(1, RANKS, greet, 0)
    for j in range(1, 4):
        pl.semaphore_signal(
            barrier, inc=1, device_id=(dp, lax.rem(z + j, 4)), device_id_type=MESH
        )
    pl.semaphore_wait(barrier, RANKS + 2)

    def piece(kind, owner):
        return pl.ds(pl.multiple_of(owner * depth[kind], depth[kind]), depth[kind])

    def first_copy(kind, j):
        to = lax.rem(z + j, 4)
        if kind == 0:
            start = pl.multiple_of(to * features + dp * depth[0], depth[0])
            source = value_ref.at[pl.ds(start, depth[0])]
        else:
            source = out_ref.at[piece(1, dp), pl.ds(pl.multiple_of(to * features, features), features)]
        return pltpu.make_async_remote_copy(
            src_ref=source,
            dst_ref=weights[kind].at[4 - j, piece(kind, dp)],
            send_sem=first_send.at[kind, j - 1],
            recv_sem=ring_recv.at[0, kind, 3 - j],
            device_id=(dp, to),
            device_id_type=MESH,
        )

    def gain_copy(j):
        to = lax.rem(z + j, 4)
        return pltpu.make_async_remote_copy(
            src_ref=gain_ref.at[to],
            dst_ref=gains.at[4 - j],
            send_sem=gain_send.at[j - 1],
            recv_sem=gain_recv.at[3 - j],
            device_id=(dp, to),
            device_id_type=MESH,
        )

    def origin(s, kind):
        return cycle_device(lax.rem(here + (CHIPS - s if kind == 0 else s), CHIPS), core)

    def ring_copy(s, kind, r, later):
        block = weights[kind].at[r, piece(kind, origin(s, kind))]
        return pltpu.make_async_remote_copy(
            src_ref=block,
            dst_ref=block,
            send_sem=ring_send.at[s, kind, r - 1],
            recv_sem=ring_recv.at[s + later, kind, r - 1],
            device_id=(ring[kind], z),
            device_id_type=MESH,
        )

    def side_copy(s, kind, owner):
        block = weights[kind].at[pl.ds(1, 3), piece(kind, owner)]
        return pltpu.make_async_remote_copy(
            src_ref=block,
            dst_ref=block,
            send_sem=side_send.at[s, kind],
            recv_sem=side_recv.at[s, kind],
            device_id=(sibling, z),
            device_id_type=MESH,
        )

    def own_copies():
        columns = pl.ds(pl.multiple_of(z * features, features), features)
        return (
            pltpu.make_async_copy(value_ref.at[columns], w_value.at[0], own_sem.at[0]),
            pltpu.make_async_copy(out_ref.at[:, columns], w_out.at[0], own_sem.at[1]),
        )

    def stage_copy(d):
        columns = pl.ds(pl.multiple_of((d * 4 + z) * LANES, LANES), LANES)
        return pltpu.make_async_copy(codes_ref.at[:, columns], stage.at[d], stage_sem.at[d])

    def code_copy(d):
        return pltpu.make_async_remote_copy(
            src_ref=staged.at[d],
            dst_ref=store_ref.at[pl.ds(pl.multiple_of(dp * rows, rows), rows)],
            send_sem=code_send.at[d],
            recv_sem=code_recv.at[dp],
            device_id=(d, z),
            device_id_type=MESH,
        )

    def code_arrival(d):
        block = store_ref.at[pl.ds(pl.multiple_of(d * rows, rows), rows)]
        return pltpu.make_async_remote_copy(
            src_ref=block,
            dst_ref=block,
            send_sem=code_send.at[d],
            recv_sem=code_recv.at[d],
            device_id=(d, z),
            device_id_type=MESH,
        )

    def sum_copy(phase, layer, k):
        source, target, send, recv = (
            (out1, in1, sum1_send, sum1_recv),
            (out2, in2, sum2_send, sum2_recv),
        )[phase]
        return pltpu.make_async_remote_copy(
            src_ref=source.at[layer, k],
            dst_ref=target.at[layer, k],
            send_sem=send.at[layer, k],
            recv_sem=recv.at[layer, k],
            device_id=(dp, zpair[k ^ phase]),
            device_id_type=MESH,
        )

    for j in range(1, 4):
        first_copy(0, j).start()
        first_copy(1, j).start()
        gain_copy(j).start()
    for copy in own_copies():
        copy.start()

    def fetch(d, carry):
        stage_copy(d).start()
        return carry

    lax.fori_loop(0, RANKS, fetch, 0)
    gains[0] = gain_ref[z]
    hidden_ref[...] = h_ref[...]

    def scale_codes(d, carry):
        stage_copy(d).wait()
        staged[d] = (stage[d].astype(jnp.float32) * scale_ref[...]).astype(jnp.bfloat16)
        return carry

    lax.fori_loop(0, RANKS, scale_codes, 0)
    store_ref[pl.ds(pl.multiple_of(dp * rows, rows), rows), :] = staged[dp]

    def pass_on(s, carry):
        for r in range(1, 4):
            for kind in range(2):
                ring_copy(s, kind, r, 0).wait_recv()

                @pl.when(s < CHIPS - 1)
                def _():
                    ring_copy(s, kind, r, 1).start()

        for kind in range(2):
            side_copy(s, kind, origin(s, kind)).start()
        return carry

    lax.fori_loop(0, CHIPS, pass_on, 0)

    def send_codes(j, carry):
        code_copy(lax.rem(dp + j, RANKS)).start()
        return carry

    lax.fori_loop(1, RANKS, send_codes, 0)

    def settle(s, carry):
        for kind in range(2):
            at = cycle_position(x, y, 1 - core)
            owner = cycle_device(lax.rem(at + (CHIPS - s if kind == 0 else s), CHIPS), 1 - core)
            side_copy(s, kind, owner).wait_recv()
            side_copy(s, kind, origin(s, kind)).wait_send()

            @pl.when(s < CHIPS - 1)
            def _():
                for r in range(1, 4):
                    ring_copy(s, kind, r, 1).wait_send()

        return carry

    lax.fori_loop(0, CHIPS, settle, 0)
    for copy in own_copies():
        copy.wait()
    for j in range(1, 4):
        gain_copy(j).wait()

    def layer_step(layer, carry):
        r = lax.rem(layer - z + 4, 4)
        gain = gains[r].astype(jnp.float32)
        squares = jnp.zeros((rows, LANES), jnp.float32)
        for j in range(features // LANES):
            columns = slice(j * LANES, (j + 1) * LANES)
            tile = hidden_ref[:, columns].astype(jnp.float32)
            squares += tile * tile
            normed[:, columns] = (tile * gain[j : j + 1, :]).astype(jnp.bfloat16)
        squares = jnp.broadcast_to(jnp.sum(squares, axis=1, keepdims=True), (rows, LANES))
        high = squares.astype(jnp.bfloat16)
        low = (squares - high.astype(jnp.float32)).astype(jnp.bfloat16)
        lane = lax.broadcasted_iota(jnp.int32, (rows, LANES), 1)
        products[:, :head] = jnp.dot(normed[...], w_value[r], preferred_element_type=jnp.float32)
        products[:, head:] = squares
        for k in range(2):
            part = slice(k * half, (k + 1) * half)
            out1[layer, k, :, :head] = products[part, :head].astype(jnp.bfloat16)
            out1[layer, k, :, head:] = jnp.where(
                lane[part] < LANES // 2, high[part].astype(jnp.float32), low[part].astype(jnp.float32)
            ).astype(jnp.bfloat16)
            sum_copy(0, layer, k).start()

        def arrived(buffer, k):
            marks = buffer[layer, k, :, head:].astype(jnp.float32)
            return buffer[layer, k, :, :head].astype(jnp.float32), marks + pltpu.roll(marks, LANES // 2, 1)

        for k in range(2):
            part = slice(k * half, (k + 1) * half)
            sum_copy(0, layer, k).wait_recv()
            more, marks = arrived(in1, k)
            so_far = products[part, :head] + more
            squares = products[part, head:] + marks
            products[part, :head] = so_far
            products[part, head:] = squares
            high = squares.astype(jnp.bfloat16)
            low = (squares - high.astype(jnp.float32)).astype(jnp.bfloat16)
            out2[layer, k, :, :head] = so_far.astype(jnp.bfloat16)
            out2[layer, k, :, head:] = jnp.where(
                lane[part] < LANES // 2, high.astype(jnp.float32), low.astype(jnp.float32)
            ).astype(jnp.bfloat16)
            sum_copy(1, layer, k).start()
        for k in range(2):
            part = slice(k * half, (k + 1) * half)
            sum_copy(1, layer, k).wait_recv()
            more, marks = arrived(in2, k)
            scale = lax.rsqrt((products[part, head:] + marks) * (1.0 / width) + eps)
            for j in range(head // LANES):
                columns = slice(j * LANES, (j + 1) * LANES)
                values[part, columns] = ((products[part, columns] + more[:, columns]) * scale).astype(
                    jnp.bfloat16
                )
        for n in range(features // 512):
            columns = slice(n * 512, (n + 1) * 512)
            branch = jnp.dot(values[...], w_out[r, :, columns], preferred_element_type=jnp.float32)
            hidden_ref[:, columns] = (hidden_ref[:, columns].astype(jnp.float32) + branch).astype(
                jnp.bfloat16
            )
        return carry

    lax.fori_loop(0, 4, layer_step, 0)

    def finish(j, carry):
        code_arrival(lax.rem(dp + j, RANKS)).wait_recv()
        code_copy(lax.rem(dp + j, RANKS)).wait_send()
        return carry

    lax.fori_loop(1, RANKS, finish, 0)
    for k in range(2):
        for layer in range(4):
            sum_copy(0, layer, k).wait_send()
            sum_copy(1, layer, k).wait_send()
    for j in range(1, 4):
        for kind in range(2):
            first_copy(kind, j).wait_send()


def layers(hidden, value_weight, folded_out, gain, codes, scales):
    rows, features = hidden.shape
    head = value_weight.shape[1]
    half = rows // 2
    vmem = pl.BlockSpec(memory_space=pltpu.VMEM)
    anywhere = pl.BlockSpec(memory_space=pl.ANY)
    dma = pltpu.SemaphoreType.DMA
    message = (4, 2, half, head + LANES)
    return pl.pallas_call(
        functools.partial(layers_kernel, 1e-5),
        out_shape=(
            jax.ShapeDtypeStruct((rows, features), jnp.bfloat16),
            jax.ShapeDtypeStruct((rows * RANKS, LANES), jnp.bfloat16),
        ),
        in_specs=[vmem, anywhere, anywhere, vmem, anywhere, vmem],
        out_specs=(vmem, vmem),
        scratch_shapes=[
            pltpu.VMEM((4, features, head), jnp.bfloat16),
            pltpu.VMEM((4, head, features), jnp.bfloat16),
            pltpu.VMEM((4, features // LANES, LANES), jnp.bfloat16),
            pltpu.VMEM((rows, head + LANES), jnp.float32),
            pltpu.VMEM((rows, features), jnp.bfloat16),
            pltpu.VMEM((rows, head), jnp.bfloat16),
            pltpu.VMEM(message, jnp.bfloat16),
            pltpu.VMEM(message, jnp.bfloat16),
            pltpu.VMEM(message, jnp.bfloat16),
            pltpu.VMEM(message, jnp.bfloat16),
            pltpu.VMEM((RANKS, rows, LANES), jnp.bfloat16),
            pltpu.VMEM((RANKS, rows, LANES), jnp.bfloat16),
            dma((2,)),
            dma((2, 3)),
            dma((CHIPS, 2, 3)),
            dma((CHIPS, 2, 3)),
            dma((CHIPS, 2)),
            dma((CHIPS, 2)),
            dma((3,)),
            dma((3,)),
            dma((4, 2)),
            dma((4, 2)),
            dma((4, 2)),
            dma((4, 2)),
            dma((RANKS,)),
            dma((RANKS,)),
            dma((RANKS,)),
        ],
        compiler_params=pltpu.CompilerParams(
            collective_id=1, has_side_effects=True, vmem_limit_bytes=40 * 1024 * 1024
        ),
    )(hidden, value_weight, folded_out, gain, codes, scales)


def wide_kernel(
    inv_root,
    h_ref,
    proj_ref,
    store_ref,
    perm_ref,
    grad_ref,
    loss_ref,
    held,
    total,
    y_own,
    y_keep,
    out1,
    in1,
    out2,
    in2,
    rows_g,
    store,
    aim,
    losses,
    own_sem,
    ring_send,
    ring_recv,
    side_send,
    side_recv,
    sum1_send,
    sum1_recv,
    sum2_send,
    sum2_recv,
    rows1_send,
    rows1_recv,
    rows2_send,
    rows2_recv,
    loss_send,
    loss_recv,
):
    dp = lax.axis_index("dp")
    z = lax.axis_index("pipe")
    x, y, core = place(dp)
    here = cycle_position(x, y, core)
    after = cycle_device(lax.rem(here + 1, CHIPS), core)
    before = cycle_device(lax.rem(here + CHIPS - 1, CHIPS), core)
    sibling = dp + 1 - 2 * core
    za = z + 1 - 2 * lax.rem(z, 2)
    zb = 3 - z
    steps = CHIPS
    part = h_ref.shape[0] // 2
    block = 4 * part
    half = block // 2
    zpair = (za, zb)
    ring = (after, before)

    sizes = (4, SIDE, 2 * SIDE)
    spots = (z, y, 2 * x + core)

    def peer(group, j):
        spot = lax.rem(spots[group] + j, sizes[group])
        if group == 0:
            return dp, spot
        if group == 1:
            return (x * SIDE + spot) * 2 + core, z
        return ((spot // 2) * SIDE + y) * 2 + lax.rem(spot, 2), z

    barrier = pltpu.get_barrier_semaphore()
    for device in ((after, z), (before, z)):
        pl.semaphore_signal(barrier, inc=1, device_id=device, device_id_type=MESH)
    for group in range(3):
        for j in range(1, sizes[group]):
            pl.semaphore_signal(barrier, inc=1, device_id=peer(group, j), device_id_type=MESH)
    pl.semaphore_wait(barrier, 2 + sum(sizes) - 3)

    mine = pl.multiple_of(core * 2 * part, 2 * part)
    theirs = pl.multiple_of((1 - core) * 2 * part, 2 * part)

    def own_copy():
        return pltpu.make_async_copy(h_ref, held.at[0, pl.ds(mine, 2 * part)], own_sem)

    def ring_copy(s, way):
        rows = pl.ds(pl.multiple_of(mine + way * part, part), part)
        return pltpu.make_async_remote_copy(
            src_ref=held.at[s, rows],
            dst_ref=held.at[s + 1, rows],
            send_sem=ring_send.at[s, way],
            recv_sem=ring_recv.at[s + 1, way],
            device_id=(ring[way], z),
            device_id_type=MESH,
        )

    def ring_arrival(s, way):
        rows = pl.ds(pl.multiple_of(mine + way * part, part), part)
        return pltpu.make_async_remote_copy(
            src_ref=held.at[s, rows],
            dst_ref=held.at[s, rows],
            send_sem=ring_send.at[s, way],
            recv_sem=ring_recv.at[s, way],
            device_id=(ring[way], z),
            device_id_type=MESH,
        )

    def side_copy(s, way, start):
        rows = pl.ds(pl.multiple_of(start + way * part, part), part)
        return pltpu.make_async_remote_copy(
            src_ref=held.at[s, rows],
            dst_ref=held.at[s, rows],
            send_sem=side_send.at[s, way],
            recv_sem=side_recv.at[s, way],
            device_id=(sibling, z),
            device_id_type=MESH,
        )

    def sum1_copy(s, k):
        return pltpu.make_async_remote_copy(
            src_ref=out1.at[s, k],
            dst_ref=in1.at[s, k],
            send_sem=sum1_send.at[s, k],
            recv_sem=sum1_recv.at[s, k],
            device_id=(dp, zpair[k]),
            device_id_type=MESH,
        )

    def sum2_copy(s, k):
        return pltpu.make_async_remote_copy(
            src_ref=out2.at[s, k],
            dst_ref=in2.at[s, k],
            send_sem=sum2_send.at[s, k],
            recv_sem=sum2_recv.at[s, k],
            device_id=(dp, zpair[1 - k]),
            device_id_type=MESH,
        )

    def rows1_copy(s, k, quarter):
        return pltpu.make_async_remote_copy(
            src_ref=rows_g.at[s, quarter],
            dst_ref=rows_g.at[s, quarter],
            send_sem=rows1_send.at[s, k],
            recv_sem=rows1_recv.at[s, k],
            device_id=(dp, zpair[k]),
            device_id_type=MESH,
        )

    def rows2_copy(s, k, quarter):
        rows = pl.ds(k * half, half)
        return pltpu.make_async_remote_copy(
            src_ref=rows_g.at[s, quarter, rows],
            dst_ref=rows_g.at[s, quarter, rows],
            send_sem=rows2_send.at[s, k],
            recv_sem=rows2_recv.at[s, k],
            device_id=(dp, zpair[k]),
            device_id_type=MESH,
        )

    def loss_copy(group, j, arrival):
        spot = lax.rem(spots[group] + j, sizes[group]) if arrival else spots[group]
        return pltpu.make_async_remote_copy(
            src_ref=losses.at[group, spot],
            dst_ref=losses.at[group, spot],
            send_sem=loss_send.at[group, j],
            recv_sem=loss_recv.at[group, spot],
            device_id=peer(group, j),
            device_id_type=MESH,
        )

    def loss_out(group):
        losses[group, spots[group]] = loss_ref[...]
        for j in range(1, sizes[group]):
            loss_copy(group, j, False).start()

    def loss_in(group):
        for j in range(1, sizes[group]):
            loss_copy(group, j, True).wait_recv()
        loss_ref[...] = functools.reduce(
            jnp.add, [losses[group, spot] for spot in range(sizes[group])]
        )

    store[...] = store_ref[...].astype(jnp.float32)
    loss_ref[...] = jnp.zeros_like(loss_ref)
    total[...] = jnp.zeros_like(total)
    own_copy().start()
    own_copy().wait()

    def body(i, carry):
        @pl.when(i < steps)
        def _():
            @pl.when(i > 0)
            def _():
                for way in range(2):
                    ring_arrival(i, way).wait_recv()

            @pl.when(i < steps - 1)
            def _():
                for way in range(2):
                    ring_copy(i, way).start()

            for way in range(2):
                side_copy(i, way, mine).start()

        @pl.when(jnp.logical_and(i >= 1, i < steps + 1))
        def _():
            s = i - 1
            slot = lax.rem(s, 2)
            for k in range(2):
                rows = pl.ds(k * half, half)
                sum1_copy(s, k).wait_recv()
                passed = y_own[slot, zpair[1 - k], rows, :] + in1[s, k, 1].astype(jnp.float32)
                out2[s, k] = passed.astype(jnp.bfloat16)
                sum2_copy(s, k).start()
                y_keep[slot, rows, :] = y_own[slot, z, rows, :] + in1[s, k, 0].astype(jnp.float32)

        @pl.when(jnp.logical_and(i >= 2, i < steps + 2))
        def _():
            s = i - 2
            slot = lax.rem(s, 2)
            for k in range(2):
                sum2_copy(s, k).wait_recv()
            for chunk in range(4):
                ring_core, way = chunk // 2, chunk % 2
                at = cycle_position(x, y, ring_core)
                origin = cycle_device(lax.rem(at + (CHIPS - s if way == 0 else s), CHIPS), ring_core)
                token = pl.multiple_of((origin * 2 + way) * part, part)
                rows = pl.ds(chunk * part, part)
                inside = pl.ds((chunk % 2) * part, part)

                def seek(group, carry):
                    for j in range(8):
                        at_row = group * 8 + j
                        aim[pl.ds(chunk * part + at_row, 1), :] = store[
                            pl.ds(perm_ref[token + at_row], 1), :
                        ]
                    return carry

                lax.fori_loop(0, part // 8, seek, 0)
                diff = (
                    y_keep[slot, rows, :]
                    + in2[s, chunk // 2, inside, :].astype(jnp.float32)
                    - aim[rows, :]
                )
                rows_g[s, z, rows, :] = (diff * inv_root).astype(jnp.bfloat16)
                loss_ref[...] += jnp.sum((diff * diff).reshape(part // 8, 8, diff.shape[1]), axis=0)
            for k in range(2):
                rows1_copy(s, k, z).start()

        @pl.when(jnp.logical_and(i >= 3, i < steps + 3))
        def _():
            s = i - 3
            for k in range(2):
                rows1_copy(s, k, zpair[k]).wait_recv()
            for k in range(2):
                rows2_copy(s, k, zpair[1 - k]).start()

        @pl.when(i == steps + 2)
        def _():
            loss_out(0)

        @pl.when(i == steps + 3)
        def _():
            loss_in(0)
            loss_out(1)

        @pl.when(i < steps)
        def _():
            slot = lax.rem(i, 2)
            for way in range(2):
                side_copy(i, way, theirs).wait_recv()
            for n in range(2):
                part_y = jnp.dot(
                    held[i], proj_ref[:, n * 256 : (n + 1) * 256], preferred_element_type=jnp.float32
                )
                y_own[slot, 2 * n] = part_y[:, :128]
                y_own[slot, 2 * n + 1] = part_y[:, 128:]
            for k in range(2):
                rows = pl.ds(k * half, half)
                other = 3 - zpair[k] if k == 0 else zpair[k] + 1 - 2 * lax.rem(zpair[k], 2)
                out1[i, k, 0] = y_own[slot, zpair[k], rows, :].astype(jnp.bfloat16)
                out1[i, k, 1] = y_own[slot, other, rows, :].astype(jnp.bfloat16)
                sum1_copy(i, k).start()

        @pl.when(i >= 4)
        def _():
            s = i - 4
            for k in range(2):
                rows2_copy(s, k, 3 - zpair[k] if k == 0 else zpair[k] + 1 - 2 * lax.rem(zpair[k], 2)).wait_recv()
            rows = jnp.concatenate([rows_g[s, q] for q in range(4)], axis=1)
            for f in range(8):
                features = slice(f * 256, (f + 1) * 256)
                total[features, :] += lax.dot_general(
                    held[s, :, features], rows, (((0,), (0,)), ((), ())), preferred_element_type=jnp.float32
                )

        return carry

    lax.fori_loop(0, steps + 4, body, 0)
    loss_in(1)
    loss_out(2)

    def finish(s, carry):
        @pl.when(s < steps - 1)
        def _():
            for way in range(2):
                ring_copy(s, way).wait_send()

        for k in range(2):
            side_copy(s, k, mine).wait_send()
            sum1_copy(s, k).wait_send()
            sum2_copy(s, k).wait_send()
            rows1_copy(s, k, z).wait_send()
            rows2_copy(s, k, zpair[1 - k]).wait_send()
        return carry

    lax.fori_loop(0, steps, finish, 0)
    loss_in(2)
    for group in range(3):
        for j in range(1, sizes[group]):
            loss_copy(group, j, False).wait_send()
    grad_ref[...] = total[...].astype(jnp.bfloat16)


def wide(hidden, proj, store, perm, inv_root):
    rows, features = hidden.shape
    columns = proj.shape[1]
    quarter = columns // 4
    block = 2 * rows
    half = block // 2
    pairs = pltpu.SemaphoreType.DMA((CHIPS, 2))
    vmem = pl.BlockSpec(memory_space=pltpu.VMEM)
    return pl.pallas_call(
        functools.partial(wide_kernel, inv_root),
        out_shape=(
            jax.ShapeDtypeStruct((features, columns), jnp.bfloat16),
            jax.ShapeDtypeStruct((8, quarter), jnp.float32),
        ),
        in_specs=[vmem, vmem, vmem, pl.BlockSpec(memory_space=pltpu.SMEM)],
        out_specs=(vmem, vmem),
        scratch_shapes=[
            pltpu.VMEM((CHIPS, block, features), jnp.bfloat16),
            pltpu.VMEM((features, columns), jnp.float32),
            pltpu.VMEM((2, 4, block, quarter), jnp.float32),
            pltpu.VMEM((2, block, quarter), jnp.float32),
            pltpu.VMEM((CHIPS, 2, 2, half, quarter), jnp.bfloat16),
            pltpu.VMEM((CHIPS, 2, 2, half, quarter), jnp.bfloat16),
            pltpu.VMEM((CHIPS, 2, half, quarter), jnp.bfloat16),
            pltpu.VMEM((CHIPS, 2, half, quarter), jnp.bfloat16),
            pltpu.VMEM((CHIPS, 4, block, quarter), jnp.bfloat16),
            pltpu.VMEM(store.shape, jnp.float32),
            pltpu.VMEM((block, quarter), jnp.float32),
            pltpu.VMEM((3, 2 * SIDE, 8, quarter), jnp.float32),
            pltpu.SemaphoreType.DMA,
        ]
        + [pairs] * 12
        + [pltpu.SemaphoreType.DMA((3, 2 * SIDE))] * 2,
        compiler_params=pltpu.CompilerParams(
            collective_id=0, has_side_effects=True, vmem_limit_bytes=56 * 1024 * 1024
        ),
    )(hidden, proj, store, perm)


def shards(
    student_in, value_weight, folded_out, norm_gain, proj, teacher_codes, teacher_scales, perm
):
    sections = lax.axis_size("pipe")
    n_ranks = lax.axis_size("dp")
    rows, features = student_in.shape
    tokens = rows * n_ranks
    columns = proj.shape[1]
    total_cols = columns * n_ranks

    gain = norm_gain.reshape(sections, features // LANES, LANES)
    scales = jnp.broadcast_to(teacher_scales.astype(jnp.float32)[:, None], (rows, LANES))
    hidden, store = layers(student_in, value_weight[0], folded_out[0], gain, teacher_codes, scales)
    grad_proj, squared = wide(hidden, proj, store, perm, 1.0 / math.sqrt(tokens))
    loss = 0.5 * jnp.sum(squared) / (tokens * total_cols)
    return (grad_proj, loss)


def solution(mesh):
    return jax.shard_map(
        shards,
        mesh=mesh,
        in_specs=(
            P("dp", "pipe"),
            P("pipe", None, None),
            P("pipe", None, None),
            P("pipe", None),
            P("pipe", "dp"),
            P("dp", None),
            P("dp"),
            P(),
        ),
        out_specs=(P("pipe", "dp"), P()),
        check_vma=False,
    )
```

```python
import functools
import math

import jax
import jax.numpy as jnp
from jax import lax
from jax.experimental import pallas as pl
from jax.experimental.pallas import tpu as pltpu
from jax.sharding import PartitionSpec as P

MESH = pl.DeviceIdType.MESH
SIDE = 4
CHIPS = SIDE * SIDE
RANKS = 2 * CHIPS
LANES = 128


def place(dp):
    core = lax.rem(dp, 2)
    chip = dp // 2
    return chip // SIDE, lax.rem(chip, SIDE), core


def cycle_position(x, y, core):
    return SIDE * (y + core * (x - y)) + lax.rem(x + y, SIDE)


def cycle_device(position, core):
    major = position // SIDE
    minor = lax.rem(lax.rem(position, SIDE) - major + SIDE, SIDE)
    x = minor + core * (major - minor)
    y = major + core * (minor - major)
    return (x * SIDE + y) * 2 + core


def layers_kernel(
    eps,
    h_ref,
    value_ref,
    out_ref,
    gain_ref,
    codes_ref,
    scale_ref,
    hidden_ref,
    store_ref,
    w_value,
    w_out,
    gains,
    products,
    normed,
    values,
    out1,
    in1,
    out2,
    in2,
    stage,
    staged,
    own_sem,
    first_send,
    first_recv,
    near_send,
    near_recv,
    far_send,
    far_recv,
    side_send,
    side_recv,
    gain_send,
    gain_recv,
    sum1_send,
    sum1_recv,
    sum2_send,
    sum2_recv,
    stage_sem,
    code_send,
    code_recv,
):
    dp = lax.axis_index("dp")
    z = lax.axis_index("pipe")
    x, y, core = place(dp)
    sibling = dp + 1 - 2 * core
    zpair = (z + 1 - 2 * lax.rem(z, 2), 3 - z)
    rows, features = h_ref.shape
    head = value_ref.shape[-1]
    half = rows // 2
    weights = (w_value, w_out)
    width = 4 * features

    barrier = pltpu.get_barrier_semaphore()

    def greet(j, carry):
        pl.semaphore_signal(
            barrier, inc=1, device_id=(lax.rem(dp + j, RANKS), z), device_id_type=MESH
        )
        return carry

    lax.fori_loop(1, RANKS, greet, 0)
    for j in range(1, 4):
        pl.semaphore_signal(
            barrier, inc=1, device_id=(dp, lax.rem(z + j, 4)), device_id_type=MESH
        )
    pl.semaphore_wait(barrier, RANKS + 2)

    def first_copy(kind, j):
        to = lax.rem(z + j, 4)
        if kind == 0:
            source = value_ref.at[to, x, y, core]
        else:
            source = out_ref.at[x, y, core, :, pl.ds(pl.multiple_of(to * features, features), features)]
        return pltpu.make_async_remote_copy(
            src_ref=source,
            dst_ref=weights[kind].at[4 - j, x, y, core],
            send_sem=first_send.at[kind, j - 1],
            recv_sem=first_recv.at[kind, 3 - j],
            device_id=(dp, to),
            device_id_type=MESH,
        )

    def first_arrival(kind, r):
        block = weights[kind].at[r, x, y, core]
        return pltpu.make_async_remote_copy(
            src_ref=block,
            dst_ref=block,
            send_sem=first_send.at[kind, r - 1],
            recv_sem=first_recv.at[kind, r - 1],
            device_id=(dp, lax.rem(z + r, 4)),
            device_id_type=MESH,
        )

    spot = (x, y)

    def near_copy(kind, r, j, arrival):
        there = lax.rem(spot[kind] + j, SIDE)
        at = there if arrival else spot[kind]
        block = w_value.at[r, at, y, core] if kind == 0 else w_out.at[r, x, at, core]
        chip = there * SIDE + y if kind == 0 else x * SIDE + there
        return pltpu.make_async_remote_copy(
            src_ref=block,
            dst_ref=block,
            send_sem=near_send.at[kind, r - 1, j],
            recv_sem=near_recv.at[kind, r - 1, at],
            device_id=(chip * 2 + core, z),
            device_id_type=MESH,
        )

    def far_copy(kind, r, j, arrival):
        there = lax.rem(spot[1 - kind] + j, SIDE)
        at = there if arrival else spot[1 - kind]
        block = w_value.at[r, :, at, core] if kind == 0 else w_out.at[r, at, :, core]
        chip = there * SIDE + y if kind == 1 else x * SIDE + there
        return pltpu.make_async_remote_copy(
            src_ref=block,
            dst_ref=block,
            send_sem=far_send.at[kind, r - 1, j],
            recv_sem=far_recv.at[kind, r - 1, at],
            device_id=(chip * 2 + core, z),
            device_id_type=MESH,
        )

    def side_copy(kind, r, j, owner):
        at = lax.rem(spot[1 - kind] + j, SIDE)
        block = w_value.at[r, :, at, owner] if kind == 0 else w_out.at[r, at, :, owner]
        return pltpu.make_async_remote_copy(
            src_ref=block,
            dst_ref=block,
            send_sem=side_send.at[kind, r - 1, at],
            recv_sem=side_recv.at[kind, r - 1, at],
            device_id=(sibling, z),
            device_id_type=MESH,
        )

    def gain_copy(j):
        to = lax.rem(z + j, 4)
        return pltpu.make_async_remote_copy(
            src_ref=gain_ref.at[to],
            dst_ref=gains.at[4 - j],
            send_sem=gain_send.at[j - 1],
            recv_sem=gain_recv.at[3 - j],
            device_id=(dp, to),
            device_id_type=MESH,
        )

    def own_copies():
        columns = pl.ds(pl.multiple_of(z * features, features), features)
        return (
            pltpu.make_async_copy(value_ref.at[z], w_value.at[0], own_sem.at[0]),
            pltpu.make_async_copy(out_ref.at[:, :, :, :, columns], w_out.at[0], own_sem.at[1]),
        )

    def stage_copy(d):
        columns = pl.ds(pl.multiple_of((d * 4 + z) * LANES, LANES), LANES)
        return pltpu.make_async_copy(codes_ref.at[:, columns], stage.at[d], stage_sem.at[d])

    def code_copy(d):
        return pltpu.make_async_remote_copy(
            src_ref=staged.at[d],
            dst_ref=store_ref.at[pl.ds(pl.multiple_of(dp * rows, rows), rows)],
            send_sem=code_send.at[d],
            recv_sem=code_recv.at[dp],
            device_id=(d, z),
            device_id_type=MESH,
        )

    def code_arrival(d):
        block = store_ref.at[pl.ds(pl.multiple_of(d * rows, rows), rows)]
        return pltpu.make_async_remote_copy(
            src_ref=block,
            dst_ref=block,
            send_sem=code_send.at[d],
            recv_sem=code_recv.at[d],
            device_id=(d, z),
            device_id_type=MESH,
        )

    def sum_copy(phase, layer, k):
        source, target, send, recv = (
            (out1, in1, sum1_send, sum1_recv),
            (out2, in2, sum2_send, sum2_recv),
        )[phase]
        return pltpu.make_async_remote_copy(
            src_ref=source.at[layer, k],
            dst_ref=target.at[layer, k],
            send_sem=send.at[layer, k],
            recv_sem=recv.at[layer, k],
            device_id=(dp, zpair[k ^ phase]),
            device_id_type=MESH,
        )

    for j in range(1, 4):
        first_copy(0, j).start()
        first_copy(1, j).start()
        gain_copy(j).start()
    for copy in own_copies():
        copy.start()

    def fetch(d, carry):
        stage_copy(d).start()
        return carry

    lax.fori_loop(0, RANKS, fetch, 0)
    gains[0] = gain_ref[z]
    hidden_ref[...] = h_ref[...]

    def scale_codes(d, carry):
        stage_copy(d).wait()
        staged[d] = (stage[d].astype(jnp.float32) * scale_ref[...]).astype(jnp.bfloat16)
        return carry

    lax.fori_loop(0, RANKS, scale_codes, 0)
    store_ref[pl.ds(pl.multiple_of(dp * rows, rows), rows), :] = staged[dp]

    def turn(k):
        layer = k + jnp.where(k >= z, 1, 0)
        return lax.rem(layer - z + 4, 4)

    def spread_near(k, carry):
        r = turn(k)
        for kind in range(2):
            first_arrival(kind, r).wait_recv()
            for j in (1, 3, 2):
                near_copy(kind, r, j, False).start()
        return carry

    def spread_far(k):
        r = turn(k)
        for kind in range(2):
            for j in (1, 3, 2):
                near_copy(kind, r, j, True).wait_recv()
            for j in (1, 3, 2):
                far_copy(kind, r, j, False).start()
        for kind in range(2):
            side_copy(kind, r, 0, core).start()

    def settle(r, order):
        for j in order:
            for kind in range(2):
                far_copy(kind, r, j, True).wait_recv()
                side_copy(kind, r, j, core).start()

    lax.fori_loop(0, 3, spread_near, 0)
    spread_far(0)
    for copy in own_copies():
        copy.wait()
    for j in range(1, 4):
        gain_copy(j).wait()

    def send_codes(j, carry):
        code_copy(lax.rem(dp + j, RANKS)).start()
        return carry

    def layer_step(layer, carry):
        r = lax.rem(layer - z + 4, 4)

        @pl.when(layer != z)
        def _():
            settle(r, (1,))

        @pl.when(layer < 2)
        def _():
            spread_far(layer + 1)

        @pl.when(layer != z)
        def _():
            settle(r, (3, 2))
            for kind in range(2):
                for j in range(SIDE):
                    side_copy(kind, r, j, 1 - core).wait_recv()

            @pl.when(layer == 3 - jnp.where(z == 3, 1, 0))
            def _():
                lax.fori_loop(1, RANKS, send_codes, 0)

        gain = gains[r].astype(jnp.float32)
        squares = jnp.zeros((rows, LANES), jnp.float32)
        for j in range(features // LANES):
            columns = slice(j * LANES, (j + 1) * LANES)
            tile = hidden_ref[:, columns].astype(jnp.float32)
            squares += tile * tile
            normed[:, columns] = (tile * gain[j : j + 1, :]).astype(jnp.bfloat16)
        squares = jnp.broadcast_to(jnp.sum(squares, axis=1, keepdims=True), (rows, LANES))
        high = squares.astype(jnp.bfloat16)
        low = (squares - high.astype(jnp.float32)).astype(jnp.bfloat16)
        lane = lax.broadcasted_iota(jnp.int32, (rows, LANES), 1)
        products[:, :head] = jnp.dot(
            normed[...], w_value[r].reshape(features, head), preferred_element_type=jnp.float32
        )
        products[:, head:] = squares
        for k in range(2):
            part = slice(k * half, (k + 1) * half)
            out1[layer, k, :, :head] = products[part, :head].astype(jnp.bfloat16)
            out1[layer, k, :, head:] = jnp.where(
                lane[part] < LANES // 2, high[part].astype(jnp.float32), low[part].astype(jnp.float32)
            ).astype(jnp.bfloat16)
            sum_copy(0, layer, k).start()

        def arrived(buffer, k):
            marks = buffer[layer, k, :, head:].astype(jnp.float32)
            return buffer[layer, k, :, :head].astype(jnp.float32), marks + pltpu.roll(marks, LANES // 2, 1)

        for k in range(2):
            part = slice(k * half, (k + 1) * half)
            sum_copy(0, layer, k).wait_recv()
            more, marks = arrived(in1, k)
            so_far = products[part, :head] + more
            squares = products[part, head:] + marks
            products[part, :head] = so_far
            products[part, head:] = squares
            high = squares.astype(jnp.bfloat16)
            low = (squares - high.astype(jnp.float32)).astype(jnp.bfloat16)
            out2[layer, k, :, :head] = so_far.astype(jnp.bfloat16)
            out2[layer, k, :, head:] = jnp.where(
                lane[part] < LANES // 2, high.astype(jnp.float32), low.astype(jnp.float32)
            ).astype(jnp.bfloat16)
            sum_copy(1, layer, k).start()
        for k in range(2):
            part = slice(k * half, (k + 1) * half)
            sum_copy(1, layer, k).wait_recv()
            more, marks = arrived(in2, k)
            scale = lax.rsqrt((products[part, head:] + marks) * (1.0 / width) + eps)
            for j in range(head // LANES):
                columns = slice(j * LANES, (j + 1) * LANES)
                values[part, columns] = ((products[part, columns] + more[:, columns]) * scale).astype(
                    jnp.bfloat16
                )
        for n in range(features // 512):
            columns = slice(n * 512, (n + 1) * 512)
            branch = jnp.dot(
                values[...],
                w_out[r, :, :, :, :, columns].reshape(head, 512),
                preferred_element_type=jnp.float32,
            )
            hidden_ref[:, columns] = (hidden_ref[:, columns].astype(jnp.float32) + branch).astype(
                jnp.bfloat16
            )
        return carry

    lax.fori_loop(0, 4, layer_step, 0)

    def finish(j, carry):
        code_arrival(lax.rem(dp + j, RANKS)).wait_recv()
        code_copy(lax.rem(dp + j, RANKS)).wait_send()
        return carry

    lax.fori_loop(1, RANKS, finish, 0)
    for k in range(2):
        for layer in range(4):
            sum_copy(0, layer, k).wait_send()
            sum_copy(1, layer, k).wait_send()
    for j in range(1, 4):
        for kind in range(2):
            first_copy(kind, j).wait_send()
            for r in range(1, 4):
                near_copy(kind, r, j, False).wait_send()
                far_copy(kind, r, j, False).wait_send()
    for kind in range(2):
        for r in range(1, 4):
            for j in range(SIDE):
                side_copy(kind, r, j, core).wait_send()


def layers(hidden, value_weight, folded_out, gain, codes, scales):
    rows, features = hidden.shape
    head = value_weight.shape[1]
    half = rows // 2
    grid = (4, SIDE, SIDE, 2)
    value_weight = value_weight.reshape(*grid, features // RANKS, head)
    folded_out = folded_out.reshape(*grid[1:], head // RANKS, 4 * features)
    vmem = pl.BlockSpec(memory_space=pltpu.VMEM)
    anywhere = pl.BlockSpec(memory_space=pl.ANY)
    dma = pltpu.SemaphoreType.DMA
    message = (4, 2, half, head + LANES)
    return pl.pallas_call(
        functools.partial(layers_kernel, 1e-5),
        out_shape=(
            jax.ShapeDtypeStruct((rows, features), jnp.bfloat16),
            jax.ShapeDtypeStruct((rows * RANKS, LANES), jnp.bfloat16),
        ),
        in_specs=[vmem, anywhere, anywhere, vmem, anywhere, vmem],
        out_specs=(vmem, vmem),
        scratch_shapes=[
            pltpu.VMEM((*grid, features // RANKS, head), jnp.bfloat16),
            pltpu.VMEM((*grid, head // RANKS, features), jnp.bfloat16),
            pltpu.VMEM((4, features // LANES, LANES), jnp.bfloat16),
            pltpu.VMEM((rows, head + LANES), jnp.float32),
            pltpu.VMEM((rows, features), jnp.bfloat16),
            pltpu.VMEM((rows, head), jnp.bfloat16),
            pltpu.VMEM(message, jnp.bfloat16),
            pltpu.VMEM(message, jnp.bfloat16),
            pltpu.VMEM(message, jnp.bfloat16),
            pltpu.VMEM(message, jnp.bfloat16),
            pltpu.VMEM((RANKS, rows, LANES), jnp.bfloat16),
            pltpu.VMEM((RANKS, rows, LANES), jnp.bfloat16),
            dma((2,)),
            dma((2, 3)),
            dma((2, 3)),
            dma((2, 3, SIDE)),
            dma((2, 3, SIDE)),
            dma((2, 3, SIDE)),
            dma((2, 3, SIDE)),
            dma((2, 3, SIDE)),
            dma((2, 3, SIDE)),
            dma((3,)),
            dma((3,)),
            dma((4, 2)),
            dma((4, 2)),
            dma((4, 2)),
            dma((4, 2)),
            dma((RANKS,)),
            dma((RANKS,)),
            dma((RANKS,)),
        ],
        compiler_params=pltpu.CompilerParams(
            collective_id=1, has_side_effects=True, vmem_limit_bytes=40 * 1024 * 1024
        ),
    )(hidden, value_weight, folded_out, gain, codes, scales)


def wide_kernel(
    inv_root,
    h_ref,
    proj_ref,
    store_ref,
    perm_ref,
    grad_ref,
    loss_ref,
    held,
    total,
    y_own,
    y_keep,
    out1,
    in1,
    out2,
    in2,
    rows_g,
    store,
    aim,
    losses,
    own_sem,
    ring_send,
    ring_recv,
    side_send,
    side_recv,
    sum1_send,
    sum1_recv,
    sum2_send,
    sum2_recv,
    rows1_send,
    rows1_recv,
    rows2_send,
    rows2_recv,
    loss_send,
    loss_recv,
):
    dp = lax.axis_index("dp")
    z = lax.axis_index("pipe")
    x, y, core = place(dp)
    here = cycle_position(x, y, core)
    after = cycle_device(lax.rem(here + 1, CHIPS), core)
    before = cycle_device(lax.rem(here + CHIPS - 1, CHIPS), core)
    sibling = dp + 1 - 2 * core
    za = z + 1 - 2 * lax.rem(z, 2)
    zb = 3 - z
    steps = CHIPS
    part = h_ref.shape[0] // 2
    block = 4 * part
    half = block // 2
    zpair = (za, zb)
    ring = (after, before)

    sizes = (4, SIDE, 2 * SIDE)
    spots = (z, y, 2 * x + core)

    def peer(group, j):
        spot = lax.rem(spots[group] + j, sizes[group])
        if group == 0:
            return dp, spot
        if group == 1:
            return (x * SIDE + spot) * 2 + core, z
        return ((spot // 2) * SIDE + y) * 2 + lax.rem(spot, 2), z

    barrier = pltpu.get_barrier_semaphore()
    for device in ((after, z), (before, z)):
        pl.semaphore_signal(barrier, inc=1, device_id=device, device_id_type=MESH)
    for group in range(3):
        for j in range(1, sizes[group]):
            pl.semaphore_signal(barrier, inc=1, device_id=peer(group, j), device_id_type=MESH)
    pl.semaphore_wait(barrier, 2 + sum(sizes) - 3)

    mine = pl.multiple_of(core * 2 * part, 2 * part)
    theirs = pl.multiple_of((1 - core) * 2 * part, 2 * part)

    def own_copy():
        return pltpu.make_async_copy(h_ref, held.at[0, pl.ds(mine, 2 * part)], own_sem)

    def ring_copy(s, way, sub, later):
        start = mine + way * part + sub * (part // 2)
        rows = pl.ds(pl.multiple_of(start, part // 2), part // 2)
        return pltpu.make_async_remote_copy(
            src_ref=held.at[s, rows],
            dst_ref=held.at[s + later, rows],
            send_sem=ring_send.at[s, way, sub],
            recv_sem=ring_recv.at[s + later, way, sub],
            device_id=(ring[way], z),
            device_id_type=MESH,
        )

    def side_copy(s, start):
        rows = pl.ds(start, 2 * part)
        return pltpu.make_async_remote_copy(
            src_ref=held.at[s, rows],
            dst_ref=held.at[s, rows],
            send_sem=side_send.at[s],
            recv_sem=side_recv.at[s],
            device_id=(sibling, z),
            device_id_type=MESH,
        )

    def sum1_copy(s, k):
        return pltpu.make_async_remote_copy(
            src_ref=out1.at[s, k],
            dst_ref=in1.at[s, k],
            send_sem=sum1_send.at[s, k],
            recv_sem=sum1_recv.at[s, k],
            device_id=(dp, zpair[k]),
            device_id_type=MESH,
        )

    def sum2_copy(s, k):
        return pltpu.make_async_remote_copy(
            src_ref=out2.at[s, k],
            dst_ref=in2.at[s, k],
            send_sem=sum2_send.at[s, k],
            recv_sem=sum2_recv.at[s, k],
            device_id=(dp, zpair[1 - k]),
            device_id_type=MESH,
        )

    def rows1_copy(s, k, quarter):
        return pltpu.make_async_remote_copy(
            src_ref=rows_g.at[s, quarter],
            dst_ref=rows_g.at[s, quarter],
            send_sem=rows1_send.at[s, k],
            recv_sem=rows1_recv.at[s, k],
            device_id=(dp, zpair[k]),
            device_id_type=MESH,
        )

    def rows2_copy(s, k, quarter):
        rows = pl.ds(k * half, half)
        return pltpu.make_async_remote_copy(
            src_ref=rows_g.at[s, quarter, rows],
            dst_ref=rows_g.at[s, quarter, rows],
            send_sem=rows2_send.at[s, k],
            recv_sem=rows2_recv.at[s, k],
            device_id=(dp, zpair[k]),
            device_id_type=MESH,
        )

    def loss_copy(group, j, arrival):
        spot = lax.rem(spots[group] + j, sizes[group]) if arrival else spots[group]
        return pltpu.make_async_remote_copy(
            src_ref=losses.at[group, spot],
            dst_ref=losses.at[group, spot],
            send_sem=loss_send.at[group, j],
            recv_sem=loss_recv.at[group, spot],
            device_id=peer(group, j),
            device_id_type=MESH,
        )

    def loss_out(group):
        losses[group, spots[group]] = loss_ref[...]
        for j in range(1, sizes[group]):
            loss_copy(group, j, False).start()

    def loss_in(group):
        for j in range(1, sizes[group]):
            loss_copy(group, j, True).wait_recv()
        loss_ref[...] = functools.reduce(
            jnp.add, [losses[group, spot] for spot in range(sizes[group])]
        )

    store[...] = store_ref[...].astype(jnp.float32)
    loss_ref[...] = jnp.zeros_like(loss_ref)
    total[...] = jnp.zeros_like(total)
    own_copy().start()
    own_copy().wait()

    def pass_on(i, sub):
        @pl.when(jnp.logical_and(i > 0, i < steps))
        def _():
            for way in range(2):
                ring_copy(i, way, sub, 0).wait_recv()

        @pl.when(i < steps - 1)
        def _():
            for way in range(2):
                ring_copy(i, way, sub, 1).start()

    def body(i, carry):
        pass_on(i, 0)

        @pl.when(jnp.logical_and(i >= 1, i < steps + 1))
        def _():
            s = i - 1
            slot = lax.rem(s, 2)
            side_copy(s, theirs).wait_recv()
            for n in range(2):
                part_y = jnp.dot(
                    held[s], proj_ref[:, n * 256 : (n + 1) * 256], preferred_element_type=jnp.float32
                )
                y_own[slot, 2 * n] = part_y[:, :128]
                y_own[slot, 2 * n + 1] = part_y[:, 128:]
            for k in range(2):
                rows = pl.ds(k * half, half)
                other = 3 - zpair[k] if k == 0 else zpair[k] + 1 - 2 * lax.rem(zpair[k], 2)
                out1[s, k, 0] = y_own[slot, zpair[k], rows, :].astype(jnp.bfloat16)
                out1[s, k, 1] = y_own[slot, other, rows, :].astype(jnp.bfloat16)
                sum1_copy(s, k).start()

        @pl.when(jnp.logical_and(i >= 2, i < steps + 2))
        def _():
            s = i - 2
            slot = lax.rem(s, 2)
            for k in range(2):
                rows = pl.ds(k * half, half)
                sum1_copy(s, k).wait_recv()
                passed = y_own[slot, zpair[1 - k], rows, :] + in1[s, k, 1].astype(jnp.float32)
                out2[s, k] = passed.astype(jnp.bfloat16)
                sum2_copy(s, k).start()
                y_keep[slot, rows, :] = y_own[slot, z, rows, :] + in1[s, k, 0].astype(jnp.float32)

        pass_on(i, 1)

        @pl.when(i < steps)
        def _():
            side_copy(i, mine).start()

        @pl.when(jnp.logical_and(i >= 3, i < steps + 3))
        def _():
            s = i - 3
            slot = lax.rem(s, 2)
            for k in range(2):
                sum2_copy(s, k).wait_recv()
            for chunk in range(4):
                ring_core, way = chunk // 2, chunk % 2
                at = cycle_position(x, y, ring_core)
                origin = cycle_device(lax.rem(at + (CHIPS - s if way == 0 else s), CHIPS), ring_core)
                token = pl.multiple_of((origin * 2 + way) * part, part)
                rows = pl.ds(chunk * part, part)
                inside = pl.ds((chunk % 2) * part, part)

                def seek(group, carry):
                    for j in range(8):
                        at_row = group * 8 + j
                        aim[pl.ds(chunk * part + at_row, 1), :] = store[
                            pl.ds(perm_ref[token + at_row], 1), :
                        ]
                    return carry

                lax.fori_loop(0, part // 8, seek, 0)
                diff = (
                    y_keep[slot, rows, :]
                    + in2[s, chunk // 2, inside, :].astype(jnp.float32)
                    - aim[rows, :]
                )
                rows_g[s, z, rows, :] = (diff * inv_root).astype(jnp.bfloat16)
                loss_ref[...] += jnp.sum((diff * diff).reshape(part // 8, 8, diff.shape[1]), axis=0)
            for k in range(2):
                rows1_copy(s, k, z).start()

        @pl.when(jnp.logical_and(i >= 4, i < steps + 4))
        def _():
            s = i - 4
            for k in range(2):
                rows1_copy(s, k, zpair[k]).wait_recv()
            for k in range(2):
                rows2_copy(s, k, zpair[1 - k]).start()

        @pl.when(i == steps + 3)
        def _():
            loss_out(0)

        @pl.when(i == steps + 4)
        def _():
            loss_in(0)
            loss_out(1)

        @pl.when(i >= 5)
        def _():
            s = i - 5
            for k in range(2):
                rows2_copy(s, k, 3 - zpair[k] if k == 0 else zpair[k] + 1 - 2 * lax.rem(zpair[k], 2)).wait_recv()
            rows = jnp.concatenate([rows_g[s, q] for q in range(4)], axis=1)
            for f in range(8):
                features = slice(f * 256, (f + 1) * 256)
                total[features, :] += lax.dot_general(
                    held[s, :, features], rows, (((0,), (0,)), ((), ())), preferred_element_type=jnp.float32
                )

        return carry

    lax.fori_loop(0, steps + 5, body, 0)
    loss_in(1)
    loss_out(2)

    def finish(s, carry):
        @pl.when(s < steps - 1)
        def _():
            for way in range(2):
                for sub in range(2):
                    ring_copy(s, way, sub, 1).wait_send()

        side_copy(s, mine).wait_send()
        for k in range(2):
            sum1_copy(s, k).wait_send()
            sum2_copy(s, k).wait_send()
            rows1_copy(s, k, z).wait_send()
            rows2_copy(s, k, zpair[1 - k]).wait_send()
        return carry

    lax.fori_loop(0, steps, finish, 0)
    loss_in(2)
    for group in range(3):
        for j in range(1, sizes[group]):
            loss_copy(group, j, False).wait_send()
    grad_ref[...] = total[...].astype(jnp.bfloat16)


def wide(hidden, proj, store, perm, inv_root):
    rows, features = hidden.shape
    columns = proj.shape[1]
    quarter = columns // 4
    block = 2 * rows
    half = block // 2
    pairs = pltpu.SemaphoreType.DMA((CHIPS, 2))
    vmem = pl.BlockSpec(memory_space=pltpu.VMEM)
    return pl.pallas_call(
        functools.partial(wide_kernel, inv_root),
        out_shape=(
            jax.ShapeDtypeStruct((features, columns), jnp.bfloat16),
            jax.ShapeDtypeStruct((8, quarter), jnp.float32),
        ),
        in_specs=[vmem, vmem, vmem, pl.BlockSpec(memory_space=pltpu.SMEM)],
        out_specs=(vmem, vmem),
        scratch_shapes=[
            pltpu.VMEM((CHIPS, block, features), jnp.bfloat16),
            pltpu.VMEM((features, columns), jnp.float32),
            pltpu.VMEM((2, 4, block, quarter), jnp.float32),
            pltpu.VMEM((2, block, quarter), jnp.float32),
            pltpu.VMEM((CHIPS, 2, 2, half, quarter), jnp.bfloat16),
            pltpu.VMEM((CHIPS, 2, 2, half, quarter), jnp.bfloat16),
            pltpu.VMEM((CHIPS, 2, half, quarter), jnp.bfloat16),
            pltpu.VMEM((CHIPS, 2, half, quarter), jnp.bfloat16),
            pltpu.VMEM((CHIPS, 4, block, quarter), jnp.bfloat16),
            pltpu.VMEM(store.shape, jnp.float32),
            pltpu.VMEM((block, quarter), jnp.float32),
            pltpu.VMEM((3, 2 * SIDE, 8, quarter), jnp.float32),
            pltpu.SemaphoreType.DMA,
        ]
        + [pltpu.SemaphoreType.DMA((CHIPS, 2, 2))] * 2
        + [pltpu.SemaphoreType.DMA((CHIPS,))] * 2
        + [pairs] * 8
        + [pltpu.SemaphoreType.DMA((3, 2 * SIDE))] * 2,
        compiler_params=pltpu.CompilerParams(
            collective_id=0, has_side_effects=True, vmem_limit_bytes=56 * 1024 * 1024
        ),
    )(hidden, proj, store, perm)


def shards(
    student_in, value_weight, folded_out, norm_gain, proj, teacher_codes, teacher_scales, perm
):
    sections = lax.axis_size("pipe")
    n_ranks = lax.axis_size("dp")
    rows, features = student_in.shape
    tokens = rows * n_ranks
    columns = proj.shape[1]
    total_cols = columns * n_ranks

    gain = norm_gain.reshape(sections, features // LANES, LANES)
    scales = jnp.broadcast_to(teacher_scales.astype(jnp.float32)[:, None], (rows, LANES))
    hidden, store = layers(student_in, value_weight[0], folded_out[0], gain, teacher_codes, scales)
    grad_proj, squared = wide(hidden, proj, store, perm, 1.0 / math.sqrt(tokens))
    loss = 0.5 * jnp.sum(squared) / (tokens * total_cols)
    return (grad_proj, loss)


def solution(mesh):
    return jax.shard_map(
        shards,
        mesh=mesh,
        in_specs=(
            P("dp", "pipe"),
            P("pipe", None, None),
            P("pipe", None, None),
            P("pipe", None),
            P("pipe", "dp"),
            P("dp", None),
            P("dp"),
            P(),
        ),
        out_specs=(P("pipe", "dp"), P()),
        check_vma=False,
    )
```

```python
import functools
import math

import jax
import jax.numpy as jnp
from jax import lax
from jax.experimental import pallas as pl
from jax.experimental.pallas import tpu as pltpu
from jax.sharding import PartitionSpec as P

MESH = pl.DeviceIdType.MESH
SIDE = 4
CHIPS = SIDE * SIDE
RANKS = 2 * CHIPS
LANES = 128


def place(dp):
    core = lax.rem(dp, 2)
    chip = dp // 2
    return chip // SIDE, lax.rem(chip, SIDE), core


def cycle_position(x, y, core):
    return SIDE * (y + core * (x - y)) + lax.rem(x + y, SIDE)


def cycle_device(position, core):
    major = position // SIDE
    minor = lax.rem(lax.rem(position, SIDE) - major + SIDE, SIDE)
    x = minor + core * (major - minor)
    y = major + core * (minor - major)
    return (x * SIDE + y) * 2 + core


def run_layers(
    eps,
    h_ref,
    value_ref,
    out_ref,
    gain_ref,
    codes_ref,
    scale_ref,
    hidden_ref,
    store_ref,
    w_value,
    w_out,
    gain_row,
    gain_own,
    gains,
    scale_row,
    products,
    normed,
    values,
    out1,
    in1,
    out2,
    in2,
    staged,
    own_sem,
    first_send,
    first_recv,
    near_send,
    near_recv,
    far_send,
    far_recv,
    side_send,
    side_recv,
    gain_send,
    gain_recv,
    sum1_send,
    sum1_recv,
    sum2_send,
    sum2_recv,
    stage_sem,
    code_send,
    code_recv,
):
    dp = lax.axis_index("dp")
    z = lax.axis_index("pipe")
    x, y, core = place(dp)
    sibling = dp + 1 - 2 * core
    zpair = (z + 1 - 2 * lax.rem(z, 2), 3 - z)
    rows, features = hidden_ref.shape
    head = value_ref.shape[-1]
    half = rows // 2
    weights = (w_value, w_out)
    width = 4 * features

    def greet_all():
        barrier = pltpu.get_barrier_semaphore()

        def greet(j, carry):
            pl.semaphore_signal(
                barrier, inc=1, device_id=(lax.rem(dp + j, RANKS), z), device_id_type=MESH
            )
            return carry

        lax.fori_loop(1, RANKS, greet, 0)
        for j in range(1, 4):
            pl.semaphore_signal(
                barrier, inc=1, device_id=(dp, lax.rem(z + j, 4)), device_id_type=MESH
            )
        pl.semaphore_wait(barrier, RANKS + 2)

    def first_copy(kind, j):
        to = lax.rem(z + j, 4)
        if kind == 0:
            source = value_ref.at[to, x, y, core]
        else:
            source = out_ref.at[x, y, core, :, pl.ds(pl.multiple_of(to * features, features), features)]
        return pltpu.make_async_remote_copy(
            src_ref=source,
            dst_ref=weights[kind].at[4 - j, x, y, core],
            send_sem=first_send.at[kind, j - 1],
            recv_sem=first_recv.at[kind, 3 - j],
            device_id=(dp, to),
            device_id_type=MESH,
        )

    def first_arrival(kind, r):
        block = weights[kind].at[r, x, y, core]
        return pltpu.make_async_remote_copy(
            src_ref=block,
            dst_ref=block,
            send_sem=first_send.at[kind, r - 1],
            recv_sem=first_recv.at[kind, r - 1],
            device_id=(dp, lax.rem(z + r, 4)),
            device_id_type=MESH,
        )

    spot = (x, y)

    def near_copy(kind, r, j, arrival):
        there = lax.rem(spot[kind] + j, SIDE)
        at = there if arrival else spot[kind]
        block = w_value.at[r, at, y, core] if kind == 0 else w_out.at[r, x, at, core]
        chip = there * SIDE + y if kind == 0 else x * SIDE + there
        return pltpu.make_async_remote_copy(
            src_ref=block,
            dst_ref=block,
            send_sem=near_send.at[kind, r - 1, j],
            recv_sem=near_recv.at[kind, r - 1, at],
            device_id=(chip * 2 + core, z),
            device_id_type=MESH,
        )

    def far_copy(kind, r, j, arrival):
        there = lax.rem(spot[1 - kind] + j, SIDE)
        at = there if arrival else spot[1 - kind]
        block = w_value.at[r, :, at, core] if kind == 0 else w_out.at[r, at, :, core]
        chip = there * SIDE + y if kind == 1 else x * SIDE + there
        return pltpu.make_async_remote_copy(
            src_ref=block,
            dst_ref=block,
            send_sem=far_send.at[kind, r - 1, j],
            recv_sem=far_recv.at[kind, r - 1, at],
            device_id=(chip * 2 + core, z),
            device_id_type=MESH,
        )

    def side_copy(kind, r, j, owner):
        at = lax.rem(spot[1 - kind] + j, SIDE)
        block = w_value.at[r, :, at, owner] if kind == 0 else w_out.at[r, at, :, owner]
        return pltpu.make_async_remote_copy(
            src_ref=block,
            dst_ref=block,
            send_sem=side_send.at[kind, r - 1, at],
            recv_sem=side_recv.at[kind, r - 1, at],
            device_id=(sibling, z),
            device_id_type=MESH,
        )

    def gain_copy(j):
        to = lax.rem(z + j, 4)
        return pltpu.make_async_remote_copy(
            src_ref=gain_own.at[to],
            dst_ref=gains.at[4 - j],
            send_sem=gain_send.at[j - 1],
            recv_sem=gain_recv.at[3 - j],
            device_id=(dp, to),
            device_id_type=MESH,
        )

    def own_copies():
        columns = pl.ds(pl.multiple_of(z * features, features), features)
        return (
            pltpu.make_async_copy(value_ref.at[z], w_value.at[0], own_sem.at[0]),
            pltpu.make_async_copy(out_ref.at[:, :, :, :, columns], w_out.at[0], own_sem.at[1]),
        )

    def stage_copy(d):
        columns = pl.ds(pl.multiple_of((d * 4 + z) * LANES, LANES), LANES)
        return pltpu.make_async_copy(codes_ref.at[:, columns], staged.at[d], stage_sem.at[d])

    def code_copy(d):
        return pltpu.make_async_remote_copy(
            src_ref=staged.at[d],
            dst_ref=store_ref.at[pl.ds(pl.multiple_of(dp * rows, rows), rows)],
            send_sem=code_send.at[d],
            recv_sem=code_recv.at[dp],
            device_id=(d, z),
            device_id_type=MESH,
        )

    def code_arrival(d):
        block = store_ref.at[pl.ds(pl.multiple_of(d * rows, rows), rows)]
        return pltpu.make_async_remote_copy(
            src_ref=block,
            dst_ref=block,
            send_sem=code_send.at[d],
            recv_sem=code_recv.at[d],
            device_id=(d, z),
            device_id_type=MESH,
        )

    def sum_copy(phase, layer, k):
        source, target, send, recv = (
            (out1, in1, sum1_send, sum1_recv),
            (out2, in2, sum2_send, sum2_recv),
        )[phase]
        return pltpu.make_async_remote_copy(
            src_ref=source.at[layer, k],
            dst_ref=target.at[layer, k],
            send_sem=send.at[layer, k],
            recv_sem=recv.at[layer, k],
            device_id=(dp, zpair[k ^ phase]),
            device_id_type=MESH,
        )

    small = (
        pltpu.make_async_copy(gain_ref, gain_row, own_sem.at[2]),
        pltpu.make_async_copy(scale_ref, scale_row, own_sem.at[3]),
        pltpu.make_async_copy(h_ref, hidden_ref, own_sem.at[4]),
    )
    for copy in small:
        copy.start()
    greet_all()
    for j in (1, 3, 2):
        first_copy(0, j).start()
        first_copy(1, j).start()
    for copy in own_copies():
        copy.start()

    def fetch(d, carry):
        stage_copy(d).start()
        return carry

    lax.fori_loop(0, RANKS, fetch, 0)
    for copy in small:
        copy.wait()
    for part in range(4):
        for j in range(features // LANES):
            at = part * features + j * LANES
            gain_own[part, j : j + 1, :] = gain_row[:, at : at + LANES]
    for j in range(1, 4):
        gain_copy(j).start()
    gains[0] = gain_own[z]
    scale = jnp.broadcast_to(scale_row[...].astype(jnp.float32), (rows, LANES)).T

    def scale_codes(d, carry):
        stage_copy(d).wait()
        staged[d] = (staged[d].astype(jnp.float32) * scale).astype(jnp.bfloat16)
        return carry

    lax.fori_loop(0, RANKS, scale_codes, 0)
    store_ref[pl.ds(pl.multiple_of(dp * rows, rows), rows), :] = staged[dp]

    def turn(k):
        layer = k + jnp.where(k >= z, 1, 0)
        return lax.rem(layer - z + 4, 4)

    def spread_near(k, carry):
        r = turn(k)
        for kind in range(2):
            first_arrival(kind, r).wait_recv()
            for j in (1, 3, 2):
                near_copy(kind, r, j, False).start()
        return carry

    def spread_far(k):
        r = turn(k)
        for kind in range(2):
            for j in (1, 3, 2):
                near_copy(kind, r, j, True).wait_recv()
            for j in (1, 3, 2):
                far_copy(kind, r, j, False).start()
        for kind in range(2):
            side_copy(kind, r, 0, core).start()

    def settle(r, order):
        for j in order:
            for kind in range(2):
                far_copy(kind, r, j, True).wait_recv()
                side_copy(kind, r, j, core).start()

    lax.fori_loop(0, 3, spread_near, 0)
    spread_far(0)
    for copy in own_copies():
        copy.wait()
    for j in range(1, 4):
        gain_copy(j).wait()

    def send_codes(j, carry):
        code_copy(lax.rem(dp + j, RANKS)).start()
        return carry

    def layer_step(layer, carry):
        r = lax.rem(layer - z + 4, 4)

        @pl.when(layer != z)
        def _():
            settle(r, (1,))

        @pl.when(layer < 2)
        def _():
            spread_far(layer + 1)

        @pl.when(layer != z)
        def _():
            settle(r, (3, 2))
            for kind in range(2):
                for j in range(SIDE):
                    side_copy(kind, r, j, 1 - core).wait_recv()

            @pl.when(layer == 3 - jnp.where(z == 3, 1, 0))
            def _():
                lax.fori_loop(1, RANKS, send_codes, 0)

        gain = gains[r].astype(jnp.float32)
        squares = jnp.zeros((rows, LANES), jnp.float32)
        for j in range(features // LANES):
            columns = slice(j * LANES, (j + 1) * LANES)
            tile = hidden_ref[:, columns].astype(jnp.float32)
            squares += tile * tile
            normed[:, columns] = (tile * gain[j : j + 1, :]).astype(jnp.bfloat16)
        squares = jnp.broadcast_to(jnp.sum(squares, axis=1, keepdims=True), (rows, LANES))
        high = squares.astype(jnp.bfloat16)
        low = (squares - high.astype(jnp.float32)).astype(jnp.bfloat16)
        lane = lax.broadcasted_iota(jnp.int32, (rows, LANES), 1)
        products[:, :head] = jnp.dot(
            normed[...], w_value[r].reshape(features, head), preferred_element_type=jnp.float32
        )
        products[:, head:] = squares
        for k in range(2):
            part = slice(k * half, (k + 1) * half)
            out1[layer, k, :, :head] = products[part, :head].astype(jnp.bfloat16)
            out1[layer, k, :, head:] = jnp.where(
                lane[part] < LANES // 2, high[part].astype(jnp.float32), low[part].astype(jnp.float32)
            ).astype(jnp.bfloat16)
            sum_copy(0, layer, k).start()

        def arrived(buffer, k):
            marks = buffer[layer, k, :, head:].astype(jnp.float32)
            return buffer[layer, k, :, :head].astype(jnp.float32), marks + pltpu.roll(marks, LANES // 2, 1)

        for k in range(2):
            part = slice(k * half, (k + 1) * half)
            sum_copy(0, layer, k).wait_recv()
            more, marks = arrived(in1, k)
            so_far = products[part, :head] + more
            squares = products[part, head:] + marks
            products[part, :head] = so_far
            products[part, head:] = squares
            high = squares.astype(jnp.bfloat16)
            low = (squares - high.astype(jnp.float32)).astype(jnp.bfloat16)
            out2[layer, k, :, :head] = so_far.astype(jnp.bfloat16)
            out2[layer, k, :, head:] = jnp.where(
                lane[part] < LANES // 2, high.astype(jnp.float32), low.astype(jnp.float32)
            ).astype(jnp.bfloat16)
            sum_copy(1, layer, k).start()
        for k in range(2):
            part = slice(k * half, (k + 1) * half)
            sum_copy(1, layer, k).wait_recv()
            more, marks = arrived(in2, k)
            scale = lax.rsqrt((products[part, head:] + marks) * (1.0 / width) + eps)
            for j in range(head // LANES):
                columns = slice(j * LANES, (j + 1) * LANES)
                values[part, columns] = ((products[part, columns] + more[:, columns]) * scale).astype(
                    jnp.bfloat16
                )
        for n in range(features // 512):
            columns = slice(n * 512, (n + 1) * 512)
            branch = jnp.dot(
                values[...],
                w_out[r, :, :, :, :, columns].reshape(head, 512),
                preferred_element_type=jnp.float32,
            )
            hidden_ref[:, columns] = (hidden_ref[:, columns].astype(jnp.float32) + branch).astype(
                jnp.bfloat16
            )
        return carry

    lax.fori_loop(0, 4, layer_step, 0)

    for k in range(2):
        for layer in range(4):
            sum_copy(0, layer, k).wait_send()
            sum_copy(1, layer, k).wait_send()
    for j in range(1, 4):
        for kind in range(2):
            first_copy(kind, j).wait_send()
            for r in range(1, 4):
                near_copy(kind, r, j, False).wait_send()
                far_copy(kind, r, j, False).wait_send()
    for kind in range(2):
        for r in range(1, 4):
            for j in range(SIDE):
                side_copy(kind, r, j, core).wait_send()

    def codes_in():
        def arrive(j, carry):
            code_arrival(lax.rem(dp + j, RANKS)).wait_recv()
            return carry

        lax.fori_loop(1, RANKS, arrive, 0)

    def codes_out():
        def leave(j, carry):
            code_copy(lax.rem(dp + j, RANKS)).wait_send()
            return carry

        lax.fori_loop(1, RANKS, leave, 0)

    return codes_in, codes_out


def run_wide(
    inv_root,
    share,
    codes_in,
    store_ref,
    perm_ref,
    proj_ref,
    grad_ref,
    loss_ref,
    held,
    squares,
    total,
    y_own,
    y_keep,
    out1,
    in1,
    out2,
    in2,
    rows_g,
    store,
    aim,
    losses,
    ring_send,
    ring_recv,
    side_send,
    side_recv,
    sum1_send,
    sum1_recv,
    sum2_send,
    sum2_recv,
    rows1_send,
    rows1_recv,
    rows2_send,
    rows2_recv,
    loss_send,
    loss_recv,
):
    dp = lax.axis_index("dp")
    z = lax.axis_index("pipe")
    x, y, core = place(dp)
    here = cycle_position(x, y, core)
    after = cycle_device(lax.rem(here + 1, CHIPS), core)
    before = cycle_device(lax.rem(here + CHIPS - 1, CHIPS), core)
    sibling = dp + 1 - 2 * core
    za = z + 1 - 2 * lax.rem(z, 2)
    zb = 3 - z
    steps = CHIPS
    part = held.shape[1] // 4
    block = 4 * part
    half = block // 2
    zpair = (za, zb)
    ring = (after, before)

    sizes = (4, SIDE, 2 * SIDE)
    spots = (z, y, 2 * x + core)

    def peer(group, j):
        spot = lax.rem(spots[group] + j, sizes[group])
        if group == 0:
            return dp, spot
        if group == 1:
            return (x * SIDE + spot) * 2 + core, z
        return ((spot // 2) * SIDE + y) * 2 + lax.rem(spot, 2), z

    mine = pl.multiple_of(core * 2 * part, 2 * part)
    theirs = pl.multiple_of((1 - core) * 2 * part, 2 * part)

    def ring_copy(s, way, sub, later):
        start = mine + way * part + sub * (part // 2)
        rows = pl.ds(pl.multiple_of(start, part // 2), part // 2)
        return pltpu.make_async_remote_copy(
            src_ref=held.at[s, rows],
            dst_ref=held.at[s + later, rows],
            send_sem=ring_send.at[s, way, sub],
            recv_sem=ring_recv.at[s + later, way, sub],
            device_id=(ring[way], z),
            device_id_type=MESH,
        )

    def side_copy(s, start):
        rows = pl.ds(start, 2 * part)
        return pltpu.make_async_remote_copy(
            src_ref=held.at[s, rows],
            dst_ref=held.at[s, rows],
            send_sem=side_send.at[s],
            recv_sem=side_recv.at[s],
            device_id=(sibling, z),
            device_id_type=MESH,
        )

    def sum1_copy(s, k):
        return pltpu.make_async_remote_copy(
            src_ref=out1.at[s, k],
            dst_ref=in1.at[s, k],
            send_sem=sum1_send.at[s, k],
            recv_sem=sum1_recv.at[s, k],
            device_id=(dp, zpair[k]),
            device_id_type=MESH,
        )

    def sum2_copy(s, k):
        return pltpu.make_async_remote_copy(
            src_ref=out2.at[s, k],
            dst_ref=in2.at[s, k],
            send_sem=sum2_send.at[s, k],
            recv_sem=sum2_recv.at[s, k],
            device_id=(dp, zpair[1 - k]),
            device_id_type=MESH,
        )

    def rows1_copy(s, k, quarter):
        return pltpu.make_async_remote_copy(
            src_ref=rows_g.at[s, quarter],
            dst_ref=rows_g.at[s, quarter],
            send_sem=rows1_send.at[s, k],
            recv_sem=rows1_recv.at[s, k],
            device_id=(dp, zpair[k]),
            device_id_type=MESH,
        )

    def rows2_copy(s, k, quarter):
        rows = pl.ds(k * half, half)
        return pltpu.make_async_remote_copy(
            src_ref=rows_g.at[s, quarter, rows],
            dst_ref=rows_g.at[s, quarter, rows],
            send_sem=rows2_send.at[s, k],
            recv_sem=rows2_recv.at[s, k],
            device_id=(dp, zpair[k]),
            device_id_type=MESH,
        )

    def loss_copy(group, j, arrival):
        spot = lax.rem(spots[group] + j, sizes[group]) if arrival else spots[group]
        return pltpu.make_async_remote_copy(
            src_ref=losses.at[group, spot],
            dst_ref=losses.at[group, spot],
            send_sem=loss_send.at[group, j],
            recv_sem=loss_recv.at[group, spot],
            device_id=peer(group, j),
            device_id_type=MESH,
        )

    def loss_out(group):
        losses[group, spots[group]] = squares[...]
        for j in range(1, sizes[group]):
            loss_copy(group, j, False).start()

    def loss_in(group):
        for j in range(1, sizes[group]):
            loss_copy(group, j, True).wait_recv()
        squares[...] = functools.reduce(
            jnp.add, [losses[group, spot] for spot in range(sizes[group])]
        )

    squares[...] = jnp.zeros_like(squares)
    total[...] = jnp.zeros_like(total)

    def pass_on(i, sub):
        @pl.when(jnp.logical_and(i > 0, i < steps))
        def _():
            for way in range(2):
                ring_copy(i, way, sub, 0).wait_recv()

        @pl.when(i < steps - 1)
        def _():
            for way in range(2):
                ring_copy(i, way, sub, 1).start()

    def body(i, carry):
        pass_on(i, 0)

        @pl.when(jnp.logical_and(i >= 1, i < steps + 1))
        def _():
            s = i - 1
            slot = lax.rem(s, 2)
            side_copy(s, theirs).wait_recv()
            for n in range(2):
                part_y = jnp.dot(
                    held[s], proj_ref[:, n * 256 : (n + 1) * 256], preferred_element_type=jnp.float32
                )
                y_own[slot, 2 * n] = part_y[:, :128]
                y_own[slot, 2 * n + 1] = part_y[:, 128:]
            for k in range(2):
                rows = pl.ds(k * half, half)
                other = 3 - zpair[k] if k == 0 else zpair[k] + 1 - 2 * lax.rem(zpair[k], 2)
                out1[s, k, 0] = y_own[slot, zpair[k], rows, :].astype(jnp.bfloat16)
                out1[s, k, 1] = y_own[slot, other, rows, :].astype(jnp.bfloat16)
                sum1_copy(s, k).start()

        @pl.when(i == 4)
        def _():
            codes_in()
            store[...] = store_ref[...].astype(jnp.float32)

        @pl.when(jnp.logical_and(i >= 4, i < steps + 4))
        def _():
            s = i - 4
            slot = lax.rem(s, 2)
            for k in range(2):
                sum2_copy(s, k).wait_recv()
            for chunk in range(4):
                ring_core, way = chunk // 2, chunk % 2
                at = cycle_position(x, y, ring_core)
                origin = cycle_device(lax.rem(at + (CHIPS - s if way == 0 else s), CHIPS), ring_core)
                token = pl.multiple_of((origin * 2 + way) * part, part)
                rows = pl.ds(chunk * part, part)
                inside = pl.ds((chunk % 2) * part, part)

                def seek(group, carry):
                    for j in range(8):
                        at_row = group * 8 + j
                        aim[pl.ds(chunk * part + at_row, 1), :] = store[
                            pl.ds(perm_ref[token + at_row], 1), :
                        ]
                    return carry

                lax.fori_loop(0, part // 8, seek, 0)
                diff = (
                    y_keep[slot, rows, :]
                    + in2[s, chunk // 2, inside, :].astype(jnp.float32)
                    - aim[rows, :]
                )
                rows_g[s, z, rows, :] = (diff * inv_root).astype(jnp.bfloat16)
                squares[...] += jnp.sum((diff * diff).reshape(part // 8, 8, diff.shape[1]), axis=0)
            for k in range(2):
                rows1_copy(s, k, z).start()

        pass_on(i, 1)

        @pl.when(i < steps)
        def _():
            side_copy(i, mine).start()

        @pl.when(jnp.logical_and(i >= 2, i < steps + 2))
        def _():
            s = i - 2
            slot = lax.rem(s, 2)
            for k in range(2):
                rows = pl.ds(k * half, half)
                sum1_copy(s, k).wait_recv()
                passed = y_own[slot, zpair[1 - k], rows, :] + in1[s, k, 1].astype(jnp.float32)
                out2[s, k] = passed.astype(jnp.bfloat16)
                sum2_copy(s, k).start()
                y_keep[slot, rows, :] = y_own[slot, z, rows, :] + in1[s, k, 0].astype(jnp.float32)

        @pl.when(jnp.logical_and(i >= 5, i < steps + 5))
        def _():
            s = i - 5
            for k in range(2):
                rows1_copy(s, k, zpair[k]).wait_recv()
            for k in range(2):
                rows2_copy(s, k, zpair[1 - k]).start()

        @pl.when(i == steps + 3)
        def _():
            loss_out(0)

        @pl.when(i == steps + 4)
        def _():
            loss_in(0)
            loss_out(1)

        @pl.when(i == steps + 5)
        def _():
            loss_in(1)
            loss_out(2)

        @pl.when(i >= 6)
        def _():
            s = i - 6
            for k in range(2):
                rows2_copy(s, k, 3 - zpair[k] if k == 0 else zpair[k] + 1 - 2 * lax.rem(zpair[k], 2)).wait_recv()
            rows = jnp.concatenate([rows_g[s, q] for q in range(4)], axis=1)
            for f in range(8):
                features = slice(f * 256, (f + 1) * 256)
                total[features, :] += lax.dot_general(
                    held[s, :, features], rows, (((0,), (0,)), ((), ())), preferred_element_type=jnp.float32
                )

        return carry

    lax.fori_loop(0, steps + 6, body, 0)

    def finish(s, carry):
        @pl.when(s < steps - 1)
        def _():
            for way in range(2):
                for sub in range(2):
                    ring_copy(s, way, sub, 1).wait_send()

        side_copy(s, mine).wait_send()
        for k in range(2):
            sum1_copy(s, k).wait_send()
            sum2_copy(s, k).wait_send()
            rows1_copy(s, k, z).wait_send()
            rows2_copy(s, k, zpair[1 - k]).wait_send()
        return carry

    lax.fori_loop(0, steps, finish, 0)
    loss_in(2)
    for group in range(3):
        for j in range(1, sizes[group]):
            loss_copy(group, j, False).wait_send()
    grad_ref[...] = total[...].astype(jnp.bfloat16)
    loss_ref[0, 0] = jnp.sum(squares[...]) * share


LAYER_SCRATCH = 32


def kernel(
    eps,
    inv_root,
    share,
    h_ref,
    value_ref,
    out_ref,
    gain_ref,
    proj_ref,
    codes_ref,
    scale_ref,
    perm_ref,
    grad_ref,
    loss_ref,
    held,
    store_ref,
    proj,
    proj_sem,
    *scratch,
):
    core = lax.rem(lax.axis_index("dp"), 2)
    rows = held.shape[1] // 2
    fetch_proj = pltpu.make_async_copy(proj_ref, proj, proj_sem)
    fetch_proj.start()
    codes_in, codes_out = run_layers(
        eps,
        h_ref,
        value_ref,
        out_ref,
        gain_ref,
        codes_ref,
        scale_ref,
        held.at[0, pl.ds(pl.multiple_of(core * rows, rows), rows)],
        store_ref,
        *scratch[:LAYER_SCRATCH],
    )
    fetch_proj.wait()
    run_wide(
        inv_root,
        share,
        codes_in,
        store_ref,
        perm_ref,
        proj,
        grad_ref,
        loss_ref,
        held,
        *scratch[LAYER_SCRATCH:],
    )
    codes_out()


def distill(hidden, value_weight, folded_out, gain, proj, codes, scales, perm):
    rows, features = hidden.shape
    head = value_weight.shape[1]
    columns = proj.shape[1]
    quarter = columns // 4
    tokens = rows * RANKS
    block = 2 * rows
    wide_half = block // 2
    half = rows // 2
    grid = (4, SIDE, SIDE, 2)
    value_weight = value_weight.reshape(*grid, features // RANKS, head)
    folded_out = folded_out.reshape(*grid[1:], head // RANKS, 4 * features)
    bf16, f32 = jnp.bfloat16, jnp.float32
    dma = pltpu.SemaphoreType.DMA
    message = pltpu.VMEM((4, 2, half, head + LANES), bf16)
    lanes = (features // LANES, LANES)
    layer_scratch = [
        pltpu.VMEM((*grid, features // RANKS, head), bf16),
        pltpu.VMEM((*grid, head // RANKS, features), bf16),
        pltpu.VMEM(gain.shape, bf16),
        pltpu.VMEM((4, *lanes), bf16),
        pltpu.VMEM((4, *lanes), bf16),
        pltpu.VMEM(scales.shape, bf16),
        pltpu.VMEM((rows, head + LANES), f32),
        pltpu.VMEM((rows, features), bf16),
        pltpu.VMEM((rows, head), bf16),
        message,
        message,
        message,
        message,
        pltpu.VMEM((RANKS, rows, LANES), bf16),
        dma((5,)),
        dma((2, 3)),
        dma((2, 3)),
        *[dma((2, 3, SIDE))] * 6,
        dma((3,)),
        dma((3,)),
        *[dma((4, 2))] * 4,
        *[dma((RANKS,))] * 3,
    ]
    wide_scratch = [
        pltpu.VMEM((8, quarter), f32),
        pltpu.VMEM((features, columns), f32),
        pltpu.VMEM((2, 4, block, quarter), f32),
        pltpu.VMEM((2, block, quarter), f32),
        pltpu.VMEM((CHIPS, 2, 2, wide_half, quarter), bf16),
        pltpu.VMEM((CHIPS, 2, 2, wide_half, quarter), bf16),
        pltpu.VMEM((CHIPS, 2, wide_half, quarter), bf16),
        pltpu.VMEM((CHIPS, 2, wide_half, quarter), bf16),
        pltpu.VMEM((CHIPS, 4, block, quarter), bf16),
        pltpu.VMEM((tokens, LANES), f32),
        pltpu.VMEM((block, quarter), f32),
        pltpu.VMEM((3, 2 * SIDE, 8, quarter), f32),
        dma((CHIPS, 2, 2)),
        dma((CHIPS, 2, 2)),
        dma((CHIPS,)),
        dma((CHIPS,)),
        dma((CHIPS, 2)),
        dma((CHIPS, 2)),
        dma((CHIPS, 2)),
        dma((CHIPS, 2)),
        dma((CHIPS, 2)),
        dma((CHIPS, 2)),
        dma((CHIPS, 2)),
        dma((CHIPS, 2)),
        dma((3, 2 * SIDE)),
        dma((3, 2 * SIDE)),
    ]
    vmem = pl.BlockSpec(memory_space=pltpu.VMEM)
    smem = pl.BlockSpec(memory_space=pltpu.SMEM)
    anywhere = pl.BlockSpec(memory_space=pl.ANY)
    return pl.pallas_call(
        functools.partial(kernel, 1e-5, 1.0 / math.sqrt(tokens), 0.5 / (tokens * columns * RANKS)),
        out_shape=(
            jax.ShapeDtypeStruct((features, columns), bf16),
            jax.ShapeDtypeStruct((1, 1), f32),
        ),
        in_specs=[anywhere] * 7 + [smem],
        out_specs=(vmem, smem),
        scratch_shapes=[
            pltpu.VMEM((CHIPS, block, features), bf16),
            pltpu.VMEM((tokens, LANES), bf16),
            pltpu.VMEM(proj.shape, bf16),
            dma,
        ]
        + layer_scratch
        + wide_scratch,
        compiler_params=pltpu.CompilerParams(
            collective_id=0, has_side_effects=True, vmem_limit_bytes=63 * 1024 * 1024
        ),
    )(hidden, value_weight, folded_out, gain, proj, codes, scales, perm)


def shards(
    student_in, value_weight, folded_out, norm_gain, proj, teacher_codes, teacher_scales, perm
):
    grad_proj, loss = distill(
        student_in,
        value_weight[0],
        folded_out[0],
        norm_gain,
        proj,
        teacher_codes,
        teacher_scales[None, :],
        perm,
    )
    return (grad_proj, loss[0, 0])


def solution(mesh):
    return jax.shard_map(
        shards,
        mesh=mesh,
        in_specs=(
            P("dp", "pipe"),
            P("pipe", None, None),
            P("pipe", None, None),
            P("pipe", None),
            P("pipe", "dp"),
            P("dp", None),
            P("dp"),
            P(),
        ),
        out_specs=(P("pipe", "dp"), P()),
        check_vma=False,
    )
```

```python
import functools
import math

import jax
import jax.numpy as jnp
from jax import lax
from jax.experimental import pallas as pl
from jax.experimental.pallas import tpu as pltpu
from jax.sharding import PartitionSpec as P

MESH = pl.DeviceIdType.MESH
SIDE = 4
CHIPS = SIDE * SIDE
RANKS = 2 * CHIPS
LANES = 128


def place(dp):
    core = lax.rem(dp, 2)
    chip = dp // 2
    return chip // SIDE, lax.rem(chip, SIDE), core


def cycle_position(x, y, core):
    return SIDE * (y + core * (x - y)) + lax.rem(x + y, SIDE)


def cycle_device(position, core):
    major = position // SIDE
    minor = lax.rem(lax.rem(position, SIDE) - major + SIDE, SIDE)
    x = minor + core * (major - minor)
    y = major + core * (minor - major)
    return (x * SIDE + y) * 2 + core


def run_layers(
    eps,
    h_ref,
    value_ref,
    out_ref,
    gain_ref,
    codes_ref,
    scale_ref,
    hidden_ref,
    store_ref,
    w_value,
    w_out,
    gain_row,
    gain_own,
    gains,
    scale_row,
    products,
    normed,
    values,
    out1,
    in1,
    out2,
    in2,
    staged,
    own_sem,
    first_send,
    first_recv,
    late_send,
    near_send,
    near_recv,
    far_send,
    far_recv,
    side_send,
    side_recv,
    gain_send,
    gain_recv,
    sum1_send,
    sum1_recv,
    sum2_send,
    sum2_recv,
    stage_sem,
    code_send,
    code_recv,
):
    dp = lax.axis_index("dp")
    z = lax.axis_index("pipe")
    x, y, core = place(dp)
    sibling = dp + 1 - 2 * core
    zpair = (z + 1 - 2 * lax.rem(z, 2), 3 - z)
    rows, features = hidden_ref.shape
    head = value_ref.shape[-1]
    half = rows // 2
    weights = (w_value, w_out)
    width = 4 * features

    def greet_all():
        barrier = pltpu.get_barrier_semaphore()

        def greet(j, carry):
            pl.semaphore_signal(
                barrier, inc=1, device_id=(lax.rem(dp + j, RANKS), z), device_id_type=MESH
            )
            return carry

        lax.fori_loop(1, RANKS, greet, 0)
        for j in range(1, 4):
            pl.semaphore_signal(
                barrier, inc=1, device_id=(dp, lax.rem(z + j, 4)), device_id_type=MESH
            )
        pl.semaphore_wait(barrier, RANKS + 2)

    def first_copy(kind, j):
        to = lax.rem(z + j, 4)
        if kind == 0:
            source = value_ref.at[to, x, y, core]
        else:
            source = out_ref.at[x, y, core, :, pl.ds(pl.multiple_of(to * features, features), features)]
        return pltpu.make_async_remote_copy(
            src_ref=source,
            dst_ref=weights[kind].at[4 - j, x, y, core],
            send_sem=first_send.at[kind, j - 1],
            recv_sem=first_recv.at[kind, 3 - j],
            device_id=(dp, to),
            device_id_type=MESH,
        )

    def first_arrival(kind, r):
        block = weights[kind].at[r, x, y, core]
        return pltpu.make_async_remote_copy(
            src_ref=block,
            dst_ref=block,
            send_sem=first_send.at[kind, r - 1],
            recv_sem=first_recv.at[kind, r - 1],
            device_id=(dp, lax.rem(z + r, 4)),
            device_id_type=MESH,
        )

    spot = (x, y)

    def near_copy(kind, r, j, arrival):
        there = lax.rem(spot[kind] + j, SIDE)
        at = there if arrival else spot[kind]
        block = w_value.at[r, at, y, core] if kind == 0 else w_out.at[r, x, at, core]
        chip = there * SIDE + y if kind == 0 else x * SIDE + there
        return pltpu.make_async_remote_copy(
            src_ref=block,
            dst_ref=block,
            send_sem=near_send.at[kind, r - 1, j],
            recv_sem=near_recv.at[kind, r - 1, at],
            device_id=(chip * 2 + core, z),
            device_id_type=MESH,
        )

    def far_copy(kind, r, j, arrival):
        there = lax.rem(spot[1 - kind] + j, SIDE)
        at = there if arrival else spot[1 - kind]
        block = w_value.at[r, :, at, core] if kind == 0 else w_out.at[r, at, :, core]
        chip = there * SIDE + y if kind == 1 else x * SIDE + there
        return pltpu.make_async_remote_copy(
            src_ref=block,
            dst_ref=block,
            send_sem=far_send.at[kind, r - 1, j],
            recv_sem=far_recv.at[kind, r - 1, at],
            device_id=(chip * 2 + core, z),
            device_id_type=MESH,
        )

    def late_copy(kind, j):
        to = lax.rem(z + j, 4)
        at = lax.rem(spot[1 - kind] + 2, SIDE)
        if kind == 0:
            source = value_ref.at[to, :, at, core]
            target = w_value.at[4 - j, :, at, core]
        else:
            source = out_ref.at[at, :, core, :, pl.ds(pl.multiple_of(to * features, features), features)]
            target = w_out.at[4 - j, at, :, core]
        return pltpu.make_async_remote_copy(
            src_ref=source,
            dst_ref=target,
            send_sem=late_send.at[kind, j - 1],
            recv_sem=far_recv.at[kind, 3 - j, at],
            device_id=(dp, to),
            device_id_type=MESH,
        )

    def is_late(j):
        return z + jnp.where(z < lax.rem(z + j, 4), 1, 0) > 1

    def side_copy(kind, r, j, owner):
        at = lax.rem(spot[1 - kind] + j, SIDE)
        block = w_value.at[r, :, at, owner] if kind == 0 else w_out.at[r, at, :, owner]
        return pltpu.make_async_remote_copy(
            src_ref=block,
            dst_ref=block,
            send_sem=side_send.at[kind, r - 1, at],
            recv_sem=side_recv.at[kind, r - 1, at],
            device_id=(sibling, z),
            device_id_type=MESH,
        )

    def gain_copy(j):
        to = lax.rem(z + j, 4)
        return pltpu.make_async_remote_copy(
            src_ref=gain_own.at[to],
            dst_ref=gains.at[4 - j],
            send_sem=gain_send.at[j - 1],
            recv_sem=gain_recv.at[3 - j],
            device_id=(dp, to),
            device_id_type=MESH,
        )

    def own_copies():
        columns = pl.ds(pl.multiple_of(z * features, features), features)
        return (
            pltpu.make_async_copy(value_ref.at[z], w_value.at[0], own_sem.at[0]),
            pltpu.make_async_copy(out_ref.at[:, :, :, :, columns], w_out.at[0], own_sem.at[1]),
        )

    def stage_copy(d):
        columns = pl.ds(pl.multiple_of((d * 4 + z) * LANES, LANES), LANES)
        return pltpu.make_async_copy(codes_ref.at[:, columns], staged.at[d], stage_sem.at[d])

    def code_copy(d):
        return pltpu.make_async_remote_copy(
            src_ref=staged.at[d],
            dst_ref=store_ref.at[pl.ds(pl.multiple_of(dp * rows, rows), rows)],
            send_sem=code_send.at[d],
            recv_sem=code_recv.at[dp],
            device_id=(d, z),
            device_id_type=MESH,
        )

    def code_arrival(d):
        block = store_ref.at[pl.ds(pl.multiple_of(d * rows, rows), rows)]
        return pltpu.make_async_remote_copy(
            src_ref=block,
            dst_ref=block,
            send_sem=code_send.at[d],
            recv_sem=code_recv.at[d],
            device_id=(d, z),
            device_id_type=MESH,
        )

    def sum_copy(phase, layer, k):
        source, target, send, recv = (
            (out1, in1, sum1_send, sum1_recv),
            (out2, in2, sum2_send, sum2_recv),
        )[phase]
        return pltpu.make_async_remote_copy(
            src_ref=source.at[layer, k],
            dst_ref=target.at[layer, k],
            send_sem=send.at[layer, k],
            recv_sem=recv.at[layer, k],
            device_id=(dp, zpair[k ^ phase]),
            device_id_type=MESH,
        )

    small = (
        pltpu.make_async_copy(gain_ref, gain_row, own_sem.at[2]),
        pltpu.make_async_copy(scale_ref, scale_row, own_sem.at[3]),
        pltpu.make_async_copy(h_ref, hidden_ref, own_sem.at[4]),
    )
    for copy in small:
        copy.start()
    greet_all()
    for j in (1, 3, 2):
        first_copy(0, j).start()
        first_copy(1, j).start()
    for j in (1, 3, 2):

        @pl.when(is_late(j))
        def _():
            for kind in range(2):
                late_copy(kind, j).start()

    for copy in own_copies():
        copy.start()

    def fetch(d, carry):
        stage_copy(d).start()
        return carry

    lax.fori_loop(0, RANKS, fetch, 0)
    for copy in small:
        copy.wait()
    for part in range(4):
        for j in range(features // LANES):
            at = part * features + j * LANES
            gain_own[part, j : j + 1, :] = gain_row[:, at : at + LANES]
    for j in range(1, 4):
        gain_copy(j).start()
    gains[0] = gain_own[z]
    scale = jnp.broadcast_to(scale_row[...].astype(jnp.float32), (rows, LANES)).T

    def scale_codes(d, carry):
        stage_copy(d).wait()
        staged[d] = (staged[d].astype(jnp.float32) * scale).astype(jnp.bfloat16)
        return carry

    lax.fori_loop(0, RANKS, scale_codes, 0)
    store_ref[pl.ds(pl.multiple_of(dp * rows, rows), rows), :] = staged[dp]

    def turn(k):
        layer = k + jnp.where(k >= z, 1, 0)
        return lax.rem(layer - z + 4, 4)

    def spread_near(k, carry):
        r = turn(k)
        for kind in range(2):
            first_arrival(kind, r).wait_recv()
            for j in (1, 3, 2):
                near_copy(kind, r, j, False).start()
        return carry

    def spread_far(k):
        r = turn(k)
        for kind in range(2):
            for j in (1, 3, 2):
                near_copy(kind, r, j, True).wait_recv()
            for j in (1, 3):
                far_copy(kind, r, j, False).start()

            @pl.when(k == 0)
            def _():
                far_copy(kind, r, 2, False).start()

        for kind in range(2):
            side_copy(kind, r, 0, core).start()

    def settle(r, order):
        for j in order:
            for kind in range(2):
                far_copy(kind, r, j, True).wait_recv()
                side_copy(kind, r, j, core).start()

    lax.fori_loop(0, 3, spread_near, 0)
    spread_far(0)
    for copy in own_copies():
        copy.wait()
    for j in range(1, 4):
        gain_copy(j).wait()

    def send_codes(j, carry):
        code_copy(lax.rem(dp + j, RANKS)).start()
        return carry

    def layer_step(layer, carry):
        r = lax.rem(layer - z + 4, 4)

        @pl.when(layer != z)
        def _():
            settle(r, (1,))

        @pl.when(layer < 2)
        def _():
            spread_far(layer + 1)

        @pl.when(layer != z)
        def _():
            settle(r, (3, 2))
            for kind in range(2):
                for j in range(SIDE):
                    side_copy(kind, r, j, 1 - core).wait_recv()

            @pl.when(layer == 3 - jnp.where(z == 3, 1, 0))
            def _():
                lax.fori_loop(1, RANKS, send_codes, 0)

        gain = gains[r].astype(jnp.float32)
        squares = jnp.zeros((rows, LANES), jnp.float32)
        for j in range(features // LANES):
            columns = slice(j * LANES, (j + 1) * LANES)
            tile = hidden_ref[:, columns].astype(jnp.float32)
            squares += tile * tile
            normed[:, columns] = (tile * gain[j : j + 1, :]).astype(jnp.bfloat16)
        squares = jnp.broadcast_to(jnp.sum(squares, axis=1, keepdims=True), (rows, LANES))
        high = squares.astype(jnp.bfloat16)
        low = (squares - high.astype(jnp.float32)).astype(jnp.bfloat16)
        lane = lax.broadcasted_iota(jnp.int32, (rows, LANES), 1)
        products[:, :head] = jnp.dot(
            normed[...], w_value[r].reshape(features, head), preferred_element_type=jnp.float32
        )
        products[:, head:] = squares
        for k in range(2):
            part = slice(k * half, (k + 1) * half)
            out1[layer, k, :, :head] = products[part, :head].astype(jnp.bfloat16)
            out1[layer, k, :, head:] = jnp.where(
                lane[part] < LANES // 2, high[part].astype(jnp.float32), low[part].astype(jnp.float32)
            ).astype(jnp.bfloat16)
            sum_copy(0, layer, k).start()

        def arrived(buffer, k):
            marks = buffer[layer, k, :, head:].astype(jnp.float32)
            return buffer[layer, k, :, :head].astype(jnp.float32), marks + pltpu.roll(marks, LANES // 2, 1)

        for k in range(2):
            part = slice(k * half, (k + 1) * half)
            sum_copy(0, layer, k).wait_recv()
            more, marks = arrived(in1, k)
            so_far = products[part, :head] + more
            squares = products[part, head:] + marks
            products[part, :head] = so_far
            products[part, head:] = squares
            high = squares.astype(jnp.bfloat16)
            low = (squares - high.astype(jnp.float32)).astype(jnp.bfloat16)
            out2[layer, k, :, :head] = so_far.astype(jnp.bfloat16)
            out2[layer, k, :, head:] = jnp.where(
                lane[part] < LANES // 2, high.astype(jnp.float32), low.astype(jnp.float32)
            ).astype(jnp.bfloat16)
            sum_copy(1, layer, k).start()
        for k in range(2):
            part = slice(k * half, (k + 1) * half)
            sum_copy(1, layer, k).wait_recv()
            more, marks = arrived(in2, k)
            scale = lax.rsqrt((products[part, head:] + marks) * (1.0 / width) + eps)
            for j in range(head // LANES):
                columns = slice(j * LANES, (j + 1) * LANES)
                values[part, columns] = ((products[part, columns] + more[:, columns]) * scale).astype(
                    jnp.bfloat16
                )
        for n in range(features // 512):
            columns = slice(n * 512, (n + 1) * 512)
            branch = jnp.dot(
                values[...],
                w_out[r, :, :, :, :, columns].reshape(head, 512),
                preferred_element_type=jnp.float32,
            )
            hidden_ref[:, columns] = (hidden_ref[:, columns].astype(jnp.float32) + branch).astype(
                jnp.bfloat16
            )
        return carry

    lax.fori_loop(0, 4, layer_step, 0)

    for k in range(2):
        for layer in range(4):
            sum_copy(0, layer, k).wait_send()
            sum_copy(1, layer, k).wait_send()
    for kind in range(2):
        for j in range(1, 4):
            first_copy(kind, j).wait_send()
            for r in range(1, 4):
                near_copy(kind, r, j, False).wait_send()
                if j != 2:
                    far_copy(kind, r, j, False).wait_send()

            @pl.when(is_late(j))
            def _():
                late_copy(kind, j).wait_send()

        far_copy(kind, turn(0), 2, False).wait_send()
    for kind in range(2):
        for r in range(1, 4):
            for j in range(SIDE):
                side_copy(kind, r, j, core).wait_send()

    def codes_in():
        def arrive(j, carry):
            code_arrival(lax.rem(dp + j, RANKS)).wait_recv()
            return carry

        lax.fori_loop(1, RANKS, arrive, 0)

    def codes_out():
        def leave(j, carry):
            code_copy(lax.rem(dp + j, RANKS)).wait_send()
            return carry

        lax.fori_loop(1, RANKS, leave, 0)

    return codes_in, codes_out


def run_wide(
    inv_root,
    share,
    codes_in,
    store_ref,
    perm_ref,
    proj_ref,
    grad_ref,
    loss_ref,
    held,
    squares,
    total,
    y_own,
    y_keep,
    out1,
    in1,
    out2,
    in2,
    rows_g,
    store,
    aim,
    losses,
    ring_send,
    ring_recv,
    side_send,
    side_recv,
    sum1_send,
    sum1_recv,
    sum2_send,
    sum2_recv,
    rows1_send,
    rows1_recv,
    rows2_send,
    rows2_recv,
    loss_send,
    loss_recv,
):
    dp = lax.axis_index("dp")
    z = lax.axis_index("pipe")
    x, y, core = place(dp)
    here = cycle_position(x, y, core)
    after = cycle_device(lax.rem(here + 1, CHIPS), core)
    before = cycle_device(lax.rem(here + CHIPS - 1, CHIPS), core)
    sibling = dp + 1 - 2 * core
    za = z + 1 - 2 * lax.rem(z, 2)
    zb = 3 - z
    steps = CHIPS
    part = held.shape[1] // 4
    block = 4 * part
    half = block // 2
    zpair = (za, zb)
    ring = (after, before)

    sizes = (4, SIDE, 2 * SIDE)
    spots = (z, y, 2 * x + core)

    def peer(group, j):
        spot = lax.rem(spots[group] + j, sizes[group])
        if group == 0:
            return dp, spot
        if group == 1:
            return (x * SIDE + spot) * 2 + core, z
        return ((spot // 2) * SIDE + y) * 2 + lax.rem(spot, 2), z

    mine = pl.multiple_of(core * 2 * part, 2 * part)
    theirs = pl.multiple_of((1 - core) * 2 * part, 2 * part)

    def ring_copy(s, way, sub, later):
        start = mine + way * part + sub * (part // 4)
        rows = pl.ds(pl.multiple_of(start, part // 4), part // 4)
        return pltpu.make_async_remote_copy(
            src_ref=held.at[s, rows],
            dst_ref=held.at[s + later, rows],
            send_sem=ring_send.at[s, way, sub],
            recv_sem=ring_recv.at[s + later, way, sub],
            device_id=(ring[way], z),
            device_id_type=MESH,
        )

    def side_copy(s, start):
        rows = pl.ds(start, 2 * part)
        return pltpu.make_async_remote_copy(
            src_ref=held.at[s, rows],
            dst_ref=held.at[s, rows],
            send_sem=side_send.at[s],
            recv_sem=side_recv.at[s],
            device_id=(sibling, z),
            device_id_type=MESH,
        )

    def sum1_copy(s, k):
        return pltpu.make_async_remote_copy(
            src_ref=out1.at[s, k],
            dst_ref=in1.at[s, k],
            send_sem=sum1_send.at[s, k],
            recv_sem=sum1_recv.at[s, k],
            device_id=(dp, zpair[k]),
            device_id_type=MESH,
        )

    def sum2_copy(s, k):
        return pltpu.make_async_remote_copy(
            src_ref=out2.at[s, k],
            dst_ref=in2.at[s, k],
            send_sem=sum2_send.at[s, k],
            recv_sem=sum2_recv.at[s, k],
            device_id=(dp, zpair[1 - k]),
            device_id_type=MESH,
        )

    def rows1_copy(s, k, quarter):
        return pltpu.make_async_remote_copy(
            src_ref=rows_g.at[s, quarter],
            dst_ref=rows_g.at[s, quarter],
            send_sem=rows1_send.at[s, k],
            recv_sem=rows1_recv.at[s, k],
            device_id=(dp, zpair[k]),
            device_id_type=MESH,
        )

    def rows2_copy(s, k, quarter):
        rows = pl.ds(k * half, half)
        return pltpu.make_async_remote_copy(
            src_ref=rows_g.at[s, quarter, rows],
            dst_ref=rows_g.at[s, quarter, rows],
            send_sem=rows2_send.at[s, k],
            recv_sem=rows2_recv.at[s, k],
            device_id=(dp, zpair[k]),
            device_id_type=MESH,
        )

    def loss_copy(group, j, arrival):
        spot = lax.rem(spots[group] + j, sizes[group]) if arrival else spots[group]
        return pltpu.make_async_remote_copy(
            src_ref=losses.at[group, spot],
            dst_ref=losses.at[group, spot],
            send_sem=loss_send.at[group, j],
            recv_sem=loss_recv.at[group, spot],
            device_id=peer(group, j),
            device_id_type=MESH,
        )

    def loss_out(group):
        losses[group, spots[group]] = squares[...]
        for j in range(1, sizes[group]):
            loss_copy(group, j, False).start()

    def loss_in(group):
        for j in range(1, sizes[group]):
            loss_copy(group, j, True).wait_recv()
        squares[...] = functools.reduce(
            jnp.add, [losses[group, spot] for spot in range(sizes[group])]
        )

    squares[...] = jnp.zeros_like(squares)
    total[...] = jnp.zeros_like(total)

    def pass_on(i, sub):
        @pl.when(jnp.logical_and(i > 0, i < steps))
        def _():
            for way in range(2):
                ring_copy(i, way, sub, 0).wait_recv()

        @pl.when(i < steps - 1)
        def _():
            for way in range(2):
                ring_copy(i, way, sub, 1).start()

    def body(i, carry):
        pass_on(i, 0)

        @pl.when(jnp.logical_and(i >= 1, i < steps + 1))
        def _():
            s = i - 1
            slot = lax.rem(s, 2)
            side_copy(s, theirs).wait_recv()
            for n in range(2):
                part_y = jnp.dot(
                    held[s], proj_ref[:, n * 256 : (n + 1) * 256], preferred_element_type=jnp.float32
                )
                y_own[slot, 2 * n] = part_y[:, :128]
                y_own[slot, 2 * n + 1] = part_y[:, 128:]
            for k in range(2):
                rows = pl.ds(k * half, half)
                other = 3 - zpair[k] if k == 0 else zpair[k] + 1 - 2 * lax.rem(zpair[k], 2)
                out1[s, k, 0] = y_own[slot, zpair[k], rows, :].astype(jnp.bfloat16)
                out1[s, k, 1] = y_own[slot, other, rows, :].astype(jnp.bfloat16)
                sum1_copy(s, k).start()

        pass_on(i, 1)

        @pl.when(i == 4)
        def _():
            codes_in()
            store[...] = store_ref[...].astype(jnp.float32)

        @pl.when(jnp.logical_and(i >= 4, i < steps + 4))
        def _():
            s = i - 4
            slot = lax.rem(s, 2)
            for k in range(2):
                sum2_copy(s, k).wait_recv()
            for chunk in range(4):
                ring_core, way = chunk // 2, chunk % 2
                at = cycle_position(x, y, ring_core)
                origin = cycle_device(lax.rem(at + (CHIPS - s if way == 0 else s), CHIPS), ring_core)
                token = pl.multiple_of((origin * 2 + way) * part, part)
                rows = pl.ds(chunk * part, part)
                inside = pl.ds((chunk % 2) * part, part)

                def seek(group, carry):
                    for j in range(8):
                        at_row = group * 8 + j
                        aim[pl.ds(chunk * part + at_row, 1), :] = store[
                            pl.ds(perm_ref[token + at_row], 1), :
                        ]
                    return carry

                lax.fori_loop(0, part // 8, seek, 0)
                diff = (
                    y_keep[slot, rows, :]
                    + in2[s, chunk // 2, inside, :].astype(jnp.float32)
                    - aim[rows, :]
                )
                rows_g[s, z, rows, :] = (diff * inv_root).astype(jnp.bfloat16)
                squares[...] += jnp.sum((diff * diff).reshape(part // 8, 8, diff.shape[1]), axis=0)
            for k in range(2):
                rows1_copy(s, k, z).start()

        pass_on(i, 2)

        @pl.when(jnp.logical_and(i >= 2, i < steps + 2))
        def _():
            s = i - 2
            slot = lax.rem(s, 2)
            for k in range(2):
                rows = pl.ds(k * half, half)
                sum1_copy(s, k).wait_recv()
                passed = y_own[slot, zpair[1 - k], rows, :] + in1[s, k, 1].astype(jnp.float32)
                out2[s, k] = passed.astype(jnp.bfloat16)
                sum2_copy(s, k).start()
                y_keep[slot, rows, :] = y_own[slot, z, rows, :] + in1[s, k, 0].astype(jnp.float32)

        @pl.when(jnp.logical_and(i >= 5, i < steps + 5))
        def _():
            s = i - 5
            for k in range(2):
                rows1_copy(s, k, zpair[k]).wait_recv()
            for k in range(2):
                rows2_copy(s, k, zpair[1 - k]).start()

        pass_on(i, 3)

        @pl.when(i < steps)
        def _():
            side_copy(i, mine).start()

        @pl.when(i == steps + 3)
        def _():
            loss_out(0)

        @pl.when(i == steps + 4)
        def _():
            loss_in(0)
            loss_out(1)

        @pl.when(i == steps + 5)
        def _():
            loss_in(1)
            loss_out(2)

        @pl.when(i >= 6)
        def _():
            s = i - 6
            for k in range(2):
                rows2_copy(s, k, 3 - zpair[k] if k == 0 else zpair[k] + 1 - 2 * lax.rem(zpair[k], 2)).wait_recv()
            rows = jnp.concatenate([rows_g[s, q] for q in range(4)], axis=1)
            for f in range(8):
                features = slice(f * 256, (f + 1) * 256)
                total[features, :] += lax.dot_general(
                    held[s, :, features], rows, (((0,), (0,)), ((), ())), preferred_element_type=jnp.float32
                )

        return carry

    lax.fori_loop(0, steps + 6, body, 0)

    def finish(s, carry):
        @pl.when(s < steps - 1)
        def _():
            for way in range(2):
                for sub in range(4):
                    ring_copy(s, way, sub, 1).wait_send()

        side_copy(s, mine).wait_send()
        for k in range(2):
            sum1_copy(s, k).wait_send()
            sum2_copy(s, k).wait_send()
            rows1_copy(s, k, z).wait_send()
            rows2_copy(s, k, zpair[1 - k]).wait_send()
        return carry

    lax.fori_loop(0, steps, finish, 0)
    loss_in(2)
    for group in range(3):
        for j in range(1, sizes[group]):
            loss_copy(group, j, False).wait_send()
    grad_ref[...] = total[...].astype(jnp.bfloat16)
    loss_ref[0, 0] = jnp.sum(squares[...]) * share


LAYER_SCRATCH = 33


def kernel(
    eps,
    inv_root,
    share,
    h_ref,
    value_ref,
    out_ref,
    gain_ref,
    proj_ref,
    codes_ref,
    scale_ref,
    perm_ref,
    grad_ref,
    loss_ref,
    held,
    store_ref,
    proj,
    proj_sem,
    *scratch,
):
    core = lax.rem(lax.axis_index("dp"), 2)
    rows = held.shape[1] // 2
    fetch_proj = pltpu.make_async_copy(proj_ref, proj, proj_sem)
    fetch_proj.start()
    codes_in, codes_out = run_layers(
        eps,
        h_ref,
        value_ref,
        out_ref,
        gain_ref,
        codes_ref,
        scale_ref,
        held.at[0, pl.ds(pl.multiple_of(core * rows, rows), rows)],
        store_ref,
        *scratch[:LAYER_SCRATCH],
    )
    fetch_proj.wait()
    run_wide(
        inv_root,
        share,
        codes_in,
        store_ref,
        perm_ref,
        proj,
        grad_ref,
        loss_ref,
        held,
        *scratch[LAYER_SCRATCH:],
    )
    codes_out()


def distill(hidden, value_weight, folded_out, gain, proj, codes, scales, perm):
    rows, features = hidden.shape
    head = value_weight.shape[1]
    columns = proj.shape[1]
    quarter = columns // 4
    tokens = rows * RANKS
    block = 2 * rows
    wide_half = block // 2
    half = rows // 2
    grid = (4, SIDE, SIDE, 2)
    value_weight = value_weight.reshape(*grid, features // RANKS, head)
    folded_out = folded_out.reshape(*grid[1:], head // RANKS, 4 * features)
    bf16, f32 = jnp.bfloat16, jnp.float32
    dma = pltpu.SemaphoreType.DMA
    message = pltpu.VMEM((4, 2, half, head + LANES), bf16)
    lanes = (features // LANES, LANES)
    layer_scratch = [
        pltpu.VMEM((*grid, features // RANKS, head), bf16),
        pltpu.VMEM((*grid, head // RANKS, features), bf16),
        pltpu.VMEM(gain.shape, bf16),
        pltpu.VMEM((4, *lanes), bf16),
        pltpu.VMEM((4, *lanes), bf16),
        pltpu.VMEM(scales.shape, bf16),
        pltpu.VMEM((rows, head + LANES), f32),
        pltpu.VMEM((rows, features), bf16),
        pltpu.VMEM((rows, head), bf16),
        message,
        message,
        message,
        message,
        pltpu.VMEM((RANKS, rows, LANES), bf16),
        dma((5,)),
        *[dma((2, 3))] * 3,
        *[dma((2, 3, SIDE))] * 6,
        dma((3,)),
        dma((3,)),
        *[dma((4, 2))] * 4,
        *[dma((RANKS,))] * 3,
    ]
    wide_scratch = [
        pltpu.VMEM((8, quarter), f32),
        pltpu.VMEM((features, columns), f32),
        pltpu.VMEM((2, 4, block, quarter), f32),
        pltpu.VMEM((2, block, quarter), f32),
        pltpu.VMEM((CHIPS, 2, 2, wide_half, quarter), bf16),
        pltpu.VMEM((CHIPS, 2, 2, wide_half, quarter), bf16),
        pltpu.VMEM((CHIPS, 2, wide_half, quarter), bf16),
        pltpu.VMEM((CHIPS, 2, wide_half, quarter), bf16),
        pltpu.VMEM((CHIPS, 4, block, quarter), bf16),
        pltpu.VMEM((tokens, LANES), f32),
        pltpu.VMEM((block, quarter), f32),
        pltpu.VMEM((3, 2 * SIDE, 8, quarter), f32),
        dma((CHIPS, 2, 4)),
        dma((CHIPS, 2, 4)),
        dma((CHIPS,)),
        dma((CHIPS,)),
        dma((CHIPS, 2)),
        dma((CHIPS, 2)),
        dma((CHIPS, 2)),
        dma((CHIPS, 2)),
        dma((CHIPS, 2)),
        dma((CHIPS, 2)),
        dma((CHIPS, 2)),
        dma((CHIPS, 2)),
        dma((3, 2 * SIDE)),
        dma((3, 2 * SIDE)),
    ]
    vmem = pl.BlockSpec(memory_space=pltpu.VMEM)
    smem = pl.BlockSpec(memory_space=pltpu.SMEM)
    anywhere = pl.BlockSpec(memory_space=pl.ANY)
    return pl.pallas_call(
        functools.partial(kernel, 1e-5, 1.0 / math.sqrt(tokens), 0.5 / (tokens * columns * RANKS)),
        out_shape=(
            jax.ShapeDtypeStruct((features, columns), bf16),
            jax.ShapeDtypeStruct((1, 1), f32),
        ),
        in_specs=[anywhere] * 7 + [smem],
        out_specs=(vmem, smem),
        scratch_shapes=[
            pltpu.VMEM((CHIPS, block, features), bf16),
            pltpu.VMEM((tokens, LANES), bf16),
            pltpu.VMEM(proj.shape, bf16),
            dma,
        ]
        + layer_scratch
        + wide_scratch,
        compiler_params=pltpu.CompilerParams(
            collective_id=0, has_side_effects=True, vmem_limit_bytes=63 * 1024 * 1024
        ),
    )(hidden, value_weight, folded_out, gain, proj, codes, scales, perm)


def shards(
    student_in, value_weight, folded_out, norm_gain, proj, teacher_codes, teacher_scales, perm
):
    grad_proj, loss = distill(
        student_in,
        value_weight[0],
        folded_out[0],
        norm_gain,
        proj,
        teacher_codes,
        teacher_scales[None, :],
        perm,
    )
    return (grad_proj, loss[0, 0])


def solution(mesh):
    return jax.shard_map(
        shards,
        mesh=mesh,
        in_specs=(
            P("dp", "pipe"),
            P("pipe", None, None),
            P("pipe", None, None),
            P("pipe", None),
            P("pipe", "dp"),
            P("dp", None),
            P("dp"),
            P(),
        ),
        out_specs=(P("pipe", "dp"), P()),
        check_vma=False,
    )
```

```python
import functools
import math

import jax
import jax.numpy as jnp
from jax import lax
from jax.experimental import pallas as pl
from jax.experimental.pallas import tpu as pltpu
from jax.sharding import PartitionSpec as P

MESH = pl.DeviceIdType.MESH
SIDE = 4
CHIPS = SIDE * SIDE
RANKS = 2 * CHIPS
LANES = 128


def place(dp):
    core = lax.rem(dp, 2)
    chip = dp // 2
    return chip // SIDE, lax.rem(chip, SIDE), core


def cycle_position(x, y, core):
    return SIDE * (y + core * (x - y)) + lax.rem(x + y, SIDE)


def cycle_device(position, core):
    major = position // SIDE
    minor = lax.rem(lax.rem(position, SIDE) - major + SIDE, SIDE)
    x = minor + core * (major - minor)
    y = major + core * (minor - major)
    return (x * SIDE + y) * 2 + core


def run_layers(
    eps,
    h_ref,
    value_ref,
    out_ref,
    gain_ref,
    codes_ref,
    scale_ref,
    hidden_ref,
    store_ref,
    w_value,
    w_out,
    gain_row,
    gain_own,
    gains,
    scale_row,
    products,
    normed,
    values,
    out1,
    in1,
    out2,
    in2,
    staged,
    own_sem,
    first_send,
    first_recv,
    near_send,
    near_recv,
    far_send,
    far_recv,
    side_send,
    side_recv,
    gain_send,
    gain_recv,
    sum1_send,
    sum1_recv,
    sum2_send,
    sum2_recv,
    stage_sem,
    code_send,
    code_recv,
):
    dp = lax.axis_index("dp")
    z = lax.axis_index("pipe")
    x, y, core = place(dp)
    sibling = dp + 1 - 2 * core
    zpair = (z + 1 - 2 * lax.rem(z, 2), 3 - z)
    rows, features = hidden_ref.shape
    head = value_ref.shape[-1]
    half = rows // 2
    quarter = rows // 4
    weights = (w_value, w_out)
    width = 4 * features

    def greet_all():
        barrier = pltpu.get_barrier_semaphore()

        def greet(j, carry):
            pl.semaphore_signal(
                barrier, inc=1, device_id=(lax.rem(dp + j, RANKS), z), device_id_type=MESH
            )
            return carry

        lax.fori_loop(1, RANKS, greet, 0)
        for j in range(1, 4):
            pl.semaphore_signal(
                barrier, inc=1, device_id=(dp, lax.rem(z + j, 4)), device_id_type=MESH
            )
        pl.semaphore_wait(barrier, RANKS + 2)

    def first_copy(kind, j):
        to = lax.rem(z + j, 4)
        if kind == 0:
            source = value_ref.at[to, x, y, core]
        else:
            source = out_ref.at[x, y, core, :, pl.ds(pl.multiple_of(to * features, features), features)]
        return pltpu.make_async_remote_copy(
            src_ref=source,
            dst_ref=weights[kind].at[4 - j, x, y, core],
            send_sem=first_send.at[kind, j - 1],
            recv_sem=first_recv.at[kind, 3 - j],
            device_id=(dp, to),
            device_id_type=MESH,
        )

    def first_arrival(kind, r):
        block = weights[kind].at[r, x, y, core]
        return pltpu.make_async_remote_copy(
            src_ref=block,
            dst_ref=block,
            send_sem=first_send.at[kind, r - 1],
            recv_sem=first_recv.at[kind, r - 1],
            device_id=(dp, lax.rem(z + r, 4)),
            device_id_type=MESH,
        )

    spot = (x, y)

    def near_copy(kind, r, j, arrival):
        there = lax.rem(spot[kind] + j, SIDE)
        at = there if arrival else spot[kind]
        block = w_value.at[r, at, y, core] if kind == 0 else w_out.at[r, x, at, core]
        chip = there * SIDE + y if kind == 0 else x * SIDE + there
        return pltpu.make_async_remote_copy(
            src_ref=block,
            dst_ref=block,
            send_sem=near_send.at[kind, r - 1, j],
            recv_sem=near_recv.at[kind, r - 1, at],
            device_id=(chip * 2 + core, z),
            device_id_type=MESH,
        )

    def far_copy(kind, r, j, arrival):
        there = lax.rem(spot[1 - kind] + j, SIDE)
        at = there if arrival else spot[1 - kind]
        block = w_value.at[r, :, at, core] if kind == 0 else w_out.at[r, at, :, core]
        chip = there * SIDE + y if kind == 1 else x * SIDE + there
        return pltpu.make_async_remote_copy(
            src_ref=block,
            dst_ref=block,
            send_sem=far_send.at[kind, r - 1, j],
            recv_sem=far_recv.at[kind, r - 1, at],
            device_id=(chip * 2 + core, z),
            device_id_type=MESH,
        )

    def side_copy(kind, r, j, owner):
        at = lax.rem(spot[1 - kind] + j, SIDE)
        block = w_value.at[r, :, at, owner] if kind == 0 else w_out.at[r, at, :, owner]
        return pltpu.make_async_remote_copy(
            src_ref=block,
            dst_ref=block,
            send_sem=side_send.at[kind, r - 1, at],
            recv_sem=side_recv.at[kind, r - 1, at],
            device_id=(sibling, z),
            device_id_type=MESH,
        )

    def gain_copy(j):
        to = lax.rem(z + j, 4)
        return pltpu.make_async_remote_copy(
            src_ref=gain_own.at[to],
            dst_ref=gains.at[4 - j],
            send_sem=gain_send.at[j - 1],
            recv_sem=gain_recv.at[3 - j],
            device_id=(dp, to),
            device_id_type=MESH,
        )

    def own_copies():
        columns = pl.ds(pl.multiple_of(z * features, features), features)
        return (
            pltpu.make_async_copy(value_ref.at[z], w_value.at[0], own_sem.at[0]),
            pltpu.make_async_copy(out_ref.at[:, :, :, :, columns], w_out.at[0], own_sem.at[1]),
        )

    def stage_copy(d):
        columns = pl.ds(pl.multiple_of((d * 4 + z) * LANES, LANES), LANES)
        return pltpu.make_async_copy(codes_ref.at[:, columns], staged.at[d], stage_sem.at[d])

    def code_copy(d):
        return pltpu.make_async_remote_copy(
            src_ref=staged.at[d],
            dst_ref=store_ref.at[pl.ds(pl.multiple_of(dp * rows, rows), rows)],
            send_sem=code_send.at[d],
            recv_sem=code_recv.at[dp],
            device_id=(d, z),
            device_id_type=MESH,
        )

    def code_arrival(d):
        block = store_ref.at[pl.ds(pl.multiple_of(d * rows, rows), rows)]
        return pltpu.make_async_remote_copy(
            src_ref=block,
            dst_ref=block,
            send_sem=code_send.at[d],
            recv_sem=code_recv.at[d],
            device_id=(d, z),
            device_id_type=MESH,
        )

    def sum_copy(phase, layer, k, part):
        source, target, send, recv = (
            (out1, in1, sum1_send, sum1_recv),
            (out2, in2, sum2_send, sum2_recv),
        )[phase]
        return pltpu.make_async_remote_copy(
            src_ref=source.at[layer, k, part],
            dst_ref=target.at[layer, k, part],
            send_sem=send.at[layer, k, part],
            recv_sem=recv.at[layer, k, part],
            device_id=(dp, zpair[k ^ phase]),
            device_id_type=MESH,
        )

    small = (
        pltpu.make_async_copy(gain_ref, gain_row, own_sem.at[2]),
        pltpu.make_async_copy(scale_ref, scale_row, own_sem.at[3]),
        pltpu.make_async_copy(h_ref, hidden_ref, own_sem.at[4]),
    )
    for copy in small:
        copy.start()
    greet_all()
    for j in (1, 3, 2):
        first_copy(0, j).start()
        first_copy(1, j).start()
    for copy in own_copies():
        copy.start()

    def fetch(d, carry):
        stage_copy(d).start()
        return carry

    lax.fori_loop(0, RANKS, fetch, 0)
    for copy in small:
        copy.wait()
    for part in range(4):
        for j in range(features // LANES):
            at = part * features + j * LANES
            gain_own[part, j : j + 1, :] = gain_row[:, at : at + LANES]
    for j in range(1, 4):
        gain_copy(j).start()
    gains[0] = gain_own[z]
    def turn(k):
        layer = k + jnp.where(k >= z, 1, 0)
        return lax.rem(layer - z + 4, 4)

    def spread_near(k, carry):
        r = turn(k)
        for kind in range(2):
            first_arrival(kind, r).wait_recv()
            for j in (1, 3, 2):
                near_copy(kind, r, j, False).start()
        return carry

    def spread_far(k):
        r = turn(k)
        for kind in range(2):
            for j in (1, 3, 2):
                near_copy(kind, r, j, True).wait_recv()
            for j in (1, 3, 2):
                far_copy(kind, r, j, False).start()
        for kind in range(2):
            side_copy(kind, r, 0, core).start()

    def settle(r, order):
        for j in order:
            for kind in range(2):
                far_copy(kind, r, j, True).wait_recv()
                side_copy(kind, r, j, core).start()

    lax.fori_loop(0, 3, spread_near, 0)
    spread_far(0)
    scale = jnp.broadcast_to(scale_row[...].astype(jnp.float32), (rows, LANES)).T

    def scale_codes(d, carry):
        stage_copy(d).wait()
        staged[d] = (staged[d].astype(jnp.float32) * scale).astype(jnp.bfloat16)
        return carry

    lax.fori_loop(0, RANKS, scale_codes, 0)
    store_ref[pl.ds(pl.multiple_of(dp * rows, rows), rows), :] = staged[dp]

    for copy in own_copies():
        copy.wait()
    for j in range(1, 4):
        gain_copy(j).wait()

    def send_codes(j, carry):
        code_copy(lax.rem(dp + j, RANKS)).start()
        return carry

    def layer_step(layer, carry):
        r = lax.rem(layer - z + 4, 4)

        @pl.when(layer != z)
        def _():
            settle(r, (1,))

        @pl.when(layer < 2)
        def _():
            spread_far(layer + 1)

        @pl.when(layer != z)
        def _():
            settle(r, (3, 2))
            for kind in range(2):
                for j in range(SIDE):
                    side_copy(kind, r, j, 1 - core).wait_recv()

        @pl.when(layer == 2)
        def _():
            lax.fori_loop(1, RANKS, send_codes, 0)

        gain = gains[r].astype(jnp.float32)
        squares = jnp.zeros((rows, LANES), jnp.float32)
        for j in range(features // LANES):
            columns = slice(j * LANES, (j + 1) * LANES)
            tile = hidden_ref[:, columns].astype(jnp.float32)
            squares += tile * tile
            normed[:, columns] = (tile * gain[j : j + 1, :]).astype(jnp.bfloat16)
        squares = jnp.broadcast_to(jnp.sum(squares, axis=1, keepdims=True), (rows, LANES))
        products[:, :head] = jnp.dot(
            normed[...], w_value[r].reshape(features, head), preferred_element_type=jnp.float32
        )
        products[:, head:] = squares
        lane = lax.broadcasted_iota(jnp.int32, (quarter, LANES), 1)

        def leave(phase, k, part):
            rows_in = slice(k * half + part * quarter, k * half + (part + 1) * quarter)
            buffer = (out1, out2)[phase]
            squares = products[rows_in, head:]
            high = squares.astype(jnp.bfloat16).astype(jnp.float32)
            buffer[layer, k, part, :, :head] = products[rows_in, :head].astype(jnp.bfloat16)
            buffer[layer, k, part, :, head:] = jnp.where(lane < LANES // 2, high, squares - high).astype(
                jnp.bfloat16
            )
            sum_copy(phase, layer, k, part).start()

        def arrive(phase, k, part):
            rows_in = slice(k * half + part * quarter, k * half + (part + 1) * quarter)
            buffer = (in1, in2)[phase]
            sum_copy(phase, layer, k, part).wait_recv()
            marks = buffer[layer, k, part, :, head:].astype(jnp.float32)
            so_far = products[rows_in, :head] + buffer[layer, k, part, :, :head].astype(jnp.float32)
            return rows_in, so_far, products[rows_in, head:] + marks + pltpu.roll(marks, LANES // 2, 1)

        order = [(k, part) for part in range(2) for k in range(2)]
        for k, part in order:
            leave(0, k, part)
        for k, part in order:
            rows_in, so_far, squares = arrive(0, k, part)
            products[rows_in, :head] = so_far
            products[rows_in, head:] = squares
            leave(1, k, part)
        for k, part in order:
            rows_in, so_far, squares = arrive(1, k, part)
            scale = lax.rsqrt(squares * (1.0 / width) + eps)
            for j in range(head // LANES):
                columns = slice(j * LANES, (j + 1) * LANES)
                values[rows_in, columns] = (so_far[:, columns] * scale).astype(jnp.bfloat16)
        for n in range(features // 512):
            columns = slice(n * 512, (n + 1) * 512)
            branch = jnp.dot(
                values[...],
                w_out[r, :, :, :, :, columns].reshape(head, 512),
                preferred_element_type=jnp.float32,
            )
            hidden_ref[:, columns] = (hidden_ref[:, columns].astype(jnp.float32) + branch).astype(
                jnp.bfloat16
            )
        return carry

    lax.fori_loop(0, 4, layer_step, 0)

    def sends_out():
        for kind in range(2):
            for j in range(1, 4):
                first_copy(kind, j).wait_send()
                for r in range(1, 4):
                    near_copy(kind, r, j, False).wait_send()
                    far_copy(kind, r, j, False).wait_send()
            for r in range(1, 4):
                for j in range(SIDE):
                    side_copy(kind, r, j, core).wait_send()
        for layer in range(4):
            for k in range(2):
                for part in range(2):
                    for phase in range(2):
                        sum_copy(phase, layer, k, part).wait_send()

    def codes_in():
        def arrive(j, carry):
            code_arrival(lax.rem(dp + j, RANKS)).wait_recv()
            return carry

        lax.fori_loop(1, RANKS, arrive, 0)

    def codes_out():
        def leave(j, carry):
            code_copy(lax.rem(dp + j, RANKS)).wait_send()
            return carry

        lax.fori_loop(1, RANKS, leave, 0)

    return codes_in, codes_out, sends_out


def run_wide(
    inv_root,
    share,
    codes_in,
    codes_out,
    sends_out,
    store_ref,
    perm_ref,
    proj_ref,
    total,
    loss_ref,
    held,
    squares,
    y_own,
    y_keep,
    out1,
    in1,
    out2,
    in2,
    rows_g,
    store,
    aim,
    losses,
    ring_send,
    ring_recv,
    side_send,
    side_recv,
    sum1_send,
    sum1_recv,
    sum2_send,
    sum2_recv,
    rows1_send,
    rows1_recv,
    rows2_send,
    rows2_recv,
    loss_send,
    loss_recv,
):
    dp = lax.axis_index("dp")
    z = lax.axis_index("pipe")
    x, y, core = place(dp)
    here = cycle_position(x, y, core)
    after = cycle_device(lax.rem(here + 1, CHIPS), core)
    before = cycle_device(lax.rem(here + CHIPS - 1, CHIPS), core)
    sibling = dp + 1 - 2 * core
    za = z + 1 - 2 * lax.rem(z, 2)
    zb = 3 - z
    steps = CHIPS
    part = held.shape[1] // 4
    block = 4 * part
    half = block // 2
    zpair = (za, zb)
    ring = (after, before)

    sizes = (4, SIDE, 2 * SIDE)
    spots = (z, y, 2 * x + core)

    def peer(group, j):
        spot = lax.rem(spots[group] + j, sizes[group])
        if group == 0:
            return dp, spot
        if group == 1:
            return (x * SIDE + spot) * 2 + core, z
        return ((spot // 2) * SIDE + y) * 2 + lax.rem(spot, 2), z

    mine = pl.multiple_of(core * 2 * part, 2 * part)
    theirs = pl.multiple_of((1 - core) * 2 * part, 2 * part)

    def ring_copy(s, way, sub, later):
        start = mine + way * part + sub * (part // 4)
        rows = pl.ds(pl.multiple_of(start, part // 4), part // 4)
        return pltpu.make_async_remote_copy(
            src_ref=held.at[s, rows],
            dst_ref=held.at[s + later, rows],
            send_sem=ring_send.at[s, way, sub],
            recv_sem=ring_recv.at[s + later, way, sub],
            device_id=(ring[way], z),
            device_id_type=MESH,
        )

    def side_copy(s, start):
        rows = pl.ds(start, 2 * part)
        return pltpu.make_async_remote_copy(
            src_ref=held.at[s, rows],
            dst_ref=held.at[s, rows],
            send_sem=side_send.at[s],
            recv_sem=side_recv.at[s],
            device_id=(sibling, z),
            device_id_type=MESH,
        )

    def sum1_copy(s, k):
        return pltpu.make_async_remote_copy(
            src_ref=out1.at[s, k],
            dst_ref=in1.at[s, k],
            send_sem=sum1_send.at[s, k],
            recv_sem=sum1_recv.at[s, k],
            device_id=(dp, zpair[k]),
            device_id_type=MESH,
        )

    def sum2_copy(s, k):
        return pltpu.make_async_remote_copy(
            src_ref=out2.at[s, k],
            dst_ref=in2.at[s, k],
            send_sem=sum2_send.at[s, k],
            recv_sem=sum2_recv.at[s, k],
            device_id=(dp, zpair[1 - k]),
            device_id_type=MESH,
        )

    def rows1_copy(s, k, quarter):
        return pltpu.make_async_remote_copy(
            src_ref=rows_g.at[s, quarter],
            dst_ref=rows_g.at[s, quarter],
            send_sem=rows1_send.at[s, k],
            recv_sem=rows1_recv.at[s, k],
            device_id=(dp, zpair[k]),
            device_id_type=MESH,
        )

    def rows2_copy(s, k, quarter):
        rows = pl.ds(k * half, half)
        return pltpu.make_async_remote_copy(
            src_ref=rows_g.at[s, quarter, rows],
            dst_ref=rows_g.at[s, quarter, rows],
            send_sem=rows2_send.at[s, k],
            recv_sem=rows2_recv.at[s, k],
            device_id=(dp, zpair[k]),
            device_id_type=MESH,
        )

    def loss_copy(group, j, arrival):
        spot = lax.rem(spots[group] + j, sizes[group]) if arrival else spots[group]
        return pltpu.make_async_remote_copy(
            src_ref=losses.at[group, spot],
            dst_ref=losses.at[group, spot],
            send_sem=loss_send.at[group, j],
            recv_sem=loss_recv.at[group, spot],
            device_id=peer(group, j),
            device_id_type=MESH,
        )

    def loss_out(group):
        losses[group, spots[group]] = squares[...]
        for j in range(1, sizes[group]):
            loss_copy(group, j, False).start()

    def loss_in(group):
        for j in range(1, sizes[group]):
            loss_copy(group, j, True).wait_recv()
        squares[...] = functools.reduce(
            jnp.add, [losses[group, spot] for spot in range(sizes[group])]
        )

    squares[...] = jnp.zeros_like(squares)
    total[...] = jnp.zeros_like(total)

    def pass_on(i, sub):
        @pl.when(jnp.logical_and(i > 0, i < steps))
        def _():
            for way in range(2):
                ring_copy(i, way, sub, 0).wait_recv()

        @pl.when(i < steps - 1)
        def _():
            for way in range(2):
                ring_copy(i, way, sub, 1).start()

    def body(i, carry):
        pass_on(i, 0)

        @pl.when(jnp.logical_and(i >= 1, i < steps + 1))
        def _():
            s = i - 1
            slot = lax.rem(s, 2)
            side_copy(s, theirs).wait_recv()
            for n in range(2):
                part_y = jnp.dot(
                    held[s], proj_ref[:, n * 256 : (n + 1) * 256], preferred_element_type=jnp.float32
                )
                y_own[slot, 2 * n] = part_y[:, :128]
                y_own[slot, 2 * n + 1] = part_y[:, 128:]
            for k in range(2):
                rows = pl.ds(k * half, half)
                other = 3 - zpair[k] if k == 0 else zpair[k] + 1 - 2 * lax.rem(zpair[k], 2)
                out1[s, k, 0] = y_own[slot, zpair[k], rows, :].astype(jnp.bfloat16)
                out1[s, k, 1] = y_own[slot, other, rows, :].astype(jnp.bfloat16)
                sum1_copy(s, k).start()

        pass_on(i, 1)

        @pl.when(i == 4)
        def _():
            codes_in()
            store[...] = store_ref[...].astype(jnp.float32)

        @pl.when(jnp.logical_and(i >= 4, i < steps + 4))
        def _():
            s = i - 4
            slot = lax.rem(s, 2)
            for k in range(2):
                sum2_copy(s, k).wait_recv()
            for chunk in range(4):
                ring_core, way = chunk // 2, chunk % 2
                at = cycle_position(x, y, ring_core)
                origin = cycle_device(lax.rem(at + (CHIPS - s if way == 0 else s), CHIPS), ring_core)
                token = pl.multiple_of((origin * 2 + way) * part, part)
                rows = pl.ds(chunk * part, part)
                inside = pl.ds((chunk % 2) * part, part)

                def seek(group, carry):
                    for j in range(8):
                        at_row = group * 8 + j
                        aim[pl.ds(chunk * part + at_row, 1), :] = store[
                            pl.ds(perm_ref[token + at_row], 1), :
                        ]
                    return carry

                lax.fori_loop(0, part // 8, seek, 0)
                diff = (
                    y_keep[slot, rows, :]
                    + in2[s, chunk // 2, inside, :].astype(jnp.float32)
                    - aim[rows, :]
                )
                rows_g[s, z, rows, :] = (diff * inv_root).astype(jnp.bfloat16)
                squares[...] += jnp.sum((diff * diff).reshape(part // 8, 8, diff.shape[1]), axis=0)
            for k in range(2):
                rows1_copy(s, k, z).start()

        pass_on(i, 2)

        @pl.when(jnp.logical_and(i >= 2, i < steps + 2))
        def _():
            s = i - 2
            slot = lax.rem(s, 2)
            for k in range(2):
                rows = pl.ds(k * half, half)
                sum1_copy(s, k).wait_recv()
                passed = y_own[slot, zpair[1 - k], rows, :] + in1[s, k, 1].astype(jnp.float32)
                out2[s, k] = passed.astype(jnp.bfloat16)
                sum2_copy(s, k).start()
                y_keep[slot, rows, :] = y_own[slot, z, rows, :] + in1[s, k, 0].astype(jnp.float32)

        @pl.when(jnp.logical_and(i >= 5, i < steps + 5))
        def _():
            s = i - 5
            for k in range(2):
                rows1_copy(s, k, zpair[k]).wait_recv()
            for k in range(2):
                rows2_copy(s, k, zpair[1 - k]).start()

        pass_on(i, 3)

        @pl.when(i < steps)
        def _():
            side_copy(i, mine).start()

        @pl.when(i == steps + 3)
        def _():
            loss_out(0)

        @pl.when(i == steps + 4)
        def _():
            loss_in(0)
            loss_out(1)

        @pl.when(i == steps + 5)
        def _():
            loss_in(1)
            loss_out(2)

        @pl.when(i >= 6)
        def _():
            s = i - 6
            for k in range(2):
                rows2_copy(s, k, 3 - zpair[k] if k == 0 else zpair[k] + 1 - 2 * lax.rem(zpair[k], 2)).wait_recv()
            rows = jnp.concatenate([rows_g[s, q] for q in range(4)], axis=1)
            for f in range(8):
                features = slice(f * 256, (f + 1) * 256)
                total[features, :] += lax.dot_general(
                    held[s, :, features], rows, (((0,), (0,)), ((), ())), preferred_element_type=jnp.float32
                )

            @pl.when(s < steps - 1)
            def _():
                for way in range(2):
                    for sub in range(4):
                        ring_copy(s, way, sub, 1).wait_send()

            side_copy(s, mine).wait_send()
            for k in range(2):
                sum1_copy(s, k).wait_send()
                sum2_copy(s, k).wait_send()
                rows1_copy(s, k, z).wait_send()
                rows2_copy(s, k, zpair[1 - k]).wait_send()

        @pl.when(i == 8)
        def _():
            sends_out()

        @pl.when(i == 10)
        def _():
            codes_out()

        return carry

    lax.fori_loop(0, steps + 6, body, 0)

    loss_in(2)
    for group in range(3):
        for j in range(1, sizes[group]):
            loss_copy(group, j, False).wait_send()
    loss_ref[0, 0] = jnp.sum(squares[...]) * share


LAYER_SCRATCH = 32


def kernel(
    eps,
    inv_root,
    share,
    h_ref,
    value_ref,
    out_ref,
    gain_ref,
    proj_ref,
    codes_ref,
    scale_ref,
    perm_ref,
    grad_ref,
    loss_ref,
    held,
    store_ref,
    proj,
    proj_sem,
    *scratch,
):
    core = lax.rem(lax.axis_index("dp"), 2)
    rows = held.shape[1] // 2
    fetch_proj = pltpu.make_async_copy(proj_ref, proj, proj_sem)
    fetch_proj.start()
    codes_in, codes_out, sends_out = run_layers(
        eps,
        h_ref,
        value_ref,
        out_ref,
        gain_ref,
        codes_ref,
        scale_ref,
        held.at[0, pl.ds(pl.multiple_of(core * rows, rows), rows)],
        store_ref,
        *scratch[:LAYER_SCRATCH],
    )
    fetch_proj.wait()
    run_wide(
        inv_root,
        share,
        codes_in,
        codes_out,
        sends_out,
        store_ref,
        perm_ref,
        proj,
        grad_ref,
        loss_ref,
        held,
        *scratch[LAYER_SCRATCH:],
    )


def distill(hidden, value_weight, folded_out, gain, proj, codes, scales, perm):
    rows, features = hidden.shape
    head = value_weight.shape[1]
    columns = proj.shape[1]
    quarter = columns // 4
    tokens = rows * RANKS
    block = 2 * rows
    wide_half = block // 2
    grid = (4, SIDE, SIDE, 2)
    value_weight = value_weight.reshape(*grid, features // RANKS, head)
    folded_out = folded_out.reshape(*grid[1:], head // RANKS, 4 * features)
    bf16, f32 = jnp.bfloat16, jnp.float32
    dma = pltpu.SemaphoreType.DMA
    message = pltpu.VMEM((4, 2, 2, rows // 4, head + LANES), bf16)
    lanes = (features // LANES, LANES)
    layer_scratch = [
        pltpu.VMEM((*grid, features // RANKS, head), bf16),
        pltpu.VMEM((*grid, head // RANKS, features), bf16),
        pltpu.VMEM(gain.shape, bf16),
        pltpu.VMEM((4, *lanes), bf16),
        pltpu.VMEM((4, *lanes), bf16),
        pltpu.VMEM(scales.shape, bf16),
        pltpu.VMEM((rows, head + LANES), f32),
        pltpu.VMEM((rows, features), bf16),
        pltpu.VMEM((rows, head), bf16),
        message,
        message,
        message,
        message,
        pltpu.VMEM((RANKS, rows, LANES), bf16),
        dma((5,)),
        *[dma((2, 3))] * 2,
        *[dma((2, 3, SIDE))] * 6,
        dma((3,)),
        dma((3,)),
        *[dma((4, 2, 2))] * 4,
        *[dma((RANKS,))] * 3,
    ]
    wide_scratch = [
        pltpu.VMEM((8, quarter), f32),
        pltpu.VMEM((2, 4, block, quarter), f32),
        pltpu.VMEM((2, block, quarter), f32),
        pltpu.VMEM((CHIPS, 2, 2, wide_half, quarter), bf16),
        pltpu.VMEM((CHIPS, 2, 2, wide_half, quarter), bf16),
        pltpu.VMEM((CHIPS, 2, wide_half, quarter), bf16),
        pltpu.VMEM((CHIPS, 2, wide_half, quarter), bf16),
        pltpu.VMEM((CHIPS, 4, block, quarter), bf16),
        pltpu.VMEM((tokens, LANES), f32),
        pltpu.VMEM((block, quarter), f32),
        pltpu.VMEM((3, 2 * SIDE, 8, quarter), f32),
        dma((CHIPS, 2, 4)),
        dma((CHIPS, 2, 4)),
        dma((CHIPS,)),
        dma((CHIPS,)),
        dma((CHIPS, 2)),
        dma((CHIPS, 2)),
        dma((CHIPS, 2)),
        dma((CHIPS, 2)),
        dma((CHIPS, 2)),
        dma((CHIPS, 2)),
        dma((CHIPS, 2)),
        dma((CHIPS, 2)),
        dma((3, 2 * SIDE)),
        dma((3, 2 * SIDE)),
    ]
    vmem = pl.BlockSpec(memory_space=pltpu.VMEM)
    smem = pl.BlockSpec(memory_space=pltpu.SMEM)
    anywhere = pl.BlockSpec(memory_space=pl.ANY)
    return pl.pallas_call(
        functools.partial(kernel, 1e-5, 1.0 / math.sqrt(tokens), 0.5 / (tokens * columns * RANKS)),
        out_shape=(
            jax.ShapeDtypeStruct((features, columns), f32),
            jax.ShapeDtypeStruct((1, 1), f32),
        ),
        in_specs=[anywhere] * 7 + [smem],
        out_specs=(vmem, smem),
        scratch_shapes=[
            pltpu.VMEM((CHIPS, block, features), bf16),
            pltpu.VMEM((tokens, LANES), bf16),
            pltpu.VMEM(proj.shape, bf16),
            dma,
        ]
        + layer_scratch
        + wide_scratch,
        compiler_params=pltpu.CompilerParams(
            collective_id=0, has_side_effects=True, vmem_limit_bytes=63 * 1024 * 1024
        ),
    )(hidden, value_weight, folded_out, gain, proj, codes, scales, perm)


def shards(
    student_in, value_weight, folded_out, norm_gain, proj, teacher_codes, teacher_scales, perm
):
    grad_proj, loss = distill(
        student_in,
        value_weight[0],
        folded_out[0],
        norm_gain,
        proj,
        teacher_codes,
        teacher_scales[None, :],
        perm,
    )
    return (grad_proj.astype(jnp.bfloat16), loss[0, 0])


def solution(mesh):
    return jax.shard_map(
        shards,
        mesh=mesh,
        in_specs=(
            P("dp", "pipe"),
            P("pipe", None, None),
            P("pipe", None, None),
            P("pipe", None),
            P("pipe", "dp"),
            P("dp", None),
            P("dp"),
            P(),
        ),
        out_specs=(P("pipe", "dp"), P()),
        check_vma=False,
    )
```

```python
import functools
import math

import jax
import jax.numpy as jnp
from jax import lax
from jax.experimental import pallas as pl
from jax.experimental.pallas import tpu as pltpu
from jax.sharding import PartitionSpec as P

MESH = pl.DeviceIdType.MESH
SIDE = 4
CHIPS = SIDE * SIDE
RANKS = 2 * CHIPS
LANES = 128


def place(dp):
    core = lax.rem(dp, 2)
    chip = dp // 2
    return chip // SIDE, lax.rem(chip, SIDE), core


def cycle_position(x, y, core):
    return SIDE * (y + core * (x - y)) + lax.rem(x + y, SIDE)


def cycle_device(position, core):
    major = position // SIDE
    minor = lax.rem(lax.rem(position, SIDE) - major + SIDE, SIDE)
    x = minor + core * (major - minor)
    y = major + core * (minor - major)
    return (x * SIDE + y) * 2 + core


def run_layers(
    eps,
    h_ref,
    value_ref,
    out_ref,
    gain_ref,
    codes_ref,
    scale_ref,
    hidden_ref,
    store_ref,
    w_value,
    w_out,
    gain_row,
    gain_own,
    gains,
    scale_row,
    products,
    normed,
    values,
    out1,
    in1,
    out2,
    in2,
    staged,
    own_sem,
    first_send,
    first_recv,
    near_send,
    near_recv,
    far_send,
    far_recv,
    relay_send,
    relay_recv,
    side_send,
    side_recv,
    gain_send,
    gain_recv,
    sum1_send,
    sum1_recv,
    sum2_send,
    sum2_recv,
    stage_sem,
    code_send,
    code_recv,
):
    dp = lax.axis_index("dp")
    z = lax.axis_index("pipe")
    x, y, core = place(dp)
    sibling = dp + 1 - 2 * core
    zpair = (z + 1 - 2 * lax.rem(z, 2), 3 - z)
    rows, features = hidden_ref.shape
    head = value_ref.shape[-1]
    half = rows // 2
    quarter = rows // 4
    weights = (w_value, w_out)
    width = 4 * features

    def greet_all():
        barrier = pltpu.get_barrier_semaphore()

        def greet(j, carry):
            pl.semaphore_signal(
                barrier, inc=1, device_id=(lax.rem(dp + j, RANKS), z), device_id_type=MESH
            )
            return carry

        lax.fori_loop(1, RANKS, greet, 0)
        for j in range(1, 4):
            pl.semaphore_signal(
                barrier, inc=1, device_id=(dp, lax.rem(z + j, 4)), device_id_type=MESH
            )
        pl.semaphore_wait(barrier, RANKS + 2)

    def first_copy(kind, j):
        to = lax.rem(z + j, 4)
        if kind == 0:
            source = value_ref.at[to, x, y, core]
        else:
            source = out_ref.at[x, y, core, :, pl.ds(pl.multiple_of(to * features, features), features)]
        return pltpu.make_async_remote_copy(
            src_ref=source,
            dst_ref=weights[kind].at[4 - j, x, y, core],
            send_sem=first_send.at[kind, j - 1],
            recv_sem=first_recv.at[kind, 3 - j],
            device_id=(dp, to),
            device_id_type=MESH,
        )

    def first_arrival(kind, r):
        block = weights[kind].at[r, x, y, core]
        return pltpu.make_async_remote_copy(
            src_ref=block,
            dst_ref=block,
            send_sem=first_send.at[kind, r - 1],
            recv_sem=first_recv.at[kind, r - 1],
            device_id=(dp, lax.rem(z + r, 4)),
            device_id_type=MESH,
        )

    spot = (x, y)

    def near_copy(kind, r, j, arrival):
        there = lax.rem(spot[kind] + j, SIDE)
        at = there if arrival else spot[kind]
        block = w_value.at[r, at, y, core] if kind == 0 else w_out.at[r, x, at, core]
        chip = there * SIDE + y if kind == 0 else x * SIDE + there
        return pltpu.make_async_remote_copy(
            src_ref=block,
            dst_ref=block,
            send_sem=near_send.at[kind, r - 1, j],
            recv_sem=near_recv.at[kind, r - 1, at],
            device_id=(chip * 2 + core, z),
            device_id_type=MESH,
        )

    def far_copy(kind, r, j, arrival):
        there = lax.rem(spot[1 - kind] + j, SIDE)
        at = there if arrival else spot[1 - kind]
        block = w_value.at[r, :, at, core] if kind == 0 else w_out.at[r, at, :, core]
        chip = there * SIDE + y if kind == 1 else x * SIDE + there
        return pltpu.make_async_remote_copy(
            src_ref=block,
            dst_ref=block,
            send_sem=far_send.at[kind, r - 1, j],
            recv_sem=far_recv.at[kind, r - 1, at],
            device_id=(chip * 2 + core, z),
            device_id_type=MESH,
        )

    def relay_copy(kind, r, part, arrival):
        place_of = spot[1 - kind]
        at = lax.rem(place_of + (2 if arrival else 1 + 2 * part), SIDE)
        there = lax.rem(place_of + 3 - 2 * part, SIDE)
        pieces = pl.ds(2 * part, 2)
        block = w_value.at[r, pieces, at, core] if kind == 0 else w_out.at[r, at, pieces, core]
        chip = there * SIDE + y if kind == 1 else x * SIDE + there
        return pltpu.make_async_remote_copy(
            src_ref=block,
            dst_ref=block,
            send_sem=relay_send.at[kind, r - 1, part],
            recv_sem=relay_recv.at[kind, r - 1, part],
            device_id=(chip * 2 + core, z),
            device_id_type=MESH,
        )

    def side_copy(kind, r, j, owner):
        at = lax.rem(spot[1 - kind] + j, SIDE)
        block = w_value.at[r, :, at, owner] if kind == 0 else w_out.at[r, at, :, owner]
        return pltpu.make_async_remote_copy(
            src_ref=block,
            dst_ref=block,
            send_sem=side_send.at[kind, r - 1, at],
            recv_sem=side_recv.at[kind, r - 1, at],
            device_id=(sibling, z),
            device_id_type=MESH,
        )

    def gain_copy(j):
        to = lax.rem(z + j, 4)
        return pltpu.make_async_remote_copy(
            src_ref=gain_own.at[to],
            dst_ref=gains.at[4 - j],
            send_sem=gain_send.at[j - 1],
            recv_sem=gain_recv.at[3 - j],
            device_id=(dp, to),
            device_id_type=MESH,
        )

    def own_copies():
        columns = pl.ds(pl.multiple_of(z * features, features), features)
        return (
            pltpu.make_async_copy(value_ref.at[z], w_value.at[0], own_sem.at[0]),
            pltpu.make_async_copy(out_ref.at[:, :, :, :, columns], w_out.at[0], own_sem.at[1]),
        )

    def stage_copy(d):
        columns = pl.ds(pl.multiple_of((d * 4 + z) * LANES, LANES), LANES)
        return pltpu.make_async_copy(codes_ref.at[:, columns], staged.at[d], stage_sem.at[d])

    def code_copy(d):
        return pltpu.make_async_remote_copy(
            src_ref=staged.at[d],
            dst_ref=store_ref.at[pl.ds(pl.multiple_of(dp * rows, rows), rows)],
            send_sem=code_send.at[d],
            recv_sem=code_recv.at[dp],
            device_id=(d, z),
            device_id_type=MESH,
        )

    def code_arrival(d):
        block = store_ref.at[pl.ds(pl.multiple_of(d * rows, rows), rows)]
        return pltpu.make_async_remote_copy(
            src_ref=block,
            dst_ref=block,
            send_sem=code_send.at[d],
            recv_sem=code_recv.at[d],
            device_id=(d, z),
            device_id_type=MESH,
        )

    def sum_copy(phase, layer, k, part):
        source, target, send, recv = (
            (out1, in1, sum1_send, sum1_recv),
            (out2, in2, sum2_send, sum2_recv),
        )[phase]
        return pltpu.make_async_remote_copy(
            src_ref=source.at[layer, k, part],
            dst_ref=target.at[layer, k, part],
            send_sem=send.at[layer, k, part],
            recv_sem=recv.at[layer, k, part],
            device_id=(dp, zpair[k ^ phase]),
            device_id_type=MESH,
        )

    small = (
        pltpu.make_async_copy(gain_ref, gain_row, own_sem.at[2]),
        pltpu.make_async_copy(scale_ref, scale_row, own_sem.at[3]),
        pltpu.make_async_copy(h_ref, hidden_ref, own_sem.at[4]),
    )
    for copy in small:
        copy.start()
    greet_all()
    for j in (1, 3, 2):
        first_copy(0, j).start()
        first_copy(1, j).start()
    for copy in own_copies():
        copy.start()

    def fetch(d, carry):
        stage_copy(d).start()
        return carry

    lax.fori_loop(0, RANKS, fetch, 0)
    for copy in small:
        copy.wait()
    for part in range(4):
        for j in range(features // LANES):
            at = part * features + j * LANES
            gain_own[part, j : j + 1, :] = gain_row[:, at : at + LANES]
    for j in range(1, 4):
        gain_copy(j).start()
    gains[0] = gain_own[z]
    def turn(k):
        layer = k + jnp.where(k >= z, 1, 0)
        return lax.rem(layer - z + 4, 4)

    def spread_near(k, carry):
        r = turn(k)
        for kind in range(2):
            first_arrival(kind, r).wait_recv()
            for j in (1, 3, 2):
                near_copy(kind, r, j, False).start()
        return carry

    def spread_far(k):
        r = turn(k)
        for kind in range(2):
            for j in (1, 3, 2):
                near_copy(kind, r, j, True).wait_recv()
            for j in (1, 3):
                far_copy(kind, r, j, False).start()
        for kind in range(2):
            side_copy(kind, r, 0, core).start()

    def settle(k):
        r = turn(k)
        for part in range(2):
            for kind in range(2):
                far_copy(kind, r, 1 + 2 * part, True).wait_recv()
                relay_copy(kind, r, part, False).start()

        @pl.when(k < 2)
        def _():
            spread_far(k + 1)

        for j in (1, 3):
            for kind in range(2):
                side_copy(kind, r, j, core).start()
        for kind in range(2):
            for part in range(2):
                relay_copy(kind, r, part, True).wait_recv()
            side_copy(kind, r, 2, core).start()
        for kind in range(2):
            for j in range(SIDE):
                side_copy(kind, r, j, 1 - core).wait_recv()

    lax.fori_loop(0, 3, spread_near, 0)
    spread_far(0)
    scale = jnp.broadcast_to(scale_row[...].astype(jnp.float32), (rows, LANES)).T

    def scale_codes(d, carry):
        stage_copy(d).wait()
        staged[d] = (staged[d].astype(jnp.float32) * scale).astype(jnp.bfloat16)
        return carry

    lax.fori_loop(0, RANKS, scale_codes, 0)
    store_ref[pl.ds(pl.multiple_of(dp * rows, rows), rows), :] = staged[dp]

    for copy in own_copies():
        copy.wait()
    for j in range(1, 4):
        gain_copy(j).wait()

    def send_codes(j, carry):
        code_copy(lax.rem(dp + j, RANKS)).start()
        return carry

    def layer_step(layer, carry):
        r = lax.rem(layer - z + 4, 4)

        @pl.when(layer < z)
        def _():
            settle(layer)

        gain = gains[r].astype(jnp.float32)
        squares = jnp.zeros((rows, LANES), jnp.float32)
        for j in range(features // LANES):
            columns = slice(j * LANES, (j + 1) * LANES)
            tile = hidden_ref[:, columns].astype(jnp.float32)
            squares += tile * tile
            normed[:, columns] = (tile * gain[j : j + 1, :]).astype(jnp.bfloat16)
        squares = jnp.broadcast_to(jnp.sum(squares, axis=1, keepdims=True), (rows, LANES))
        products[:, :head] = jnp.dot(
            normed[...], w_value[r].reshape(features, head), preferred_element_type=jnp.float32
        )
        products[:, head:] = squares
        lane = lax.broadcasted_iota(jnp.int32, (quarter, LANES), 1)

        def leave(phase, k, part):
            rows_in = slice(k * half + part * quarter, k * half + (part + 1) * quarter)
            buffer = (out1, out2)[phase]
            squares = products[rows_in, head:]
            high = squares.astype(jnp.bfloat16).astype(jnp.float32)
            buffer[layer, k, part, :, :head] = products[rows_in, :head].astype(jnp.bfloat16)
            buffer[layer, k, part, :, head:] = jnp.where(lane < LANES // 2, high, squares - high).astype(
                jnp.bfloat16
            )
            sum_copy(phase, layer, k, part).start()

        def arrive(phase, k, part):
            rows_in = slice(k * half + part * quarter, k * half + (part + 1) * quarter)
            buffer = (in1, in2)[phase]
            sum_copy(phase, layer, k, part).wait_recv()
            marks = buffer[layer, k, part, :, head:].astype(jnp.float32)
            so_far = products[rows_in, :head] + buffer[layer, k, part, :, :head].astype(jnp.float32)
            return rows_in, so_far, products[rows_in, head:] + marks + pltpu.roll(marks, LANES // 2, 1)

        order = [(k, part) for part in range(2) for k in range(2)]
        for k, part in order:
            leave(0, k, part)

        @pl.when(jnp.logical_and(layer >= z, layer < 3))
        def _():
            settle(layer)

        @pl.when(layer == 2)
        def _():
            lax.fori_loop(1, RANKS, send_codes, 0)

        for k, part in order:
            rows_in, so_far, squares = arrive(0, k, part)
            products[rows_in, :head] = so_far
            products[rows_in, head:] = squares
            leave(1, k, part)
        for k, part in order:
            rows_in, so_far, squares = arrive(1, k, part)
            scale = lax.rsqrt(squares * (1.0 / width) + eps)
            for j in range(head // LANES):
                columns = slice(j * LANES, (j + 1) * LANES)
                values[rows_in, columns] = (so_far[:, columns] * scale).astype(jnp.bfloat16)
        for n in range(features // 512):
            columns = slice(n * 512, (n + 1) * 512)
            branch = jnp.dot(
                values[...],
                w_out[r, :, :, :, :, columns].reshape(head, 512),
                preferred_element_type=jnp.float32,
            )
            hidden_ref[:, columns] = (hidden_ref[:, columns].astype(jnp.float32) + branch).astype(
                jnp.bfloat16
            )
        return carry

    lax.fori_loop(0, 4, layer_step, 0)

    def sends_out():
        for kind in range(2):
            for j in range(1, 4):
                first_copy(kind, j).wait_send()
                for r in range(1, 4):
                    near_copy(kind, r, j, False).wait_send()
                    if j != 2:
                        far_copy(kind, r, j, False).wait_send()
            for r in range(1, 4):
                for part in range(2):
                    relay_copy(kind, r, part, False).wait_send()
                for j in range(SIDE):
                    side_copy(kind, r, j, core).wait_send()
        for layer in range(4):
            for k in range(2):
                for part in range(2):
                    for phase in range(2):
                        sum_copy(phase, layer, k, part).wait_send()

    def codes_in():
        def arrive(j, carry):
            code_arrival(lax.rem(dp + j, RANKS)).wait_recv()
            return carry

        lax.fori_loop(1, RANKS, arrive, 0)

    def codes_out():
        def leave(j, carry):
            code_copy(lax.rem(dp + j, RANKS)).wait_send()
            return carry

        lax.fori_loop(1, RANKS, leave, 0)

    return codes_in, codes_out, sends_out


def run_wide(
    inv_root,
    share,
    codes_in,
    codes_out,
    sends_out,
    store_ref,
    perm_ref,
    proj_ref,
    total,
    loss_ref,
    held,
    squares,
    y_own,
    y_keep,
    out1,
    in1,
    out2,
    in2,
    rows_g,
    store,
    aim,
    losses,
    ring_send,
    ring_recv,
    side_send,
    side_recv,
    sum1_send,
    sum1_recv,
    sum2_send,
    sum2_recv,
    rows1_send,
    rows1_recv,
    rows2_send,
    rows2_recv,
    loss_send,
    loss_recv,
):
    dp = lax.axis_index("dp")
    z = lax.axis_index("pipe")
    x, y, core = place(dp)
    here = cycle_position(x, y, core)
    after = cycle_device(lax.rem(here + 1, CHIPS), core)
    before = cycle_device(lax.rem(here + CHIPS - 1, CHIPS), core)
    sibling = dp + 1 - 2 * core
    za = z + 1 - 2 * lax.rem(z, 2)
    zb = 3 - z
    steps = CHIPS
    part = held.shape[1] // 4
    block = 4 * part
    half = block // 2
    zpair = (za, zb)
    ring = (after, before)

    sizes = (4, SIDE, 2 * SIDE)
    spots = (z, y, 2 * x + core)

    def peer(group, j):
        spot = lax.rem(spots[group] + j, sizes[group])
        if group == 0:
            return dp, spot
        if group == 1:
            return (x * SIDE + spot) * 2 + core, z
        return ((spot // 2) * SIDE + y) * 2 + lax.rem(spot, 2), z

    mine = pl.multiple_of(core * 2 * part, 2 * part)
    theirs = pl.multiple_of((1 - core) * 2 * part, 2 * part)

    def ring_copy(s, way, sub, later):
        start = mine + way * part + sub * (part // 4)
        rows = pl.ds(pl.multiple_of(start, part // 4), part // 4)
        return pltpu.make_async_remote_copy(
            src_ref=held.at[s, rows],
            dst_ref=held.at[s + later, rows],
            send_sem=ring_send.at[s, way, sub],
            recv_sem=ring_recv.at[s + later, way, sub],
            device_id=(ring[way], z),
            device_id_type=MESH,
        )

    def side_copy(s, start):
        rows = pl.ds(start, 2 * part)
        return pltpu.make_async_remote_copy(
            src_ref=held.at[s, rows],
            dst_ref=held.at[s, rows],
            send_sem=side_send.at[s],
            recv_sem=side_recv.at[s],
            device_id=(sibling, z),
            device_id_type=MESH,
        )

    def sum1_copy(s, k):
        return pltpu.make_async_remote_copy(
            src_ref=out1.at[s, k],
            dst_ref=in1.at[s, k],
            send_sem=sum1_send.at[s, k],
            recv_sem=sum1_recv.at[s, k],
            device_id=(dp, zpair[k]),
            device_id_type=MESH,
        )

    def sum2_copy(s, k):
        return pltpu.make_async_remote_copy(
            src_ref=out2.at[s, k],
            dst_ref=in2.at[s, k],
            send_sem=sum2_send.at[s, k],
            recv_sem=sum2_recv.at[s, k],
            device_id=(dp, zpair[1 - k]),
            device_id_type=MESH,
        )

    def rows1_copy(s, k, quarter):
        return pltpu.make_async_remote_copy(
            src_ref=rows_g.at[s, quarter],
            dst_ref=rows_g.at[s, quarter],
            send_sem=rows1_send.at[s, k],
            recv_sem=rows1_recv.at[s, k],
            device_id=(dp, zpair[k]),
            device_id_type=MESH,
        )

    def rows2_copy(s, k, quarter):
        rows = pl.ds(k * half, half)
        return pltpu.make_async_remote_copy(
            src_ref=rows_g.at[s, quarter, rows],
            dst_ref=rows_g.at[s, quarter, rows],
            send_sem=rows2_send.at[s, k],
            recv_sem=rows2_recv.at[s, k],
            device_id=(dp, zpair[k]),
            device_id_type=MESH,
        )

    def loss_copy(group, j, arrival):
        spot = lax.rem(spots[group] + j, sizes[group]) if arrival else spots[group]
        return pltpu.make_async_remote_copy(
            src_ref=losses.at[group, spot],
            dst_ref=losses.at[group, spot],
            send_sem=loss_send.at[group, j],
            recv_sem=loss_recv.at[group, spot],
            device_id=peer(group, j),
            device_id_type=MESH,
        )

    def loss_out(group):
        losses[group, spots[group]] = squares[...]
        for j in range(1, sizes[group]):
            loss_copy(group, j, False).start()

    def loss_in(group):
        for j in range(1, sizes[group]):
            loss_copy(group, j, True).wait_recv()
        squares[...] = functools.reduce(
            jnp.add, [losses[group, spot] for spot in range(sizes[group])]
        )

    squares[...] = jnp.zeros_like(squares)
    total[...] = jnp.zeros_like(total)

    def pass_on(i, sub):
        @pl.when(jnp.logical_and(i > 0, i < steps))
        def _():
            for way in range(2):
                ring_copy(i, way, sub, 0).wait_recv()

        @pl.when(i < steps - 1)
        def _():
            for way in range(2):
                ring_copy(i, way, sub, 1).start()

    def body(i, carry):
        pass_on(i, 0)

        @pl.when(jnp.logical_and(i >= 1, i < steps + 1))
        def _():
            s = i - 1
            slot = lax.rem(s, 2)
            side_copy(s, theirs).wait_recv()
            for n in range(2):
                part_y = jnp.dot(
                    held[s], proj_ref[:, n * 256 : (n + 1) * 256], preferred_element_type=jnp.float32
                )
                y_own[slot, 2 * n] = part_y[:, :128]
                y_own[slot, 2 * n + 1] = part_y[:, 128:]
            for k in range(2):
                rows = pl.ds(k * half, half)
                other = 3 - zpair[k] if k == 0 else zpair[k] + 1 - 2 * lax.rem(zpair[k], 2)
                out1[s, k, 0] = y_own[slot, zpair[k], rows, :].astype(jnp.bfloat16)
                out1[s, k, 1] = y_own[slot, other, rows, :].astype(jnp.bfloat16)
                sum1_copy(s, k).start()

        pass_on(i, 1)

        @pl.when(i == 4)
        def _():
            codes_in()
            store[...] = store_ref[...].astype(jnp.float32)

        @pl.when(jnp.logical_and(i >= 4, i < steps + 4))
        def _():
            s = i - 4
            slot = lax.rem(s, 2)
            for k in range(2):
                sum2_copy(s, k).wait_recv()
            for chunk in range(4):
                ring_core, way = chunk // 2, chunk % 2
                at = cycle_position(x, y, ring_core)
                origin = cycle_device(lax.rem(at + (CHIPS - s if way == 0 else s), CHIPS), ring_core)
                token = pl.multiple_of((origin * 2 + way) * part, part)
                rows = pl.ds(chunk * part, part)
                inside = pl.ds((chunk % 2) * part, part)

                def seek(group, carry):
                    for j in range(8):
                        at_row = group * 8 + j
                        aim[pl.ds(chunk * part + at_row, 1), :] = store[
                            pl.ds(perm_ref[token + at_row], 1), :
                        ]
                    return carry

                lax.fori_loop(0, part // 8, seek, 0)
                diff = (
                    y_keep[slot, rows, :]
                    + in2[s, chunk // 2, inside, :].astype(jnp.float32)
                    - aim[rows, :]
                )
                rows_g[s, z, rows, :] = (diff * inv_root).astype(jnp.bfloat16)
                squares[...] += jnp.sum((diff * diff).reshape(part // 8, 8, diff.shape[1]), axis=0)
            for k in range(2):
                rows1_copy(s, k, z).start()

        pass_on(i, 2)

        @pl.when(jnp.logical_and(i >= 2, i < steps + 2))
        def _():
            s = i - 2
            slot = lax.rem(s, 2)
            for k in range(2):
                rows = pl.ds(k * half, half)
                sum1_copy(s, k).wait_recv()
                passed = y_own[slot, zpair[1 - k], rows, :] + in1[s, k, 1].astype(jnp.float32)
                out2[s, k] = passed.astype(jnp.bfloat16)
                sum2_copy(s, k).start()
                y_keep[slot, rows, :] = y_own[slot, z, rows, :] + in1[s, k, 0].astype(jnp.float32)

        @pl.when(jnp.logical_and(i >= 5, i < steps + 5))
        def _():
            s = i - 5
            for k in range(2):
                rows1_copy(s, k, zpair[k]).wait_recv()
            for k in range(2):
                rows2_copy(s, k, zpair[1 - k]).start()

        pass_on(i, 3)

        @pl.when(i < steps)
        def _():
            side_copy(i, mine).start()

        @pl.when(i == steps + 3)
        def _():
            loss_out(0)

        @pl.when(i == steps + 4)
        def _():
            loss_in(0)
            loss_out(1)

        @pl.when(i == steps + 5)
        def _():
            loss_in(1)
            loss_out(2)

        @pl.when(i >= 6)
        def _():
            s = i - 6
            for k in range(2):
                rows2_copy(s, k, 3 - zpair[k] if k == 0 else zpair[k] + 1 - 2 * lax.rem(zpair[k], 2)).wait_recv()
            rows = jnp.concatenate([rows_g[s, q] for q in range(4)], axis=1)
            for f in range(8):
                features = slice(f * 256, (f + 1) * 256)
                total[features, :] += lax.dot_general(
                    held[s, :, features], rows, (((0,), (0,)), ((), ())), preferred_element_type=jnp.float32
                )

            @pl.when(s < steps - 1)
            def _():
                for way in range(2):
                    for sub in range(4):
                        ring_copy(s, way, sub, 1).wait_send()

            side_copy(s, mine).wait_send()
            for k in range(2):
                sum1_copy(s, k).wait_send()
                sum2_copy(s, k).wait_send()
                rows1_copy(s, k, z).wait_send()
                rows2_copy(s, k, zpair[1 - k]).wait_send()

        @pl.when(i == 8)
        def _():
            sends_out()

        @pl.when(i == 10)
        def _():
            codes_out()

        return carry

    lax.fori_loop(0, steps + 6, body, 0)

    loss_in(2)
    for group in range(3):
        for j in range(1, sizes[group]):
            loss_copy(group, j, False).wait_send()
    loss_ref[0, 0] = jnp.sum(squares[...]) * share


LAYER_SCRATCH = 34


def kernel(
    eps,
    inv_root,
    share,
    h_ref,
    value_ref,
    out_ref,
    gain_ref,
    proj_ref,
    codes_ref,
    scale_ref,
    perm_ref,
    grad_ref,
    loss_ref,
    held,
    store_ref,
    proj,
    proj_sem,
    *scratch,
):
    core = lax.rem(lax.axis_index("dp"), 2)
    rows = held.shape[1] // 2
    fetch_proj = pltpu.make_async_copy(proj_ref, proj, proj_sem)
    fetch_proj.start()
    codes_in, codes_out, sends_out = run_layers(
        eps,
        h_ref,
        value_ref,
        out_ref,
        gain_ref,
        codes_ref,
        scale_ref,
        held.at[0, pl.ds(pl.multiple_of(core * rows, rows), rows)],
        store_ref,
        *scratch[:LAYER_SCRATCH],
    )
    fetch_proj.wait()
    run_wide(
        inv_root,
        share,
        codes_in,
        codes_out,
        sends_out,
        store_ref,
        perm_ref,
        proj,
        grad_ref,
        loss_ref,
        held,
        *scratch[LAYER_SCRATCH:],
    )


def distill(hidden, value_weight, folded_out, gain, proj, codes, scales, perm):
    rows, features = hidden.shape
    head = value_weight.shape[1]
    columns = proj.shape[1]
    quarter = columns // 4
    tokens = rows * RANKS
    block = 2 * rows
    wide_half = block // 2
    grid = (4, SIDE, SIDE, 2)
    value_weight = value_weight.reshape(*grid, features // RANKS, head)
    folded_out = folded_out.reshape(*grid[1:], head // RANKS, 4 * features)
    bf16, f32 = jnp.bfloat16, jnp.float32
    dma = pltpu.SemaphoreType.DMA
    message = pltpu.VMEM((4, 2, 2, rows // 4, head + LANES), bf16)
    lanes = (features // LANES, LANES)
    layer_scratch = [
        pltpu.VMEM((*grid, features // RANKS, head), bf16),
        pltpu.VMEM((*grid, head // RANKS, features), bf16),
        pltpu.VMEM(gain.shape, bf16),
        pltpu.VMEM((4, *lanes), bf16),
        pltpu.VMEM((4, *lanes), bf16),
        pltpu.VMEM(scales.shape, bf16),
        pltpu.VMEM((rows, head + LANES), f32),
        pltpu.VMEM((rows, features), bf16),
        pltpu.VMEM((rows, head), bf16),
        message,
        message,
        message,
        message,
        pltpu.VMEM((RANKS, rows, LANES), bf16),
        dma((5,)),
        *[dma((2, 3))] * 2,
        *[dma((2, 3, SIDE))] * 4,
        *[dma((2, 3, 2))] * 2,
        *[dma((2, 3, SIDE))] * 2,
        dma((3,)),
        dma((3,)),
        *[dma((4, 2, 2))] * 4,
        *[dma((RANKS,))] * 3,
    ]
    wide_scratch = [
        pltpu.VMEM((8, quarter), f32),
        pltpu.VMEM((2, 4, block, quarter), f32),
        pltpu.VMEM((2, block, quarter), f32),
        pltpu.VMEM((CHIPS, 2, 2, wide_half, quarter), bf16),
        pltpu.VMEM((CHIPS, 2, 2, wide_half, quarter), bf16),
        pltpu.VMEM((CHIPS, 2, wide_half, quarter), bf16),
        pltpu.VMEM((CHIPS, 2, wide_half, quarter), bf16),
        pltpu.VMEM((CHIPS, 4, block, quarter), bf16),
        pltpu.VMEM((tokens, LANES), f32),
        pltpu.VMEM((block, quarter), f32),
        pltpu.VMEM((3, 2 * SIDE, 8, quarter), f32),
        dma((CHIPS, 2, 4)),
        dma((CHIPS, 2, 4)),
        dma((CHIPS,)),
        dma((CHIPS,)),
        dma((CHIPS, 2)),
        dma((CHIPS, 2)),
        dma((CHIPS, 2)),
        dma((CHIPS, 2)),
        dma((CHIPS, 2)),
        dma((CHIPS, 2)),
        dma((CHIPS, 2)),
        dma((CHIPS, 2)),
        dma((3, 2 * SIDE)),
        dma((3, 2 * SIDE)),
    ]
    vmem = pl.BlockSpec(memory_space=pltpu.VMEM)
    smem = pl.BlockSpec(memory_space=pltpu.SMEM)
    anywhere = pl.BlockSpec(memory_space=pl.ANY)
    return pl.pallas_call(
        functools.partial(kernel, 1e-5, 1.0 / math.sqrt(tokens), 0.5 / (tokens * columns * RANKS)),
        out_shape=(
            jax.ShapeDtypeStruct((features, columns), f32),
            jax.ShapeDtypeStruct((1, 1), f32),
        ),
        in_specs=[anywhere] * 7 + [smem],
        out_specs=(vmem, smem),
        scratch_shapes=[
            pltpu.VMEM((CHIPS, block, features), bf16),
            pltpu.VMEM((tokens, LANES), bf16),
            pltpu.VMEM(proj.shape, bf16),
            dma,
        ]
        + layer_scratch
        + wide_scratch,
        compiler_params=pltpu.CompilerParams(
            collective_id=0, has_side_effects=True, vmem_limit_bytes=63 * 1024 * 1024
        ),
    )(hidden, value_weight, folded_out, gain, proj, codes, scales, perm)


def shards(
    student_in, value_weight, folded_out, norm_gain, proj, teacher_codes, teacher_scales, perm
):
    grad_proj, loss = distill(
        student_in,
        value_weight[0],
        folded_out[0],
        norm_gain,
        proj,
        teacher_codes,
        teacher_scales[None, :],
        perm,
    )
    return (grad_proj.astype(jnp.bfloat16), loss[0, 0])


def solution(mesh):
    return jax.shard_map(
        shards,
        mesh=mesh,
        in_specs=(
            P("dp", "pipe"),
            P("pipe", None, None),
            P("pipe", None, None),
            P("pipe", None),
            P("pipe", "dp"),
            P("dp", None),
            P("dp"),
            P(),
        ),
        out_specs=(P("pipe", "dp"), P()),
        check_vma=False,
    )
```

```python
import functools
import math

import jax
import jax.numpy as jnp
from jax import lax
from jax.experimental import pallas as pl
from jax.experimental.pallas import tpu as pltpu
from jax.sharding import PartitionSpec as P

MESH = pl.DeviceIdType.MESH
SIDE = 4
CHIPS = SIDE * SIDE
RANKS = 2 * CHIPS
LANES = 128


def place(dp):
    core = lax.rem(dp, 2)
    chip = dp // 2
    return chip // SIDE, lax.rem(chip, SIDE), core


def cycle_position(x, y, core):
    return SIDE * (y + core * (x - y)) + lax.rem(x + y, SIDE)


def cycle_device(position, core):
    major = position // SIDE
    minor = lax.rem(lax.rem(position, SIDE) - major + SIDE, SIDE)
    x = minor + core * (major - minor)
    y = major + core * (minor - major)
    return (x * SIDE + y) * 2 + core


def run_layers(
    eps,
    h_ref,
    value_ref,
    out_ref,
    gain_ref,
    codes_ref,
    scale_ref,
    hidden_ref,
    store_ref,
    w_value,
    w_out,
    gain_row,
    gain_own,
    gains,
    scale_row,
    products,
    normed,
    values,
    out1,
    in1,
    out2,
    in2,
    staged,
    own_sem,
    first_send,
    first_recv,
    late_send,
    near_send,
    near_recv,
    far_send,
    far_recv,
    side_send,
    side_recv,
    gain_send,
    gain_recv,
    sum1_send,
    sum1_recv,
    sum2_send,
    sum2_recv,
    stage_sem,
    code_send,
    code_recv,
):
    dp = lax.axis_index("dp")
    z = lax.axis_index("pipe")
    x, y, core = place(dp)
    sibling = dp + 1 - 2 * core
    zpair = (z + 1 - 2 * lax.rem(z, 2), 3 - z)
    rows, features = hidden_ref.shape
    head = value_ref.shape[-1]
    half = rows // 2
    quarter = rows // 8
    weights = (w_value, w_out)
    width = 4 * features

    def greet_all():
        barrier = pltpu.get_barrier_semaphore()

        def greet(j, carry):
            pl.semaphore_signal(
                barrier, inc=1, device_id=(lax.rem(dp + j, RANKS), z), device_id_type=MESH
            )
            return carry

        lax.fori_loop(1, RANKS, greet, 0)
        for j in range(1, 4):
            pl.semaphore_signal(
                barrier, inc=1, device_id=(dp, lax.rem(z + j, 4)), device_id_type=MESH
            )
        pl.semaphore_wait(barrier, RANKS + 2)

    def first_copy(kind, j):
        to = lax.rem(z + j, 4)
        if kind == 0:
            source = value_ref.at[to, x, y, core]
        else:
            source = out_ref.at[x, y, core, :, pl.ds(pl.multiple_of(to * features, features), features)]
        return pltpu.make_async_remote_copy(
            src_ref=source,
            dst_ref=weights[kind].at[4 - j, x, y, core],
            send_sem=first_send.at[kind, j - 1],
            recv_sem=first_recv.at[kind, 3 - j],
            device_id=(dp, to),
            device_id_type=MESH,
        )

    def first_arrival(kind, r):
        block = weights[kind].at[r, x, y, core]
        return pltpu.make_async_remote_copy(
            src_ref=block,
            dst_ref=block,
            send_sem=first_send.at[kind, r - 1],
            recv_sem=first_recv.at[kind, r - 1],
            device_id=(dp, lax.rem(z + r, 4)),
            device_id_type=MESH,
        )

    spot = (x, y)

    def near_copy(kind, r, j, arrival):
        there = lax.rem(spot[kind] + j, SIDE)
        at = there if arrival else spot[kind]
        block = w_value.at[r, at, y, core] if kind == 0 else w_out.at[r, x, at, core]
        chip = there * SIDE + y if kind == 0 else x * SIDE + there
        return pltpu.make_async_remote_copy(
            src_ref=block,
            dst_ref=block,
            send_sem=near_send.at[kind, r - 1, j],
            recv_sem=near_recv.at[kind, r - 1, at],
            device_id=(chip * 2 + core, z),
            device_id_type=MESH,
        )

    def far_copy(kind, r, j, arrival):
        there = lax.rem(spot[1 - kind] + j, SIDE)
        at = there if arrival else spot[1 - kind]
        block = w_value.at[r, :, at, core] if kind == 0 else w_out.at[r, at, :, core]
        chip = there * SIDE + y if kind == 1 else x * SIDE + there
        return pltpu.make_async_remote_copy(
            src_ref=block,
            dst_ref=block,
            send_sem=far_send.at[kind, r - 1, j],
            recv_sem=far_recv.at[kind, r - 1, at],
            device_id=(chip * 2 + core, z),
            device_id_type=MESH,
        )

    def late_copy(kind, j):
        to = lax.rem(z + j, 4)
        at = lax.rem(spot[1 - kind] + 2, SIDE)
        if kind == 0:
            source = value_ref.at[to, :, at, core]
            target = w_value.at[4 - j, :, at, core]
        else:
            source = out_ref.at[at, :, core, :, pl.ds(pl.multiple_of(to * features, features), features)]
            target = w_out.at[4 - j, at, :, core]
        return pltpu.make_async_remote_copy(
            src_ref=source,
            dst_ref=target,
            send_sem=late_send.at[kind, j - 1],
            recv_sem=far_recv.at[kind, 3 - j, at],
            device_id=(dp, to),
            device_id_type=MESH,
        )

    def gives_late(j):
        return jnp.logical_and(z >= 1, z < lax.rem(z + j, 4))

    def takes_late(k):
        return jnp.logical_and(k >= 1, k < z)

    def side_copy(kind, r, j, owner):
        at = lax.rem(spot[1 - kind] + j, SIDE)
        block = w_value.at[r, :, at, owner] if kind == 0 else w_out.at[r, at, :, owner]
        return pltpu.make_async_remote_copy(
            src_ref=block,
            dst_ref=block,
            send_sem=side_send.at[kind, r - 1, at],
            recv_sem=side_recv.at[kind, r - 1, at],
            device_id=(sibling, z),
            device_id_type=MESH,
        )

    def gain_copy(j):
        to = lax.rem(z + j, 4)
        return pltpu.make_async_remote_copy(
            src_ref=gain_own.at[to],
            dst_ref=gains.at[4 - j],
            send_sem=gain_send.at[j - 1],
            recv_sem=gain_recv.at[3 - j],
            device_id=(dp, to),
            device_id_type=MESH,
        )

    def own_copies():
        columns = pl.ds(pl.multiple_of(z * features, features), features)
        return (
            pltpu.make_async_copy(value_ref.at[z], w_value.at[0], own_sem.at[0]),
            pltpu.make_async_copy(out_ref.at[:, :, :, :, columns], w_out.at[0], own_sem.at[1]),
        )

    def stage_copy(d):
        columns = pl.ds(pl.multiple_of((d * 4 + z) * LANES, LANES), LANES)
        return pltpu.make_async_copy(codes_ref.at[:, columns], staged.at[d], stage_sem.at[d])

    def code_copy(d):
        return pltpu.make_async_remote_copy(
            src_ref=staged.at[d],
            dst_ref=store_ref.at[pl.ds(pl.multiple_of(dp * rows, rows), rows)],
            send_sem=code_send.at[d],
            recv_sem=code_recv.at[dp],
            device_id=(d, z),
            device_id_type=MESH,
        )

    def code_arrival(d):
        block = store_ref.at[pl.ds(pl.multiple_of(d * rows, rows), rows)]
        return pltpu.make_async_remote_copy(
            src_ref=block,
            dst_ref=block,
            send_sem=code_send.at[d],
            recv_sem=code_recv.at[d],
            device_id=(d, z),
            device_id_type=MESH,
        )

    def sum_copy(phase, layer, k, part):
        source, target, send, recv = (
            (out1, in1, sum1_send, sum1_recv),
            (out2, in2, sum2_send, sum2_recv),
        )[phase]
        return pltpu.make_async_remote_copy(
            src_ref=source.at[layer, k, part],
            dst_ref=target.at[layer, k, part],
            send_sem=send.at[layer, k, part],
            recv_sem=recv.at[layer, k, part],
            device_id=(dp, zpair[k ^ phase]),
            device_id_type=MESH,
        )

    small = (
        pltpu.make_async_copy(gain_ref, gain_row, own_sem.at[2]),
        pltpu.make_async_copy(scale_ref, scale_row, own_sem.at[3]),
        pltpu.make_async_copy(h_ref, hidden_ref, own_sem.at[4]),
    )
    for copy in small:
        copy.start()
    greet_all()
    for j in (1, 3, 2):
        first_copy(0, j).start()
        first_copy(1, j).start()
    for j in (1, 2):

        @pl.when(gives_late(j))
        def _():
            for kind in range(2):
                late_copy(kind, j).start()

    for copy in own_copies():
        copy.start()

    def fetch(d, carry):
        stage_copy(d).start()
        return carry

    lax.fori_loop(0, RANKS, fetch, 0)
    for copy in small:
        copy.wait()
    for part in range(4):
        for j in range(features // LANES):
            at = part * features + j * LANES
            gain_own[part, j : j + 1, :] = gain_row[:, at : at + LANES]
    for j in range(1, 4):
        gain_copy(j).start()
    gains[0] = gain_own[z]
    def turn(k):
        layer = k + jnp.where(k >= z, 1, 0)
        return lax.rem(layer - z + 4, 4)

    def spread_near(k, carry):
        r = turn(k)
        for kind in range(2):
            first_arrival(kind, r).wait_recv()
            for j in (1, 3, 2):
                near_copy(kind, r, j, False).start()
        return carry

    def spread_far(k):
        r = turn(k)
        for kind in range(2):
            for j in (1, 3, 2):
                near_copy(kind, r, j, True).wait_recv()
            for j in (1, 3):
                far_copy(kind, r, j, False).start()

            @pl.when(jnp.logical_not(takes_late(k)))
            def _():
                far_copy(kind, r, 2, False).start()

        for kind in range(2):
            side_copy(kind, r, 0, core).start()

    def settle(r, order):
        for j in order:
            for kind in range(2):
                far_copy(kind, r, j, True).wait_recv()
                side_copy(kind, r, j, core).start()

    lax.fori_loop(0, 3, spread_near, 0)
    spread_far(0)
    scale = jnp.broadcast_to(scale_row[...].astype(jnp.float32), (rows, LANES)).T

    def scale_codes(d, carry):
        stage_copy(d).wait()
        staged[d] = (staged[d].astype(jnp.float32) * scale).astype(jnp.bfloat16)
        return carry

    lax.fori_loop(0, RANKS, scale_codes, 0)
    store_ref[pl.ds(pl.multiple_of(dp * rows, rows), rows), :] = staged[dp]

    for copy in own_copies():
        copy.wait()
    for j in range(1, 4):
        gain_copy(j).wait()

    def send_codes(j, carry):
        code_copy(lax.rem(dp + j, RANKS)).start()
        return carry

    def layer_step(layer, carry):
        r = lax.rem(layer - z + 4, 4)

        @pl.when(layer != z)
        def _():
            settle(r, (1,))

        @pl.when(layer < 2)
        def _():
            spread_far(layer + 1)

        @pl.when(layer != z)
        def _():
            settle(r, (3, 2))
            for kind in range(2):
                for j in range(SIDE):
                    side_copy(kind, r, j, 1 - core).wait_recv()

        @pl.when(layer == 2)
        def _():
            lax.fori_loop(1, RANKS, send_codes, 0)

        gain = gains[r].astype(jnp.float32)
        squares = jnp.zeros((rows, LANES), jnp.float32)
        for j in range(features // LANES):
            columns = slice(j * LANES, (j + 1) * LANES)
            tile = hidden_ref[:, columns].astype(jnp.float32)
            squares += tile * tile
            normed[:, columns] = (tile * gain[j : j + 1, :]).astype(jnp.bfloat16)
        squares = jnp.broadcast_to(jnp.sum(squares, axis=1, keepdims=True), (rows, LANES))
        products[:, :head] = jnp.dot(
            normed[...], w_value[r].reshape(features, head), preferred_element_type=jnp.float32
        )
        products[:, head:] = squares
        lane = lax.broadcasted_iota(jnp.int32, (quarter, LANES), 1)

        def leave(phase, k, part):
            rows_in = slice(k * half + part * quarter, k * half + (part + 1) * quarter)
            buffer = (out1, out2)[phase]
            squares = products[rows_in, head:]
            high = squares.astype(jnp.bfloat16).astype(jnp.float32)
            buffer[layer, k, part, :, :head] = products[rows_in, :head].astype(jnp.bfloat16)
            buffer[layer, k, part, :, head:] = jnp.where(lane < LANES // 2, high, squares - high).astype(
                jnp.bfloat16
            )
            sum_copy(phase, layer, k, part).start()

        def arrive(phase, k, part):
            rows_in = slice(k * half + part * quarter, k * half + (part + 1) * quarter)
            buffer = (in1, in2)[phase]
            sum_copy(phase, layer, k, part).wait_recv()
            marks = buffer[layer, k, part, :, head:].astype(jnp.float32)
            so_far = products[rows_in, :head] + buffer[layer, k, part, :, :head].astype(jnp.float32)
            return rows_in, so_far, products[rows_in, head:] + marks + pltpu.roll(marks, LANES // 2, 1)

        order = [(k, part) for part in range(4) for k in range(2)]
        for k, part in order:
            leave(0, k, part)
        for k, part in order:
            rows_in, so_far, squares = arrive(0, k, part)
            products[rows_in, :head] = so_far
            products[rows_in, head:] = squares
            leave(1, k, part)
        for k, part in order:
            rows_in, so_far, squares = arrive(1, k, part)
            scale = lax.rsqrt(squares * (1.0 / width) + eps)
            for j in range(head // LANES):
                columns = slice(j * LANES, (j + 1) * LANES)
                values[rows_in, columns] = (so_far[:, columns] * scale).astype(jnp.bfloat16)
        for n in range(features // 512):
            columns = slice(n * 512, (n + 1) * 512)
            branch = jnp.dot(
                values[...],
                w_out[r, :, :, :, :, columns].reshape(head, 512),
                preferred_element_type=jnp.float32,
            )
            hidden_ref[:, columns] = (hidden_ref[:, columns].astype(jnp.float32) + branch).astype(
                jnp.bfloat16
            )
        return carry

    lax.fori_loop(0, 4, layer_step, 0)

    def sends_out():
        for kind in range(2):
            for j in range(1, 4):
                first_copy(kind, j).wait_send()
                for r in range(1, 4):
                    near_copy(kind, r, j, False).wait_send()
                    if j != 2:
                        far_copy(kind, r, j, False).wait_send()
            for j in (1, 2):

                @pl.when(gives_late(j))
                def _():
                    late_copy(kind, j).wait_send()

            for k in range(3):

                @pl.when(jnp.logical_not(takes_late(k)))
                def _():
                    far_copy(kind, turn(k), 2, False).wait_send()

            for r in range(1, 4):
                for j in range(SIDE):
                    side_copy(kind, r, j, core).wait_send()
        for layer in range(4):
            for k in range(2):
                for part in range(4):
                    for phase in range(2):
                        sum_copy(phase, layer, k, part).wait_send()

    def codes_in():
        def arrive(j, carry):
            code_arrival(lax.rem(dp + j, RANKS)).wait_recv()
            return carry

        lax.fori_loop(1, RANKS, arrive, 0)

    def codes_out():
        def leave(j, carry):
            code_copy(lax.rem(dp + j, RANKS)).wait_send()
            return carry

        lax.fori_loop(1, RANKS, leave, 0)

    return codes_in, codes_out, sends_out


def run_wide(
    inv_root,
    share,
    codes_in,
    codes_out,
    sends_out,
    store_ref,
    perm_ref,
    proj_ref,
    grad_ref,
    loss_ref,
    held,
    squares,
    total,
    rounded,
    rounded_sem,
    y_own,
    y_keep,
    out1,
    in1,
    out2,
    in2,
    rows_g,
    store,
    aim,
    losses,
    ring_send,
    ring_recv,
    side_send,
    side_recv,
    sum1_send,
    sum1_recv,
    sum2_send,
    sum2_recv,
    rows1_send,
    rows1_recv,
    rows2_send,
    rows2_recv,
    loss_send,
    loss_recv,
):
    dp = lax.axis_index("dp")
    z = lax.axis_index("pipe")
    x, y, core = place(dp)
    here = cycle_position(x, y, core)
    after = cycle_device(lax.rem(here + 1, CHIPS), core)
    before = cycle_device(lax.rem(here + CHIPS - 1, CHIPS), core)
    sibling = dp + 1 - 2 * core
    za = z + 1 - 2 * lax.rem(z, 2)
    zb = 3 - z
    steps = CHIPS
    part = held.shape[1] // 4
    block = 4 * part
    half = block // 2
    zpair = (za, zb)
    ring = (after, before)

    sizes = (4, SIDE, 2 * SIDE)
    spots = (z, y, 2 * x + core)

    def peer(group, j):
        spot = lax.rem(spots[group] + j, sizes[group])
        if group == 0:
            return dp, spot
        if group == 1:
            return (x * SIDE + spot) * 2 + core, z
        return ((spot // 2) * SIDE + y) * 2 + lax.rem(spot, 2), z

    mine = pl.multiple_of(core * 2 * part, 2 * part)
    theirs = pl.multiple_of((1 - core) * 2 * part, 2 * part)

    def ring_copy(s, way, sub, later):
        start = mine + way * part + sub * (part // 4)
        rows = pl.ds(pl.multiple_of(start, part // 4), part // 4)
        return pltpu.make_async_remote_copy(
            src_ref=held.at[s, rows],
            dst_ref=held.at[s + later, rows],
            send_sem=ring_send.at[s, way, sub],
            recv_sem=ring_recv.at[s + later, way, sub],
            device_id=(ring[way], z),
            device_id_type=MESH,
        )

    def side_copy(s, start):
        rows = pl.ds(start, 2 * part)
        return pltpu.make_async_remote_copy(
            src_ref=held.at[s, rows],
            dst_ref=held.at[s, rows],
            send_sem=side_send.at[s],
            recv_sem=side_recv.at[s],
            device_id=(sibling, z),
            device_id_type=MESH,
        )

    def sum1_copy(s, k):
        return pltpu.make_async_remote_copy(
            src_ref=out1.at[s, k],
            dst_ref=in1.at[s, k],
            send_sem=sum1_send.at[s, k],
            recv_sem=sum1_recv.at[s, k],
            device_id=(dp, zpair[k]),
            device_id_type=MESH,
        )

    def sum2_copy(s, k):
        return pltpu.make_async_remote_copy(
            src_ref=out2.at[s, k],
            dst_ref=in2.at[s, k],
            send_sem=sum2_send.at[s, k],
            recv_sem=sum2_recv.at[s, k],
            device_id=(dp, zpair[1 - k]),
            device_id_type=MESH,
        )

    def rows1_copy(s, k, quarter):
        return pltpu.make_async_remote_copy(
            src_ref=rows_g.at[s, quarter],
            dst_ref=rows_g.at[s, quarter],
            send_sem=rows1_send.at[s, k],
            recv_sem=rows1_recv.at[s, k],
            device_id=(dp, zpair[k]),
            device_id_type=MESH,
        )

    def rows2_copy(s, k, quarter):
        rows = pl.ds(k * half, half)
        return pltpu.make_async_remote_copy(
            src_ref=rows_g.at[s, quarter, rows],
            dst_ref=rows_g.at[s, quarter, rows],
            send_sem=rows2_send.at[s, k],
            recv_sem=rows2_recv.at[s, k],
            device_id=(dp, zpair[k]),
            device_id_type=MESH,
        )

    def loss_copy(group, j, arrival):
        spot = lax.rem(spots[group] + j, sizes[group]) if arrival else spots[group]
        return pltpu.make_async_remote_copy(
            src_ref=losses.at[group, spot],
            dst_ref=losses.at[group, spot],
            send_sem=loss_send.at[group, j],
            recv_sem=loss_recv.at[group, spot],
            device_id=peer(group, j),
            device_id_type=MESH,
        )

    def loss_out(group):
        losses[group, spots[group]] = squares[...]
        for j in range(1, sizes[group]):
            loss_copy(group, j, False).start()

    def loss_in(group):
        for j in range(1, sizes[group]):
            loss_copy(group, j, True).wait_recv()
        squares[...] = functools.reduce(
            jnp.add, [losses[group, spot] for spot in range(sizes[group])]
        )

    squares[...] = jnp.zeros_like(squares)
    total[...] = jnp.zeros_like(total)

    def pass_on(i, sub):
        @pl.when(jnp.logical_and(i > 0, i < steps))
        def _():
            for way in range(2):
                ring_copy(i, way, sub, 0).wait_recv()

        @pl.when(i < steps - 1)
        def _():
            for way in range(2):
                ring_copy(i, way, sub, 1).start()

    def body(i, carry):
        pass_on(i, 0)

        @pl.when(jnp.logical_and(i >= 1, i < steps + 1))
        def _():
            s = i - 1
            slot = lax.rem(s, 2)
            side_copy(s, theirs).wait_recv()
            for n in range(2):
                part_y = jnp.dot(
                    held[s], proj_ref[:, n * 256 : (n + 1) * 256], preferred_element_type=jnp.float32
                )
                y_own[slot, 2 * n] = part_y[:, :128]
                y_own[slot, 2 * n + 1] = part_y[:, 128:]
            for k in range(2):
                rows = pl.ds(k * half, half)
                other = 3 - zpair[k] if k == 0 else zpair[k] + 1 - 2 * lax.rem(zpair[k], 2)
                out1[s, k, 0] = y_own[slot, zpair[k], rows, :].astype(jnp.bfloat16)
                out1[s, k, 1] = y_own[slot, other, rows, :].astype(jnp.bfloat16)
                sum1_copy(s, k).start()

        pass_on(i, 1)

        @pl.when(i == 4)
        def _():
            codes_in()
            store[...] = store_ref[...].astype(jnp.float32)

        @pl.when(jnp.logical_and(i >= 4, i < steps + 4))
        def _():
            s = i - 4
            slot = lax.rem(s, 2)
            for k in range(2):
                sum2_copy(s, k).wait_recv()
            for chunk in range(4):
                ring_core, way = chunk // 2, chunk % 2
                at = cycle_position(x, y, ring_core)
                origin = cycle_device(lax.rem(at + (CHIPS - s if way == 0 else s), CHIPS), ring_core)
                token = pl.multiple_of((origin * 2 + way) * part, part)
                rows = pl.ds(chunk * part, part)
                inside = pl.ds((chunk % 2) * part, part)

                def seek(group, carry):
                    for j in range(8):
                        at_row = group * 8 + j
                        aim[pl.ds(chunk * part + at_row, 1), :] = store[
                            pl.ds(perm_ref[token + at_row], 1), :
                        ]
                    return carry

                lax.fori_loop(0, part // 8, seek, 0)
                diff = (
                    y_keep[slot, rows, :]
                    + in2[s, chunk // 2, inside, :].astype(jnp.float32)
                    - aim[rows, :]
                )
                rows_g[s, z, rows, :] = (diff * inv_root).astype(jnp.bfloat16)
                squares[...] += jnp.sum((diff * diff).reshape(part // 8, 8, diff.shape[1]), axis=0)
            for k in range(2):
                rows1_copy(s, k, z).start()

        pass_on(i, 2)

        @pl.when(jnp.logical_and(i >= 2, i < steps + 2))
        def _():
            s = i - 2
            slot = lax.rem(s, 2)
            for k in range(2):
                rows = pl.ds(k * half, half)
                sum1_copy(s, k).wait_recv()
                passed = y_own[slot, zpair[1 - k], rows, :] + in1[s, k, 1].astype(jnp.float32)
                out2[s, k] = passed.astype(jnp.bfloat16)
                sum2_copy(s, k).start()
                y_keep[slot, rows, :] = y_own[slot, z, rows, :] + in1[s, k, 0].astype(jnp.float32)

        @pl.when(jnp.logical_and(i >= 5, i < steps + 5))
        def _():
            s = i - 5
            for k in range(2):
                rows1_copy(s, k, zpair[k]).wait_recv()
            for k in range(2):
                rows2_copy(s, k, zpair[1 - k]).start()

        pass_on(i, 3)

        @pl.when(i < steps)
        def _():
            side_copy(i, mine).start()

        @pl.when(i == steps + 3)
        def _():
            loss_out(0)

        @pl.when(i == steps + 4)
        def _():
            loss_in(0)
            loss_out(1)

        @pl.when(i == steps + 5)
        def _():
            loss_in(1)
            loss_out(2)

        @pl.when(i >= 6)
        def _():
            s = i - 6
            for k in range(2):
                rows2_copy(s, k, 3 - zpair[k] if k == 0 else zpair[k] + 1 - 2 * lax.rem(zpair[k], 2)).wait_recv()
            rows = jnp.concatenate([rows_g[s, q] for q in range(4)], axis=1)
            for f in range(8):
                features = slice(f * 256, (f + 1) * 256)
                total[features, :] += lax.dot_general(
                    held[s, :, features], rows, (((0,), (0,)), ((), ())), preferred_element_type=jnp.float32
                )

            @pl.when(s < steps - 1)
            def _():
                for way in range(2):
                    for sub in range(4):
                        ring_copy(s, way, sub, 1).wait_send()

            side_copy(s, mine).wait_send()
            for k in range(2):
                sum1_copy(s, k).wait_send()
                sum2_copy(s, k).wait_send()
                rows1_copy(s, k, z).wait_send()
                rows2_copy(s, k, zpair[1 - k]).wait_send()

        @pl.when(i == 8)
        def _():
            sends_out()

        @pl.when(i == 10)
        def _():
            codes_out()

        return carry

    lax.fori_loop(0, steps + 6, body, 0)

    def piece_out(f):
        rows = pl.ds(f * 256, 256)
        return pltpu.make_async_copy(rounded.at[rows], grad_ref.at[rows], rounded_sem.at[f])

    for f in range(8):
        rounded[f * 256 : (f + 1) * 256, :] = total[f * 256 : (f + 1) * 256, :].astype(jnp.bfloat16)
        piece_out(f).start()
    loss_in(2)
    for group in range(3):
        for j in range(1, sizes[group]):
            loss_copy(group, j, False).wait_send()
    loss_ref[0, 0] = jnp.sum(squares[...]) * share
    for f in range(8):
        piece_out(f).wait()


LAYER_SCRATCH = 33


def kernel(
    eps,
    inv_root,
    share,
    h_ref,
    value_ref,
    out_ref,
    gain_ref,
    proj_ref,
    codes_ref,
    scale_ref,
    perm_ref,
    grad_ref,
    loss_ref,
    held,
    store_ref,
    proj,
    proj_sem,
    *scratch,
):
    core = lax.rem(lax.axis_index("dp"), 2)
    rows = held.shape[1] // 2
    fetch_proj = pltpu.make_async_copy(proj_ref, proj, proj_sem)
    fetch_proj.start()
    codes_in, codes_out, sends_out = run_layers(
        eps,
        h_ref,
        value_ref,
        out_ref,
        gain_ref,
        codes_ref,
        scale_ref,
        held.at[0, pl.ds(pl.multiple_of(core * rows, rows), rows)],
        store_ref,
        *scratch[:LAYER_SCRATCH],
    )
    fetch_proj.wait()
    run_wide(
        inv_root,
        share,
        codes_in,
        codes_out,
        sends_out,
        store_ref,
        perm_ref,
        proj,
        grad_ref,
        loss_ref,
        held,
        *scratch[LAYER_SCRATCH:],
    )


def distill(hidden, value_weight, folded_out, gain, proj, codes, scales, perm):
    rows, features = hidden.shape
    head = value_weight.shape[1]
    columns = proj.shape[1]
    quarter = columns // 4
    tokens = rows * RANKS
    block = 2 * rows
    wide_half = block // 2
    grid = (4, SIDE, SIDE, 2)
    value_weight = value_weight.reshape(*grid, features // RANKS, head)
    folded_out = folded_out.reshape(*grid[1:], head // RANKS, 4 * features)
    bf16, f32 = jnp.bfloat16, jnp.float32
    dma = pltpu.SemaphoreType.DMA
    message = pltpu.VMEM((4, 2, 4, rows // 8, head + LANES), bf16)
    lanes = (features // LANES, LANES)
    layer_scratch = [
        pltpu.VMEM((*grid, features // RANKS, head), bf16),
        pltpu.VMEM((*grid, head // RANKS, features), bf16),
        pltpu.VMEM(gain.shape, bf16),
        pltpu.VMEM((4, *lanes), bf16),
        pltpu.VMEM((4, *lanes), bf16),
        pltpu.VMEM(scales.shape, bf16),
        pltpu.VMEM((rows, head + LANES), f32),
        pltpu.VMEM((rows, features), bf16),
        pltpu.VMEM((rows, head), bf16),
        message,
        message,
        message,
        message,
        pltpu.VMEM((RANKS, rows, LANES), bf16),
        dma((5,)),
        *[dma((2, 3))] * 3,
        *[dma((2, 3, SIDE))] * 6,
        dma((3,)),
        dma((3,)),
        *[dma((4, 2, 4))] * 4,
        *[dma((RANKS,))] * 3,
    ]
    wide_scratch = [
        pltpu.VMEM((8, quarter), f32),
        pltpu.VMEM((features, columns), f32),
        pltpu.VMEM((features, columns), bf16),
        dma((8,)),
        pltpu.VMEM((2, 4, block, quarter), f32),
        pltpu.VMEM((2, block, quarter), f32),
        pltpu.VMEM((CHIPS, 2, 2, wide_half, quarter), bf16),
        pltpu.VMEM((CHIPS, 2, 2, wide_half, quarter), bf16),
        pltpu.VMEM((CHIPS, 2, wide_half, quarter), bf16),
        pltpu.VMEM((CHIPS, 2, wide_half, quarter), bf16),
        pltpu.VMEM((CHIPS, 4, block, quarter), bf16),
        pltpu.VMEM((tokens, LANES), f32),
        pltpu.VMEM((block, quarter), f32),
        pltpu.VMEM((3, 2 * SIDE, 8, quarter), f32),
        dma((CHIPS, 2, 4)),
        dma((CHIPS, 2, 4)),
        dma((CHIPS,)),
        dma((CHIPS,)),
        dma((CHIPS, 2)),
        dma((CHIPS, 2)),
        dma((CHIPS, 2)),
        dma((CHIPS, 2)),
        dma((CHIPS, 2)),
        dma((CHIPS, 2)),
        dma((CHIPS, 2)),
        dma((CHIPS, 2)),
        dma((3, 2 * SIDE)),
        dma((3, 2 * SIDE)),
    ]
    smem = pl.BlockSpec(memory_space=pltpu.SMEM)
    anywhere = pl.BlockSpec(memory_space=pl.ANY)
    return pl.pallas_call(
        functools.partial(kernel, 1e-5, 1.0 / math.sqrt(tokens), 0.5 / (tokens * columns * RANKS)),
        out_shape=(
            jax.ShapeDtypeStruct((features, columns), bf16),
            jax.ShapeDtypeStruct((1, 1), f32),
        ),
        in_specs=[anywhere] * 7 + [smem],
        out_specs=(anywhere, smem),
        scratch_shapes=[
            pltpu.VMEM((CHIPS, block, features), bf16),
            pltpu.VMEM((tokens, LANES), bf16),
            pltpu.VMEM(proj.shape, bf16),
            dma,
        ]
        + layer_scratch
        + wide_scratch,
        compiler_params=pltpu.CompilerParams(
            collective_id=0, has_side_effects=True, vmem_limit_bytes=63 * 1024 * 1024
        ),
    )(hidden, value_weight, folded_out, gain, proj, codes, scales, perm)


def shards(
    student_in, value_weight, folded_out, norm_gain, proj, teacher_codes, teacher_scales, perm
):
    grad_proj, loss = distill(
        student_in,
        value_weight[0],
        folded_out[0],
        norm_gain,
        proj,
        teacher_codes,
        teacher_scales[None, :],
        perm,
    )
    return (grad_proj, loss[0, 0])


def solution(mesh):
    return jax.shard_map(
        shards,
        mesh=mesh,
        in_specs=(
            P("dp", "pipe"),
            P("pipe", None, None),
            P("pipe", None, None),
            P("pipe", None),
            P("pipe", "dp"),
            P("dp", None),
            P("dp"),
            P(),
        ),
        out_specs=(P("pipe", "dp"), P()),
        check_vma=False,
    )
```

```python
import functools
import math

import jax
import jax.numpy as jnp
from jax import lax
from jax.experimental import pallas as pl
from jax.experimental.pallas import tpu as pltpu
from jax.sharding import PartitionSpec as P

MESH = pl.DeviceIdType.MESH
SIDE = 4
CHIPS = SIDE * SIDE
RANKS = 2 * CHIPS
LANES = 128


def place(dp):
    core = lax.rem(dp, 2)
    chip = dp // 2
    return chip // SIDE, lax.rem(chip, SIDE), core


def cycle_position(x, y, core):
    return SIDE * (y + core * (x - y)) + lax.rem(x + y, SIDE)


def cycle_device(position, core):
    major = position // SIDE
    minor = lax.rem(lax.rem(position, SIDE) - major + SIDE, SIDE)
    x = minor + core * (major - minor)
    y = major + core * (minor - major)
    return (x * SIDE + y) * 2 + core


def run_layers(
    eps,
    h_ref,
    value_ref,
    out_ref,
    gain_ref,
    codes_ref,
    scale_ref,
    hidden_ref,
    store_ref,
    w_value,
    w_out,
    gain_row,
    gain_own,
    gains,
    scale_row,
    products,
    normed,
    values,
    out1,
    in1,
    out2,
    in2,
    staged,
    own_sem,
    first_send,
    first_recv,
    late_send,
    near_send,
    near_recv,
    far_send,
    far_recv,
    side_send,
    side_recv,
    gain_send,
    gain_recv,
    sum1_send,
    sum1_recv,
    sum2_send,
    sum2_recv,
    stage_sem,
    code_send,
    code_recv,
):
    dp = lax.axis_index("dp")
    z = lax.axis_index("pipe")
    x, y, core = place(dp)
    sibling = dp + 1 - 2 * core
    zpair = (z + 1 - 2 * lax.rem(z, 2), 3 - z)
    rows, features = hidden_ref.shape
    head = value_ref.shape[-1]
    half = rows // 2
    quarter = rows // 8
    weights = (w_value, w_out)
    width = 4 * features

    def greet_all():
        barrier = pltpu.get_barrier_semaphore()

        def greet(j, carry):
            pl.semaphore_signal(
                barrier, inc=1, device_id=(lax.rem(dp + j, RANKS), z), device_id_type=MESH
            )
            return carry

        lax.fori_loop(1, RANKS, greet, 0)
        for j in range(1, 4):
            pl.semaphore_signal(
                barrier, inc=1, device_id=(dp, lax.rem(z + j, 4)), device_id_type=MESH
            )
        pl.semaphore_wait(barrier, RANKS + 2)

    def first_copy(kind, j):
        to = lax.rem(z + j, 4)
        if kind == 0:
            source = value_ref.at[to, x, y, core]
        else:
            source = out_ref.at[x, y, core, :, pl.ds(pl.multiple_of(to * features, features), features)]
        return pltpu.make_async_remote_copy(
            src_ref=source,
            dst_ref=weights[kind].at[4 - j, x, y, core],
            send_sem=first_send.at[kind, j - 1],
            recv_sem=first_recv.at[kind, 3 - j],
            device_id=(dp, to),
            device_id_type=MESH,
        )

    def first_arrival(kind, r):
        block = weights[kind].at[r, x, y, core]
        return pltpu.make_async_remote_copy(
            src_ref=block,
            dst_ref=block,
            send_sem=first_send.at[kind, r - 1],
            recv_sem=first_recv.at[kind, r - 1],
            device_id=(dp, lax.rem(z + r, 4)),
            device_id_type=MESH,
        )

    spot = (x, y)

    def near_copy(kind, r, j, arrival):
        there = lax.rem(spot[kind] + j, SIDE)
        at = there if arrival else spot[kind]
        block = w_value.at[r, at, y, core] if kind == 0 else w_out.at[r, x, at, core]
        chip = there * SIDE + y if kind == 0 else x * SIDE + there
        return pltpu.make_async_remote_copy(
            src_ref=block,
            dst_ref=block,
            send_sem=near_send.at[kind, r - 1, j],
            recv_sem=near_recv.at[kind, r - 1, at],
            device_id=(chip * 2 + core, z),
            device_id_type=MESH,
        )

    def far_copy(kind, r, j, arrival):
        there = lax.rem(spot[1 - kind] + j, SIDE)
        at = there if arrival else spot[1 - kind]
        block = w_value.at[r, :, at, core] if kind == 0 else w_out.at[r, at, :, core]
        chip = there * SIDE + y if kind == 1 else x * SIDE + there
        return pltpu.make_async_remote_copy(
            src_ref=block,
            dst_ref=block,
            send_sem=far_send.at[kind, r - 1, j],
            recv_sem=far_recv.at[kind, r - 1, at],
            device_id=(chip * 2 + core, z),
            device_id_type=MESH,
        )

    def late_copy(kind, j):
        to = lax.rem(z + j, 4)
        at = lax.rem(spot[1 - kind] + 2, SIDE)
        if kind == 0:
            source = value_ref.at[to, :, at, core]
            target = w_value.at[4 - j, :, at, core]
        else:
            source = out_ref.at[at, :, core, :, pl.ds(pl.multiple_of(to * features, features), features)]
            target = w_out.at[4 - j, at, :, core]
        return pltpu.make_async_remote_copy(
            src_ref=source,
            dst_ref=target,
            send_sem=late_send.at[kind, j - 1],
            recv_sem=far_recv.at[kind, 3 - j, at],
            device_id=(dp, to),
            device_id_type=MESH,
        )

    def gives_late(j):
        return jnp.logical_and(z >= 1, z < lax.rem(z + j, 4))

    def takes_late(k):
        return jnp.logical_and(k >= 1, k < z)

    def side_copy(kind, r, j, owner):
        at = lax.rem(spot[1 - kind] + j, SIDE)
        block = w_value.at[r, :, at, owner] if kind == 0 else w_out.at[r, at, :, owner]
        return pltpu.make_async_remote_copy(
            src_ref=block,
            dst_ref=block,
            send_sem=side_send.at[kind, r - 1, at],
            recv_sem=side_recv.at[kind, r - 1, at],
            device_id=(sibling, z),
            device_id_type=MESH,
        )

    def gain_copy(j):
        to = lax.rem(z + j, 4)
        return pltpu.make_async_remote_copy(
            src_ref=gain_own.at[to],
            dst_ref=gains.at[4 - j],
            send_sem=gain_send.at[j - 1],
            recv_sem=gain_recv.at[3 - j],
            device_id=(dp, to),
            device_id_type=MESH,
        )

    def own_copies():
        columns = pl.ds(pl.multiple_of(z * features, features), features)
        return (
            pltpu.make_async_copy(value_ref.at[z], w_value.at[0], own_sem.at[0]),
            pltpu.make_async_copy(out_ref.at[:, :, :, :, columns], w_out.at[0], own_sem.at[1]),
        )

    def stage_copy(d):
        columns = pl.ds(pl.multiple_of((d * 4 + z) * LANES, LANES), LANES)
        return pltpu.make_async_copy(codes_ref.at[:, columns], staged.at[d], stage_sem.at[d])

    def code_copy(d):
        return pltpu.make_async_remote_copy(
            src_ref=staged.at[d],
            dst_ref=store_ref.at[pl.ds(pl.multiple_of(dp * rows, rows), rows)],
            send_sem=code_send.at[d],
            recv_sem=code_recv.at[dp],
            device_id=(d, z),
            device_id_type=MESH,
        )

    def code_arrival(d):
        block = store_ref.at[pl.ds(pl.multiple_of(d * rows, rows), rows)]
        return pltpu.make_async_remote_copy(
            src_ref=block,
            dst_ref=block,
            send_sem=code_send.at[d],
            recv_sem=code_recv.at[d],
            device_id=(d, z),
            device_id_type=MESH,
        )

    def sum_copy(phase, layer, k, part):
        source, target, send, recv = (
            (out1, in1, sum1_send, sum1_recv),
            (out2, in2, sum2_send, sum2_recv),
        )[phase]
        return pltpu.make_async_remote_copy(
            src_ref=source.at[layer, k, part],
            dst_ref=target.at[layer, k, part],
            send_sem=send.at[layer, k, part],
            recv_sem=recv.at[layer, k, part],
            device_id=(dp, zpair[k ^ phase]),
            device_id_type=MESH,
        )

    small = (
        pltpu.make_async_copy(gain_ref, gain_row, own_sem.at[2]),
        pltpu.make_async_copy(scale_ref, scale_row, own_sem.at[3]),
        pltpu.make_async_copy(h_ref, hidden_ref, own_sem.at[4]),
    )
    for copy in small:
        copy.start()
    greet_all()
    for j in (1, 3, 2):
        first_copy(0, j).start()
        first_copy(1, j).start()
    for j in (1, 2):

        @pl.when(gives_late(j))
        def _():
            for kind in range(2):
                late_copy(kind, j).start()

    for copy in own_copies():
        copy.start()

    def fetch(d, carry):
        stage_copy(d).start()
        return carry

    lax.fori_loop(0, RANKS, fetch, 0)
    for copy in small:
        copy.wait()
    for part in range(4):
        for j in range(features // LANES):
            at = part * features + j * LANES
            gain_own[part, j : j + 1, :] = gain_row[:, at : at + LANES]
    for j in range(1, 4):
        gain_copy(j).start()
    gains[0] = gain_own[z]
    def turn(k):
        layer = k + jnp.where(k >= z, 1, 0)
        return lax.rem(layer - z + 4, 4)

    def spread_near(k, carry):
        r = turn(k)
        for kind in range(2):
            first_arrival(kind, r).wait_recv()
            for j in (1, 3, 2):
                near_copy(kind, r, j, False).start()
        return carry

    def spread_far(k):
        r = turn(k)
        for kind in range(2):
            for j in (1, 3, 2):
                near_copy(kind, r, j, True).wait_recv()
            for j in (1, 3):
                far_copy(kind, r, j, False).start()

            @pl.when(jnp.logical_not(takes_late(k)))
            def _():
                far_copy(kind, r, 2, False).start()

        for kind in range(2):
            side_copy(kind, r, 0, core).start()

    def settle(r, order):
        for j in order:
            for kind in range(2):
                far_copy(kind, r, j, True).wait_recv()
                side_copy(kind, r, j, core).start()

    lax.fori_loop(0, 3, spread_near, 0)
    def spread_all(k, carry):
        spread_far(k)
        return carry

    lax.fori_loop(0, 3, spread_all, 0)
    scale = jnp.broadcast_to(scale_row[...].astype(jnp.float32), (rows, LANES)).T

    def scale_codes(d, carry):
        stage_copy(d).wait()
        staged[d] = (staged[d].astype(jnp.float32) * scale).astype(jnp.bfloat16)
        return carry

    lax.fori_loop(0, RANKS, scale_codes, 0)
    store_ref[pl.ds(pl.multiple_of(dp * rows, rows), rows), :] = staged[dp]

    for copy in own_copies():
        copy.wait()
    for j in range(1, 4):
        gain_copy(j).wait()

    def send_codes(j, carry):
        code_copy(lax.rem(dp + j, RANKS)).start()
        return carry

    def layer_step(layer, carry):
        r = lax.rem(layer - z + 4, 4)

        @pl.when(layer != z)
        def _():
            settle(r, (1, 3, 2))
            for kind in range(2):
                for j in range(SIDE):
                    side_copy(kind, r, j, 1 - core).wait_recv()

        @pl.when(layer == 2)
        def _():
            lax.fori_loop(1, RANKS, send_codes, 0)

        gain = gains[r].astype(jnp.float32)
        squares = jnp.zeros((rows, LANES), jnp.float32)
        for j in range(features // LANES):
            columns = slice(j * LANES, (j + 1) * LANES)
            tile = hidden_ref[:, columns].astype(jnp.float32)
            squares += tile * tile
            normed[:, columns] = (tile * gain[j : j + 1, :]).astype(jnp.bfloat16)
        squares = jnp.broadcast_to(jnp.sum(squares, axis=1, keepdims=True), (rows, LANES))
        products[:, :head] = jnp.dot(
            normed[...], w_value[r].reshape(features, head), preferred_element_type=jnp.float32
        )
        products[:, head:] = squares
        lane = lax.broadcasted_iota(jnp.int32, (quarter, LANES), 1)

        def leave(phase, k, part):
            rows_in = slice(k * half + part * quarter, k * half + (part + 1) * quarter)
            buffer = (out1, out2)[phase]
            squares = products[rows_in, head:]
            high = squares.astype(jnp.bfloat16).astype(jnp.float32)
            buffer[layer, k, part, :, :head] = products[rows_in, :head].astype(jnp.bfloat16)
            buffer[layer, k, part, :, head:] = jnp.where(lane < LANES // 2, high, squares - high).astype(
                jnp.bfloat16
            )
            sum_copy(phase, layer, k, part).start()

        def arrive(phase, k, part):
            rows_in = slice(k * half + part * quarter, k * half + (part + 1) * quarter)
            buffer = (in1, in2)[phase]
            sum_copy(phase, layer, k, part).wait_recv()
            marks = buffer[layer, k, part, :, head:].astype(jnp.float32)
            so_far = products[rows_in, :head] + buffer[layer, k, part, :, :head].astype(jnp.float32)
            return rows_in, so_far, products[rows_in, head:] + marks + pltpu.roll(marks, LANES // 2, 1)

        order = [(k, part) for part in range(4) for k in range(2)]
        for k, part in order:
            leave(0, k, part)
        for k, part in order:
            rows_in, so_far, squares = arrive(0, k, part)
            products[rows_in, :head] = so_far
            products[rows_in, head:] = squares
            leave(1, k, part)
        for k, part in order:
            rows_in, so_far, squares = arrive(1, k, part)
            scale = lax.rsqrt(squares * (1.0 / width) + eps)
            for j in range(head // LANES):
                columns = slice(j * LANES, (j + 1) * LANES)
                values[rows_in, columns] = (so_far[:, columns] * scale).astype(jnp.bfloat16)
        for n in range(features // 512):
            columns = slice(n * 512, (n + 1) * 512)
            branch = jnp.dot(
                values[...],
                w_out[r, :, :, :, :, columns].reshape(head, 512),
                preferred_element_type=jnp.float32,
            )
            hidden_ref[:, columns] = (hidden_ref[:, columns].astype(jnp.float32) + branch).astype(
                jnp.bfloat16
            )
        return carry

    lax.fori_loop(0, 4, layer_step, 0)

    def sends_out():
        for kind in range(2):
            for j in range(1, 4):
                first_copy(kind, j).wait_send()
                for r in range(1, 4):
                    near_copy(kind, r, j, False).wait_send()
                    if j != 2:
                        far_copy(kind, r, j, False).wait_send()
            for j in (1, 2):

                @pl.when(gives_late(j))
                def _():
                    late_copy(kind, j).wait_send()

            for k in range(3):

                @pl.when(jnp.logical_not(takes_late(k)))
                def _():
                    far_copy(kind, turn(k), 2, False).wait_send()

            for r in range(1, 4):
                for j in range(SIDE):
                    side_copy(kind, r, j, core).wait_send()
        for layer in range(4):
            for k in range(2):
                for part in range(4):
                    for phase in range(2):
                        sum_copy(phase, layer, k, part).wait_send()

    def codes_in():
        def arrive(j, carry):
            code_arrival(lax.rem(dp + j, RANKS)).wait_recv()
            return carry

        lax.fori_loop(1, RANKS, arrive, 0)

    def codes_out():
        def leave(j, carry):
            code_copy(lax.rem(dp + j, RANKS)).wait_send()
            return carry

        lax.fori_loop(1, RANKS, leave, 0)

    return codes_in, codes_out, sends_out


def run_wide(
    inv_root,
    share,
    codes_in,
    codes_out,
    sends_out,
    store_ref,
    perm_ref,
    proj_ref,
    grad_ref,
    loss_ref,
    held,
    squares,
    total,
    rounded,
    rounded_sem,
    y_own,
    y_keep,
    out1,
    in1,
    out2,
    in2,
    rows_g,
    store,
    aim,
    losses,
    ring_send,
    ring_recv,
    side_send,
    side_recv,
    sum1_send,
    sum1_recv,
    sum2_send,
    sum2_recv,
    rows1_send,
    rows1_recv,
    rows2_send,
    rows2_recv,
    loss_send,
    loss_recv,
):
    dp = lax.axis_index("dp")
    z = lax.axis_index("pipe")
    x, y, core = place(dp)
    here = cycle_position(x, y, core)
    after = cycle_device(lax.rem(here + 1, CHIPS), core)
    before = cycle_device(lax.rem(here + CHIPS - 1, CHIPS), core)
    sibling = dp + 1 - 2 * core
    za = z + 1 - 2 * lax.rem(z, 2)
    zb = 3 - z
    steps = CHIPS
    part = held.shape[1] // 4
    block = 4 * part
    half = block // 2
    zpair = (za, zb)
    ring = (after, before)

    sizes = (4, SIDE, 2 * SIDE)
    spots = (z, y, 2 * x + core)

    def peer(group, j):
        spot = lax.rem(spots[group] + j, sizes[group])
        if group == 0:
            return dp, spot
        if group == 1:
            return (x * SIDE + spot) * 2 + core, z
        return ((spot // 2) * SIDE + y) * 2 + lax.rem(spot, 2), z

    mine = pl.multiple_of(core * 2 * part, 2 * part)
    theirs = pl.multiple_of((1 - core) * 2 * part, 2 * part)

    def ring_copy(s, way, sub, later):
        start = mine + way * part + sub * (part // 4)
        rows = pl.ds(pl.multiple_of(start, part // 4), part // 4)
        return pltpu.make_async_remote_copy(
            src_ref=held.at[s, rows],
            dst_ref=held.at[s + later, rows],
            send_sem=ring_send.at[s, way, sub],
            recv_sem=ring_recv.at[s + later, way, sub],
            device_id=(ring[way], z),
            device_id_type=MESH,
        )

    def side_copy(s, start):
        rows = pl.ds(start, 2 * part)
        return pltpu.make_async_remote_copy(
            src_ref=held.at[s, rows],
            dst_ref=held.at[s, rows],
            send_sem=side_send.at[s],
            recv_sem=side_recv.at[s],
            device_id=(sibling, z),
            device_id_type=MESH,
        )

    def sum1_copy(s, k):
        return pltpu.make_async_remote_copy(
            src_ref=out1.at[s, k],
            dst_ref=in1.at[s, k],
            send_sem=sum1_send.at[s, k],
            recv_sem=sum1_recv.at[s, k],
            device_id=(dp, zpair[k]),
            device_id_type=MESH,
        )

    def sum2_copy(s, k):
        return pltpu.make_async_remote_copy(
            src_ref=out2.at[s, k],
            dst_ref=in2.at[s, k],
            send_sem=sum2_send.at[s, k],
            recv_sem=sum2_recv.at[s, k],
            device_id=(dp, zpair[1 - k]),
            device_id_type=MESH,
        )

    def rows1_copy(s, k, quarter):
        return pltpu.make_async_remote_copy(
            src_ref=rows_g.at[s, quarter],
            dst_ref=rows_g.at[s, quarter],
            send_sem=rows1_send.at[s, k],
            recv_sem=rows1_recv.at[s, k],
            device_id=(dp, zpair[k]),
            device_id_type=MESH,
        )

    def rows2_copy(s, k, quarter):
        rows = pl.ds(k * half, half)
        return pltpu.make_async_remote_copy(
            src_ref=rows_g.at[s, quarter, rows],
            dst_ref=rows_g.at[s, quarter, rows],
            send_sem=rows2_send.at[s, k],
            recv_sem=rows2_recv.at[s, k],
            device_id=(dp, zpair[k]),
            device_id_type=MESH,
        )

    def loss_copy(group, j, arrival):
        spot = lax.rem(spots[group] + j, sizes[group]) if arrival else spots[group]
        return pltpu.make_async_remote_copy(
            src_ref=losses.at[group, spot],
            dst_ref=losses.at[group, spot],
            send_sem=loss_send.at[group, j],
            recv_sem=loss_recv.at[group, spot],
            device_id=peer(group, j),
            device_id_type=MESH,
        )

    def loss_out(group):
        losses[group, spots[group]] = squares[...]
        for j in range(1, sizes[group]):
            loss_copy(group, j, False).start()

    def loss_in(group):
        for j in range(1, sizes[group]):
            loss_copy(group, j, True).wait_recv()
        squares[...] = functools.reduce(
            jnp.add, [losses[group, spot] for spot in range(sizes[group])]
        )

    squares[...] = jnp.zeros_like(squares)
    total[...] = jnp.zeros_like(total)

    def pass_on(i, sub):
        @pl.when(jnp.logical_and(i > 0, i < steps))
        def _():
            for way in range(2):
                ring_copy(i, way, sub, 0).wait_recv()

        @pl.when(i < steps - 1)
        def _():
            for way in range(2):
                ring_copy(i, way, sub, 1).start()

    def body(i, carry):
        pass_on(i, 0)

        @pl.when(jnp.logical_and(i >= 1, i < steps + 1))
        def _():
            s = i - 1
            slot = lax.rem(s, 2)
            side_copy(s, theirs).wait_recv()
            for n in range(2):
                part_y = jnp.dot(
                    held[s], proj_ref[:, n * 256 : (n + 1) * 256], preferred_element_type=jnp.float32
                )
                y_own[slot, 2 * n] = part_y[:, :128]
                y_own[slot, 2 * n + 1] = part_y[:, 128:]
            for k in range(2):
                rows = pl.ds(k * half, half)
                other = 3 - zpair[k] if k == 0 else zpair[k] + 1 - 2 * lax.rem(zpair[k], 2)
                out1[s, k, 0] = y_own[slot, zpair[k], rows, :].astype(jnp.bfloat16)
                out1[s, k, 1] = y_own[slot, other, rows, :].astype(jnp.bfloat16)
                sum1_copy(s, k).start()

        pass_on(i, 1)

        @pl.when(i == 4)
        def _():
            codes_in()
            store[...] = store_ref[...].astype(jnp.float32)

        @pl.when(jnp.logical_and(i >= 4, i < steps + 4))
        def _():
            s = i - 4
            slot = lax.rem(s, 2)
            for k in range(2):
                sum2_copy(s, k).wait_recv()
            for chunk in range(4):
                ring_core, way = chunk // 2, chunk % 2
                at = cycle_position(x, y, ring_core)
                origin = cycle_device(lax.rem(at + (CHIPS - s if way == 0 else s), CHIPS), ring_core)
                token = pl.multiple_of((origin * 2 + way) * part, part)
                rows = pl.ds(chunk * part, part)
                inside = pl.ds((chunk % 2) * part, part)

                def seek(group, carry):
                    for j in range(8):
                        at_row = group * 8 + j
                        aim[pl.ds(chunk * part + at_row, 1), :] = store[
                            pl.ds(perm_ref[token + at_row], 1), :
                        ]
                    return carry

                lax.fori_loop(0, part // 8, seek, 0)
                diff = (
                    y_keep[slot, rows, :]
                    + in2[s, chunk // 2, inside, :].astype(jnp.float32)
                    - aim[rows, :]
                )
                rows_g[s, z, rows, :] = (diff * inv_root).astype(jnp.bfloat16)
                squares[...] += jnp.sum((diff * diff).reshape(part // 8, 8, diff.shape[1]), axis=0)
            for k in range(2):
                rows1_copy(s, k, z).start()

        pass_on(i, 2)

        @pl.when(jnp.logical_and(i >= 2, i < steps + 2))
        def _():
            s = i - 2
            slot = lax.rem(s, 2)
            for k in range(2):
                rows = pl.ds(k * half, half)
                sum1_copy(s, k).wait_recv()
                passed = y_own[slot, zpair[1 - k], rows, :] + in1[s, k, 1].astype(jnp.float32)
                out2[s, k] = passed.astype(jnp.bfloat16)
                sum2_copy(s, k).start()
                y_keep[slot, rows, :] = y_own[slot, z, rows, :] + in1[s, k, 0].astype(jnp.float32)

        @pl.when(jnp.logical_and(i >= 5, i < steps + 5))
        def _():
            s = i - 5
            for k in range(2):
                rows1_copy(s, k, zpair[k]).wait_recv()
            for k in range(2):
                rows2_copy(s, k, zpair[1 - k]).start()

        pass_on(i, 3)

        @pl.when(i < steps)
        def _():
            side_copy(i, mine).start()

        @pl.when(i == steps + 3)
        def _():
            loss_out(0)

        @pl.when(i == steps + 4)
        def _():
            loss_in(0)
            loss_out(1)

        @pl.when(i == steps + 5)
        def _():
            loss_in(1)
            loss_out(2)

        @pl.when(i >= 6)
        def _():
            s = i - 6
            for k in range(2):
                rows2_copy(s, k, 3 - zpair[k] if k == 0 else zpair[k] + 1 - 2 * lax.rem(zpair[k], 2)).wait_recv()
            rows = jnp.concatenate([rows_g[s, q] for q in range(4)], axis=1)
            for f in range(8):
                features = slice(f * 256, (f + 1) * 256)
                total[features, :] += lax.dot_general(
                    held[s, :, features], rows, (((0,), (0,)), ((), ())), preferred_element_type=jnp.float32
                )

            @pl.when(s < steps - 1)
            def _():
                for way in range(2):
                    for sub in range(4):
                        ring_copy(s, way, sub, 1).wait_send()

            side_copy(s, mine).wait_send()
            for k in range(2):
                sum1_copy(s, k).wait_send()
                sum2_copy(s, k).wait_send()
                rows1_copy(s, k, z).wait_send()
                rows2_copy(s, k, zpair[1 - k]).wait_send()

        @pl.when(i == 8)
        def _():
            sends_out()

        @pl.when(i == 10)
        def _():
            codes_out()

        return carry

    lax.fori_loop(0, steps + 6, body, 0)

    def piece_out(f):
        rows = pl.ds(f * 256, 256)
        return pltpu.make_async_copy(rounded.at[rows], grad_ref.at[rows], rounded_sem.at[f])

    for f in range(8):
        rounded[f * 256 : (f + 1) * 256, :] = total[f * 256 : (f + 1) * 256, :].astype(jnp.bfloat16)
        piece_out(f).start()
    loss_in(2)
    for group in range(3):
        for j in range(1, sizes[group]):
            loss_copy(group, j, False).wait_send()
    loss_ref[0, 0] = jnp.sum(squares[...]) * share
    for f in range(8):
        piece_out(f).wait()


LAYER_SCRATCH = 33


def kernel(
    eps,
    inv_root,
    share,
    h_ref,
    value_ref,
    out_ref,
    gain_ref,
    proj_ref,
    codes_ref,
    scale_ref,
    perm_ref,
    grad_ref,
    loss_ref,
    held,
    store_ref,
    proj,
    proj_sem,
    *scratch,
):
    core = lax.rem(lax.axis_index("dp"), 2)
    rows = held.shape[1] // 2
    fetch_proj = pltpu.make_async_copy(proj_ref, proj, proj_sem)
    fetch_proj.start()
    codes_in, codes_out, sends_out = run_layers(
        eps,
        h_ref,
        value_ref,
        out_ref,
        gain_ref,
        codes_ref,
        scale_ref,
        held.at[0, pl.ds(pl.multiple_of(core * rows, rows), rows)],
        store_ref,
        *scratch[:LAYER_SCRATCH],
    )
    fetch_proj.wait()
    run_wide(
        inv_root,
        share,
        codes_in,
        codes_out,
        sends_out,
        store_ref,
        perm_ref,
        proj,
        grad_ref,
        loss_ref,
        held,
        *scratch[LAYER_SCRATCH:],
    )


def distill(hidden, value_weight, folded_out, gain, proj, codes, scales, perm):
    rows, features = hidden.shape
    head = value_weight.shape[1]
    columns = proj.shape[1]
    quarter = columns // 4
    tokens = rows * RANKS
    block = 2 * rows
    wide_half = block // 2
    grid = (4, SIDE, SIDE, 2)
    value_weight = value_weight.reshape(*grid, features // RANKS, head)
    folded_out = folded_out.reshape(*grid[1:], head // RANKS, 4 * features)
    bf16, f32 = jnp.bfloat16, jnp.float32
    dma = pltpu.SemaphoreType.DMA
    message = pltpu.VMEM((4, 2, 4, rows // 8, head + LANES), bf16)
    lanes = (features // LANES, LANES)
    layer_scratch = [
        pltpu.VMEM((*grid, features // RANKS, head), bf16),
        pltpu.VMEM((*grid, head // RANKS, features), bf16),
        pltpu.VMEM(gain.shape, bf16),
        pltpu.VMEM((4, *lanes), bf16),
        pltpu.VMEM((4, *lanes), bf16),
        pltpu.VMEM(scales.shape, bf16),
        pltpu.VMEM((rows, head + LANES), f32),
        pltpu.VMEM((rows, features), bf16),
        pltpu.VMEM((rows, head), bf16),
        message,
        message,
        message,
        message,
        pltpu.VMEM((RANKS, rows, LANES), bf16),
        dma((5,)),
        *[dma((2, 3))] * 3,
        *[dma((2, 3, SIDE))] * 6,
        dma((3,)),
        dma((3,)),
        *[dma((4, 2, 4))] * 4,
        *[dma((RANKS,))] * 3,
    ]
    wide_scratch = [
        pltpu.VMEM((8, quarter), f32),
        pltpu.VMEM((features, columns), f32),
        pltpu.VMEM((features, columns), bf16),
        dma((8,)),
        pltpu.VMEM((2, 4, block, quarter), f32),
        pltpu.VMEM((2, block, quarter), f32),
        pltpu.VMEM((CHIPS, 2, 2, wide_half, quarter), bf16),
        pltpu.VMEM((CHIPS, 2, 2, wide_half, quarter), bf16),
        pltpu.VMEM((CHIPS, 2, wide_half, quarter), bf16),
        pltpu.VMEM((CHIPS, 2, wide_half, quarter), bf16),
        pltpu.VMEM((CHIPS, 4, block, quarter), bf16),
        pltpu.VMEM((tokens, LANES), f32),
        pltpu.VMEM((block, quarter), f32),
        pltpu.VMEM((3, 2 * SIDE, 8, quarter), f32),
        dma((CHIPS, 2, 4)),
        dma((CHIPS, 2, 4)),
        dma((CHIPS,)),
        dma((CHIPS,)),
        dma((CHIPS, 2)),
        dma((CHIPS, 2)),
        dma((CHIPS, 2)),
        dma((CHIPS, 2)),
        dma((CHIPS, 2)),
        dma((CHIPS, 2)),
        dma((CHIPS, 2)),
        dma((CHIPS, 2)),
        dma((3, 2 * SIDE)),
        dma((3, 2 * SIDE)),
    ]
    smem = pl.BlockSpec(memory_space=pltpu.SMEM)
    anywhere = pl.BlockSpec(memory_space=pl.ANY)
    return pl.pallas_call(
        functools.partial(kernel, 1e-5, 1.0 / math.sqrt(tokens), 0.5 / (tokens * columns * RANKS)),
        out_shape=(
            jax.ShapeDtypeStruct((features, columns), bf16),
            jax.ShapeDtypeStruct((1, 1), f32),
        ),
        in_specs=[anywhere] * 7 + [smem],
        out_specs=(anywhere, smem),
        scratch_shapes=[
            pltpu.VMEM((CHIPS, block, features), bf16),
            pltpu.VMEM((tokens, LANES), bf16),
            pltpu.VMEM(proj.shape, bf16),
            dma,
        ]
        + layer_scratch
        + wide_scratch,
        compiler_params=pltpu.CompilerParams(
            collective_id=0, has_side_effects=True, vmem_limit_bytes=63 * 1024 * 1024
        ),
    )(hidden, value_weight, folded_out, gain, proj, codes, scales, perm)


def shards(
    student_in, value_weight, folded_out, norm_gain, proj, teacher_codes, teacher_scales, perm
):
    grad_proj, loss = distill(
        student_in,
        value_weight[0],
        folded_out[0],
        norm_gain,
        proj,
        teacher_codes,
        teacher_scales[None, :],
        perm,
    )
    return (grad_proj, loss[0, 0])


def solution(mesh):
    return jax.shard_map(
        shards,
        mesh=mesh,
        in_specs=(
            P("dp", "pipe"),
            P("pipe", None, None),
            P("pipe", None, None),
            P("pipe", None),
            P("pipe", "dp"),
            P("dp", None),
            P("dp"),
            P(),
        ),
        out_specs=(P("pipe", "dp"), P()),
        check_vma=False,
    )
```

```python
import functools
import math

import jax
import jax.numpy as jnp
from jax import lax
from jax.experimental import pallas as pl
from jax.experimental.pallas import tpu as pltpu
from jax.sharding import PartitionSpec as P

MESH = pl.DeviceIdType.MESH
SIDE = 4
CHIPS = SIDE * SIDE
RANKS = 2 * CHIPS
LANES = 128


def place(dp):
    core = lax.rem(dp, 2)
    chip = dp // 2
    return chip // SIDE, lax.rem(chip, SIDE), core


def cycle_position(x, y, core):
    return SIDE * (y + core * (x - y)) + lax.rem(x + y, SIDE)


def cycle_device(position, core):
    major = position // SIDE
    minor = lax.rem(lax.rem(position, SIDE) - major + SIDE, SIDE)
    x = minor + core * (major - minor)
    y = major + core * (minor - major)
    return (x * SIDE + y) * 2 + core


def run_layers(
    eps,
    h_ref,
    value_ref,
    out_ref,
    gain_ref,
    codes_ref,
    scale_ref,
    hidden_ref,
    store_ref,
    w_value,
    w_out,
    gain_row,
    gain_own,
    gains,
    scale_row,
    products,
    normed,
    values,
    out1,
    in1,
    out2,
    in2,
    staged,
    own_sem,
    first_send,
    first_recv,
    late_send,
    near_send,
    near_recv,
    far_send,
    far_recv,
    side_send,
    side_recv,
    gain_send,
    gain_recv,
    sum1_send,
    sum1_recv,
    sum2_send,
    sum2_recv,
    stage_sem,
    code_send,
    code_recv,
):
    dp = lax.axis_index("dp")
    z = lax.axis_index("pipe")
    x, y, core = place(dp)
    sibling = dp + 1 - 2 * core
    zpair = (z + 1 - 2 * lax.rem(z, 2), 3 - z)
    rows, features = hidden_ref.shape
    head = value_ref.shape[-1]
    half = rows // 2
    quarter = rows // 8
    weights = (w_value, w_out)
    width = 4 * features

    def greet_all():
        barrier = pltpu.get_barrier_semaphore()

        def greet(j, carry):
            pl.semaphore_signal(
                barrier, inc=1, device_id=(lax.rem(dp + j, RANKS), z), device_id_type=MESH
            )
            return carry

        lax.fori_loop(1, RANKS, greet, 0)
        for j in range(1, 4):
            pl.semaphore_signal(
                barrier, inc=1, device_id=(dp, lax.rem(z + j, 4)), device_id_type=MESH
            )
        pl.semaphore_wait(barrier, RANKS + 2)

    def first_copy(kind, j):
        to = lax.rem(z + j, 4)
        if kind == 0:
            source = value_ref.at[to, x, y, core]
        else:
            source = out_ref.at[x, y, core, :, pl.ds(pl.multiple_of(to * features, features), features)]
        return pltpu.make_async_remote_copy(
            src_ref=source,
            dst_ref=weights[kind].at[4 - j, x, y, core],
            send_sem=first_send.at[kind, j - 1],
            recv_sem=first_recv.at[kind, 3 - j],
            device_id=(dp, to),
            device_id_type=MESH,
        )

    def first_arrival(kind, r):
        block = weights[kind].at[r, x, y, core]
        return pltpu.make_async_remote_copy(
            src_ref=block,
            dst_ref=block,
            send_sem=first_send.at[kind, r - 1],
            recv_sem=first_recv.at[kind, r - 1],
            device_id=(dp, lax.rem(z + r, 4)),
            device_id_type=MESH,
        )

    spot = (x, y)

    def near_copy(kind, r, j, arrival):
        there = lax.rem(spot[kind] + j, SIDE)
        at = there if arrival else spot[kind]
        block = w_value.at[r, at, y, core] if kind == 0 else w_out.at[r, x, at, core]
        chip = there * SIDE + y if kind == 0 else x * SIDE + there
        return pltpu.make_async_remote_copy(
            src_ref=block,
            dst_ref=block,
            send_sem=near_send.at[kind, r - 1, j],
            recv_sem=near_recv.at[kind, r - 1, at],
            device_id=(chip * 2 + core, z),
            device_id_type=MESH,
        )

    def far_copy(kind, r, j, arrival):
        there = lax.rem(spot[1 - kind] + j, SIDE)
        at = there if arrival else spot[1 - kind]
        block = w_value.at[r, :, at, core] if kind == 0 else w_out.at[r, at, :, core]
        chip = there * SIDE + y if kind == 1 else x * SIDE + there
        return pltpu.make_async_remote_copy(
            src_ref=block,
            dst_ref=block,
            send_sem=far_send.at[kind, r - 1, j],
            recv_sem=far_recv.at[kind, r - 1, at],
            device_id=(chip * 2 + core, z),
            device_id_type=MESH,
        )

    def late_copy(kind, j):
        to = lax.rem(z + j, 4)
        at = lax.rem(spot[1 - kind] + 2, SIDE)
        if kind == 0:
            source = value_ref.at[to, :, at, core]
            target = w_value.at[4 - j, :, at, core]
        else:
            source = out_ref.at[at, :, core, :, pl.ds(pl.multiple_of(to * features, features), features)]
            target = w_out.at[4 - j, at, :, core]
        return pltpu.make_async_remote_copy(
            src_ref=source,
            dst_ref=target,
            send_sem=late_send.at[kind, j - 1],
            recv_sem=far_recv.at[kind, 3 - j, at],
            device_id=(dp, to),
            device_id_type=MESH,
        )

    def gives_late(j):
        return jnp.logical_and(z >= 1, z < lax.rem(z + j, 4))

    def takes_late(k):
        return jnp.logical_and(k >= 1, k < z)

    def side_copy(kind, r, j, owner):
        at = lax.rem(spot[1 - kind] + j, SIDE)
        block = w_value.at[r, :, at, owner] if kind == 0 else w_out.at[r, at, :, owner]
        return pltpu.make_async_remote_copy(
            src_ref=block,
            dst_ref=block,
            send_sem=side_send.at[kind, r - 1, at],
            recv_sem=side_recv.at[kind, r - 1, at],
            device_id=(sibling, z),
            device_id_type=MESH,
        )

    def gain_copy(j):
        to = lax.rem(z + j, 4)
        return pltpu.make_async_remote_copy(
            src_ref=gain_own.at[to],
            dst_ref=gains.at[4 - j],
            send_sem=gain_send.at[j - 1],
            recv_sem=gain_recv.at[3 - j],
            device_id=(dp, to),
            device_id_type=MESH,
        )

    def own_copies():
        columns = pl.ds(pl.multiple_of(z * features, features), features)
        return (
            pltpu.make_async_copy(value_ref.at[z], w_value.at[0], own_sem.at[0]),
            pltpu.make_async_copy(out_ref.at[:, :, :, :, columns], w_out.at[0], own_sem.at[1]),
        )

    def stage_copy(d):
        columns = pl.ds(pl.multiple_of((d * 4 + z) * LANES, LANES), LANES)
        return pltpu.make_async_copy(codes_ref.at[:, columns], staged.at[d], stage_sem.at[d])

    def code_copy(d):
        return pltpu.make_async_remote_copy(
            src_ref=staged.at[d],
            dst_ref=store_ref.at[pl.ds(pl.multiple_of(dp * rows, rows), rows)],
            send_sem=code_send.at[d],
            recv_sem=code_recv.at[dp],
            device_id=(d, z),
            device_id_type=MESH,
        )

    def code_arrival(d):
        block = store_ref.at[pl.ds(pl.multiple_of(d * rows, rows), rows)]
        return pltpu.make_async_remote_copy(
            src_ref=block,
            dst_ref=block,
            send_sem=code_send.at[d],
            recv_sem=code_recv.at[d],
            device_id=(d, z),
            device_id_type=MESH,
        )

    def sum_copy(phase, layer, k, part):
        source, target, send, recv = (
            (out1, in1, sum1_send, sum1_recv),
            (out2, in2, sum2_send, sum2_recv),
        )[phase]
        return pltpu.make_async_remote_copy(
            src_ref=source.at[layer, k, part],
            dst_ref=target.at[layer, k, part],
            send_sem=send.at[layer, k, part],
            recv_sem=recv.at[layer, k, part],
            device_id=(dp, zpair[k ^ phase]),
            device_id_type=MESH,
        )

    small = (
        pltpu.make_async_copy(gain_ref, gain_row, own_sem.at[2]),
        pltpu.make_async_copy(scale_ref, scale_row, own_sem.at[3]),
        pltpu.make_async_copy(h_ref, hidden_ref, own_sem.at[4]),
    )
    for copy in small:
        copy.start()
    greet_all()
    for j in (1, 3, 2):
        first_copy(0, j).start()
        first_copy(1, j).start()
    for j in (1, 2):

        @pl.when(gives_late(j))
        def _():
            for kind in range(2):
                late_copy(kind, j).start()

    for copy in own_copies():
        copy.start()

    def fetch(d, carry):
        stage_copy(d).start()
        return carry

    lax.fori_loop(0, RANKS, fetch, 0)
    for copy in small:
        copy.wait()
    for part in range(4):
        for j in range(features // LANES):
            at = part * features + j * LANES
            gain_own[part, j : j + 1, :] = gain_row[:, at : at + LANES]
    for j in range(1, 4):
        gain_copy(j).start()
    gains[0] = gain_own[z]
    def turn(k):
        layer = k + jnp.where(k >= z, 1, 0)
        return lax.rem(layer - z + 4, 4)

    def spread_near(k, carry):
        r = turn(k)
        for kind in range(2):
            first_arrival(kind, r).wait_recv()
            for j in (1, 3, 2):
                near_copy(kind, r, j, False).start()
        return carry

    def spread_far(k):
        r = turn(k)
        for kind in range(2):
            for j in (1, 3, 2):
                near_copy(kind, r, j, True).wait_recv()
            for j in (1, 3):
                far_copy(kind, r, j, False).start()

            @pl.when(jnp.logical_not(takes_late(k)))
            def _():
                far_copy(kind, r, 2, False).start()

        for kind in range(2):
            side_copy(kind, r, 0, core).start()

    def serve(k):
        r = turn(k)
        for j in (1, 3, 2):
            for kind in range(2):
                far_copy(kind, r, j, True).wait_recv()
                side_copy(kind, r, j, core).start()

    lax.fori_loop(0, 3, spread_near, 0)
    def spread_all(k, carry):
        spread_far(k)
        return carry

    lax.fori_loop(0, 3, spread_all, 0)

    scale = jnp.broadcast_to(scale_row[...].astype(jnp.float32), (rows, LANES)).T

    def scale_codes(d, carry):
        stage_copy(d).wait()
        staged[d] = (staged[d].astype(jnp.float32) * scale).astype(jnp.bfloat16)
        return carry

    lax.fori_loop(0, RANKS, scale_codes, 0)
    store_ref[pl.ds(pl.multiple_of(dp * rows, rows), rows), :] = staged[dp]

    for copy in own_copies():
        copy.wait()
    for j in range(1, 4):
        gain_copy(j).wait()

    def send_codes(j, carry):
        code_copy(lax.rem(dp + j, RANKS)).start()
        return carry

    def layer_step(layer, carry):
        r = lax.rem(layer - z + 4, 4)

        @pl.when(layer != z)
        def _():
            for kind in range(2):
                for j in range(SIDE):
                    side_copy(kind, r, j, 1 - core).wait_recv()

        gain = gains[r].astype(jnp.float32)
        squares = jnp.zeros((rows, LANES), jnp.float32)
        for j in range(features // LANES):
            columns = slice(j * LANES, (j + 1) * LANES)
            tile = hidden_ref[:, columns].astype(jnp.float32)
            squares += tile * tile
            normed[:, columns] = (tile * gain[j : j + 1, :]).astype(jnp.bfloat16)
        squares = jnp.broadcast_to(jnp.sum(squares, axis=1, keepdims=True), (rows, LANES))
        products[:, :head] = jnp.dot(
            normed[...], w_value[r].reshape(features, head), preferred_element_type=jnp.float32
        )
        products[:, head:] = squares
        lane = lax.broadcasted_iota(jnp.int32, (quarter, LANES), 1)

        def leave(phase, k, part):
            rows_in = slice(k * half + part * quarter, k * half + (part + 1) * quarter)
            buffer = (out1, out2)[phase]
            squares = products[rows_in, head:]
            high = squares.astype(jnp.bfloat16).astype(jnp.float32)
            buffer[layer, k, part, :, :head] = products[rows_in, :head].astype(jnp.bfloat16)
            buffer[layer, k, part, :, head:] = jnp.where(lane < LANES // 2, high, squares - high).astype(
                jnp.bfloat16
            )
            sum_copy(phase, layer, k, part).start()

        def arrive(phase, k, part):
            rows_in = slice(k * half + part * quarter, k * half + (part + 1) * quarter)
            buffer = (in1, in2)[phase]
            sum_copy(phase, layer, k, part).wait_recv()
            marks = buffer[layer, k, part, :, head:].astype(jnp.float32)
            so_far = products[rows_in, :head] + buffer[layer, k, part, :, :head].astype(jnp.float32)
            return rows_in, so_far, products[rows_in, head:] + marks + pltpu.roll(marks, LANES // 2, 1)

        order = [(k, part) for part in range(4) for k in range(2)]
        for k, part in order:
            leave(0, k, part)
        for k, part in order:
            rows_in, so_far, squares = arrive(0, k, part)
            products[rows_in, :head] = so_far
            products[rows_in, head:] = squares
            leave(1, k, part)

        @pl.when(layer + 1 < z)
        def _():
            serve(layer + 1)

        @pl.when(jnp.logical_and(layer >= z, layer < 3))
        def _():
            serve(layer)

        @pl.when(layer == 2)
        def _():
            lax.fori_loop(1, RANKS, send_codes, 0)

        for k, part in order:
            rows_in, so_far, squares = arrive(1, k, part)
            scale = lax.rsqrt(squares * (1.0 / width) + eps)
            for j in range(head // LANES):
                columns = slice(j * LANES, (j + 1) * LANES)
                values[rows_in, columns] = (so_far[:, columns] * scale).astype(jnp.bfloat16)
        for n in range(features // 512):
            columns = slice(n * 512, (n + 1) * 512)
            branch = jnp.dot(
                values[...],
                w_out[r, :, :, :, :, columns].reshape(head, 512),
                preferred_element_type=jnp.float32,
            )
            hidden_ref[:, columns] = (hidden_ref[:, columns].astype(jnp.float32) + branch).astype(
                jnp.bfloat16
            )
        return carry

    @pl.when(z > 0)
    def _():
        serve(0)

    lax.fori_loop(0, 4, layer_step, 0)

    def sends_out():
        for kind in range(2):
            for j in range(1, 4):
                first_copy(kind, j).wait_send()
                for r in range(1, 4):
                    near_copy(kind, r, j, False).wait_send()
                    if j != 2:
                        far_copy(kind, r, j, False).wait_send()
            for j in (1, 2):

                @pl.when(gives_late(j))
                def _():
                    late_copy(kind, j).wait_send()

            for k in range(3):

                @pl.when(jnp.logical_not(takes_late(k)))
                def _():
                    far_copy(kind, turn(k), 2, False).wait_send()

            for r in range(1, 4):
                for j in range(SIDE):
                    side_copy(kind, r, j, core).wait_send()
        for layer in range(4):
            for k in range(2):
                for part in range(4):
                    for phase in range(2):
                        sum_copy(phase, layer, k, part).wait_send()

    def codes_in():
        def arrive(j, carry):
            code_arrival(lax.rem(dp + j, RANKS)).wait_recv()
            return carry

        lax.fori_loop(1, RANKS, arrive, 0)

    def codes_out():
        def leave(j, carry):
            code_copy(lax.rem(dp + j, RANKS)).wait_send()
            return carry

        lax.fori_loop(1, RANKS, leave, 0)

    return codes_in, codes_out, sends_out


def run_wide(
    inv_root,
    share,
    codes_in,
    codes_out,
    sends_out,
    store_ref,
    perm_ref,
    proj_ref,
    grad_ref,
    loss_ref,
    held,
    squares,
    total,
    rounded,
    rounded_sem,
    y_own,
    y_keep,
    out1,
    in1,
    out2,
    in2,
    rows_g,
    store,
    aim,
    losses,
    ring_send,
    ring_recv,
    side_send,
    side_recv,
    sum1_send,
    sum1_recv,
    sum2_send,
    sum2_recv,
    rows1_send,
    rows1_recv,
    rows2_send,
    rows2_recv,
    loss_send,
    loss_recv,
):
    dp = lax.axis_index("dp")
    z = lax.axis_index("pipe")
    x, y, core = place(dp)
    here = cycle_position(x, y, core)
    after = cycle_device(lax.rem(here + 1, CHIPS), core)
    before = cycle_device(lax.rem(here + CHIPS - 1, CHIPS), core)
    sibling = dp + 1 - 2 * core
    za = z + 1 - 2 * lax.rem(z, 2)
    zb = 3 - z
    steps = CHIPS
    part = held.shape[1] // 4
    block = 4 * part
    half = block // 2
    zpair = (za, zb)
    ring = (after, before)

    sizes = (4, SIDE, 2 * SIDE)
    spots = (z, y, 2 * x + core)

    def peer(group, j):
        spot = lax.rem(spots[group] + j, sizes[group])
        if group == 0:
            return dp, spot
        if group == 1:
            return (x * SIDE + spot) * 2 + core, z
        return ((spot // 2) * SIDE + y) * 2 + lax.rem(spot, 2), z

    mine = pl.multiple_of(core * 2 * part, 2 * part)
    theirs = pl.multiple_of((1 - core) * 2 * part, 2 * part)

    def ring_copy(s, way, sub, later):
        start = mine + way * part + sub * (part // 4)
        rows = pl.ds(pl.multiple_of(start, part // 4), part // 4)
        return pltpu.make_async_remote_copy(
            src_ref=held.at[s, rows],
            dst_ref=held.at[s + later, rows],
            send_sem=ring_send.at[s, way, sub],
            recv_sem=ring_recv.at[s + later, way, sub],
            device_id=(ring[way], z),
            device_id_type=MESH,
        )

    def side_copy(s, start):
        rows = pl.ds(start, 2 * part)
        return pltpu.make_async_remote_copy(
            src_ref=held.at[s, rows],
            dst_ref=held.at[s, rows],
            send_sem=side_send.at[s],
            recv_sem=side_recv.at[s],
            device_id=(sibling, z),
            device_id_type=MESH,
        )

    def sum1_copy(s, k):
        return pltpu.make_async_remote_copy(
            src_ref=out1.at[s, k],
            dst_ref=in1.at[s, k],
            send_sem=sum1_send.at[s, k],
            recv_sem=sum1_recv.at[s, k],
            device_id=(dp, zpair[k]),
            device_id_type=MESH,
        )

    def sum2_copy(s, k):
        return pltpu.make_async_remote_copy(
            src_ref=out2.at[s, k],
            dst_ref=in2.at[s, k],
            send_sem=sum2_send.at[s, k],
            recv_sem=sum2_recv.at[s, k],
            device_id=(dp, zpair[1 - k]),
            device_id_type=MESH,
        )

    def rows1_copy(s, k, quarter):
        return pltpu.make_async_remote_copy(
            src_ref=rows_g.at[s, quarter],
            dst_ref=rows_g.at[s, quarter],
            send_sem=rows1_send.at[s, k],
            recv_sem=rows1_recv.at[s, k],
            device_id=(dp, zpair[k]),
            device_id_type=MESH,
        )

    def rows2_copy(s, k, quarter):
        rows = pl.ds(k * half, half)
        return pltpu.make_async_remote_copy(
            src_ref=rows_g.at[s, quarter, rows],
            dst_ref=rows_g.at[s, quarter, rows],
            send_sem=rows2_send.at[s, k],
            recv_sem=rows2_recv.at[s, k],
            device_id=(dp, zpair[k]),
            device_id_type=MESH,
        )

    def loss_copy(group, j, arrival):
        spot = lax.rem(spots[group] + j, sizes[group]) if arrival else spots[group]
        return pltpu.make_async_remote_copy(
            src_ref=losses.at[group, spot],
            dst_ref=losses.at[group, spot],
            send_sem=loss_send.at[group, j],
            recv_sem=loss_recv.at[group, spot],
            device_id=peer(group, j),
            device_id_type=MESH,
        )

    def loss_out(group):
        losses[group, spots[group]] = squares[...]
        for j in range(1, sizes[group]):
            loss_copy(group, j, False).start()

    def loss_in(group):
        for j in range(1, sizes[group]):
            loss_copy(group, j, True).wait_recv()
        squares[...] = functools.reduce(
            jnp.add, [losses[group, spot] for spot in range(sizes[group])]
        )

    squares[...] = jnp.zeros_like(squares)
    total[...] = jnp.zeros_like(total)

    def pass_on(i, sub):
        @pl.when(jnp.logical_and(i > 0, i < steps))
        def _():
            for way in range(2):
                ring_copy(i, way, sub, 0).wait_recv()

        @pl.when(i < steps - 1)
        def _():
            for way in range(2):
                ring_copy(i, way, sub, 1).start()

    def body(i, carry):
        pass_on(i, 0)

        @pl.when(jnp.logical_and(i >= 1, i < steps + 1))
        def _():
            s = i - 1
            slot = lax.rem(s, 2)
            side_copy(s, theirs).wait_recv()
            for n in range(2):
                part_y = jnp.dot(
                    held[s], proj_ref[:, n * 256 : (n + 1) * 256], preferred_element_type=jnp.float32
                )
                y_own[slot, 2 * n] = part_y[:, :128]
                y_own[slot, 2 * n + 1] = part_y[:, 128:]
            for k in range(2):
                rows = pl.ds(k * half, half)
                other = 3 - zpair[k] if k == 0 else zpair[k] + 1 - 2 * lax.rem(zpair[k], 2)
                out1[s, k, 0] = y_own[slot, zpair[k], rows, :].astype(jnp.bfloat16)
                out1[s, k, 1] = y_own[slot, other, rows, :].astype(jnp.bfloat16)
                sum1_copy(s, k).start()

        pass_on(i, 1)

        @pl.when(i == 4)
        def _():
            codes_in()
            store[...] = store_ref[...].astype(jnp.float32)

        @pl.when(jnp.logical_and(i >= 4, i < steps + 4))
        def _():
            s = i - 4
            slot = lax.rem(s, 2)
            for k in range(2):
                sum2_copy(s, k).wait_recv()
            for chunk in range(4):
                ring_core, way = chunk // 2, chunk % 2
                at = cycle_position(x, y, ring_core)
                origin = cycle_device(lax.rem(at + (CHIPS - s if way == 0 else s), CHIPS), ring_core)
                token = pl.multiple_of((origin * 2 + way) * part, part)
                rows = pl.ds(chunk * part, part)
                inside = pl.ds((chunk % 2) * part, part)

                def seek(group, carry):
                    for j in range(8):
                        at_row = group * 8 + j
                        aim[pl.ds(chunk * part + at_row, 1), :] = store[
                            pl.ds(perm_ref[token + at_row], 1), :
                        ]
                    return carry

                lax.fori_loop(0, part // 8, seek, 0)
                diff = (
                    y_keep[slot, rows, :]
                    + in2[s, chunk // 2, inside, :].astype(jnp.float32)
                    - aim[rows, :]
                )
                rows_g[s, z, rows, :] = (diff * inv_root).astype(jnp.bfloat16)
                squares[...] += jnp.sum((diff * diff).reshape(part // 8, 8, diff.shape[1]), axis=0)
            for k in range(2):
                rows1_copy(s, k, z).start()

        pass_on(i, 2)

        @pl.when(jnp.logical_and(i >= 2, i < steps + 2))
        def _():
            s = i - 2
            slot = lax.rem(s, 2)
            for k in range(2):
                rows = pl.ds(k * half, half)
                sum1_copy(s, k).wait_recv()
                passed = y_own[slot, zpair[1 - k], rows, :] + in1[s, k, 1].astype(jnp.float32)
                out2[s, k] = passed.astype(jnp.bfloat16)
                sum2_copy(s, k).start()
                y_keep[slot, rows, :] = y_own[slot, z, rows, :] + in1[s, k, 0].astype(jnp.float32)

        @pl.when(jnp.logical_and(i >= 5, i < steps + 5))
        def _():
            s = i - 5
            for k in range(2):
                rows1_copy(s, k, zpair[k]).wait_recv()
            for k in range(2):
                rows2_copy(s, k, zpair[1 - k]).start()

        pass_on(i, 3)

        @pl.when(i < steps)
        def _():
            side_copy(i, mine).start()

        @pl.when(i == steps + 3)
        def _():
            loss_out(0)

        @pl.when(i == steps + 4)
        def _():
            loss_in(0)
            loss_out(1)

        @pl.when(i == steps + 5)
        def _():
            loss_in(1)
            loss_out(2)

        @pl.when(i >= 6)
        def _():
            s = i - 6
            for k in range(2):
                rows2_copy(s, k, 3 - zpair[k] if k == 0 else zpair[k] + 1 - 2 * lax.rem(zpair[k], 2)).wait_recv()
            rows = jnp.concatenate([rows_g[s, q] for q in range(4)], axis=1)
            for f in range(8):
                features = slice(f * 256, (f + 1) * 256)
                total[features, :] += lax.dot_general(
                    held[s, :, features], rows, (((0,), (0,)), ((), ())), preferred_element_type=jnp.float32
                )

            @pl.when(s < steps - 1)
            def _():
                for way in range(2):
                    for sub in range(4):
                        ring_copy(s, way, sub, 1).wait_send()

            side_copy(s, mine).wait_send()
            for k in range(2):
                sum1_copy(s, k).wait_send()
                sum2_copy(s, k).wait_send()
                rows1_copy(s, k, z).wait_send()
                rows2_copy(s, k, zpair[1 - k]).wait_send()

        @pl.when(i == 8)
        def _():
            sends_out()

        @pl.when(i == 10)
        def _():
            codes_out()

        return carry

    lax.fori_loop(0, steps + 6, body, 0)

    def piece_out(f):
        rows = pl.ds(f * 256, 256)
        return pltpu.make_async_copy(rounded.at[rows], grad_ref.at[rows], rounded_sem.at[f])

    for f in range(8):
        rounded[f * 256 : (f + 1) * 256, :] = total[f * 256 : (f + 1) * 256, :].astype(jnp.bfloat16)
        piece_out(f).start()
    loss_in(2)
    for group in range(3):
        for j in range(1, sizes[group]):
            loss_copy(group, j, False).wait_send()
    loss_ref[0, 0] = jnp.sum(squares[...]) * share
    for f in range(8):
        piece_out(f).wait()


LAYER_SCRATCH = 33


def kernel(
    eps,
    inv_root,
    share,
    h_ref,
    value_ref,
    out_ref,
    gain_ref,
    proj_ref,
    codes_ref,
    scale_ref,
    perm_ref,
    grad_ref,
    loss_ref,
    held,
    store_ref,
    proj,
    proj_sem,
    *scratch,
):
    core = lax.rem(lax.axis_index("dp"), 2)
    rows = held.shape[1] // 2
    fetch_proj = pltpu.make_async_copy(proj_ref, proj, proj_sem)
    fetch_proj.start()
    codes_in, codes_out, sends_out = run_layers(
        eps,
        h_ref,
        value_ref,
        out_ref,
        gain_ref,
        codes_ref,
        scale_ref,
        held.at[0, pl.ds(pl.multiple_of(core * rows, rows), rows)],
        store_ref,
        *scratch[:LAYER_SCRATCH],
    )
    fetch_proj.wait()
    run_wide(
        inv_root,
        share,
        codes_in,
        codes_out,
        sends_out,
        store_ref,
        perm_ref,
        proj,
        grad_ref,
        loss_ref,
        held,
        *scratch[LAYER_SCRATCH:],
    )


def distill(hidden, value_weight, folded_out, gain, proj, codes, scales, perm):
    rows, features = hidden.shape
    head = value_weight.shape[1]
    columns = proj.shape[1]
    quarter = columns // 4
    tokens = rows * RANKS
    block = 2 * rows
    wide_half = block // 2
    grid = (4, SIDE, SIDE, 2)
    value_weight = value_weight.reshape(*grid, features // RANKS, head)
    folded_out = folded_out.reshape(*grid[1:], head // RANKS, 4 * features)
    bf16, f32 = jnp.bfloat16, jnp.float32
    dma = pltpu.SemaphoreType.DMA
    message = pltpu.VMEM((4, 2, 4, rows // 8, head + LANES), bf16)
    lanes = (features // LANES, LANES)
    layer_scratch = [
        pltpu.VMEM((*grid, features // RANKS, head), bf16),
        pltpu.VMEM((*grid, head // RANKS, features), bf16),
        pltpu.VMEM(gain.shape, bf16),
        pltpu.VMEM((4, *lanes), bf16),
        pltpu.VMEM((4, *lanes), bf16),
        pltpu.VMEM(scales.shape, bf16),
        pltpu.VMEM((rows, head + LANES), f32),
        pltpu.VMEM((rows, features), bf16),
        pltpu.VMEM((rows, head), bf16),
        message,
        message,
        message,
        message,
        pltpu.VMEM((RANKS, rows, LANES), bf16),
        dma((5,)),
        *[dma((2, 3))] * 3,
        *[dma((2, 3, SIDE))] * 6,
        dma((3,)),
        dma((3,)),
        *[dma((4, 2, 4))] * 4,
        *[dma((RANKS,))] * 3,
    ]
    wide_scratch = [
        pltpu.VMEM((8, quarter), f32),
        pltpu.VMEM((features, columns), f32),
        pltpu.VMEM((features, columns), bf16),
        dma((8,)),
        pltpu.VMEM((2, 4, block, quarter), f32),
        pltpu.VMEM((2, block, quarter), f32),
        pltpu.VMEM((CHIPS, 2, 2, wide_half, quarter), bf16),
        pltpu.VMEM((CHIPS, 2, 2, wide_half, quarter), bf16),
        pltpu.VMEM((CHIPS, 2, wide_half, quarter), bf16),
        pltpu.VMEM((CHIPS, 2, wide_half, quarter), bf16),
        pltpu.VMEM((CHIPS, 4, block, quarter), bf16),
        pltpu.VMEM((tokens, LANES), f32),
        pltpu.VMEM((block, quarter), f32),
        pltpu.VMEM((3, 2 * SIDE, 8, quarter), f32),
        dma((CHIPS, 2, 4)),
        dma((CHIPS, 2, 4)),
        dma((CHIPS,)),
        dma((CHIPS,)),
        dma((CHIPS, 2)),
        dma((CHIPS, 2)),
        dma((CHIPS, 2)),
        dma((CHIPS, 2)),
        dma((CHIPS, 2)),
        dma((CHIPS, 2)),
        dma((CHIPS, 2)),
        dma((CHIPS, 2)),
        dma((3, 2 * SIDE)),
        dma((3, 2 * SIDE)),
    ]
    smem = pl.BlockSpec(memory_space=pltpu.SMEM)
    anywhere = pl.BlockSpec(memory_space=pl.ANY)
    return pl.pallas_call(
        functools.partial(kernel, 1e-5, 1.0 / math.sqrt(tokens), 0.5 / (tokens * columns * RANKS)),
        out_shape=(
            jax.ShapeDtypeStruct((features, columns), bf16),
            jax.ShapeDtypeStruct((1, 1), f32),
        ),
        in_specs=[anywhere] * 7 + [smem],
        out_specs=(anywhere, smem),
        scratch_shapes=[
            pltpu.VMEM((CHIPS, block, features), bf16),
            pltpu.VMEM((tokens, LANES), bf16),
            pltpu.VMEM(proj.shape, bf16),
            dma,
        ]
        + layer_scratch
        + wide_scratch,
        compiler_params=pltpu.CompilerParams(
            collective_id=0, has_side_effects=True, vmem_limit_bytes=63 * 1024 * 1024
        ),
    )(hidden, value_weight, folded_out, gain, proj, codes, scales, perm)


def shards(
    student_in, value_weight, folded_out, norm_gain, proj, teacher_codes, teacher_scales, perm
):
    grad_proj, loss = distill(
        student_in,
        value_weight[0],
        folded_out[0],
        norm_gain,
        proj,
        teacher_codes,
        teacher_scales[None, :],
        perm,
    )
    return (grad_proj, loss[0, 0])


def solution(mesh):
    return jax.shard_map(
        shards,
        mesh=mesh,
        in_specs=(
            P("dp", "pipe"),
            P("pipe", None, None),
            P("pipe", None, None),
            P("pipe", None),
            P("pipe", "dp"),
            P("dp", None),
            P("dp"),
            P(),
        ),
        out_specs=(P("pipe", "dp"), P()),
        check_vma=False,
    )
```

```python
import functools
import math

import jax
import jax.numpy as jnp
from jax import lax
from jax.experimental import pallas as pl
from jax.experimental.pallas import tpu as pltpu
from jax.sharding import PartitionSpec as P

MESH = pl.DeviceIdType.MESH
SIDE = 4
CHIPS = SIDE * SIDE
RANKS = 2 * CHIPS
LANES = 128


def place(dp):
    core = lax.rem(dp, 2)
    chip = dp // 2
    return chip // SIDE, lax.rem(chip, SIDE), core


def cycle_position(x, y, core):
    return SIDE * (y + core * (x - y)) + lax.rem(x + y, SIDE)


def cycle_device(position, core):
    major = position // SIDE
    minor = lax.rem(lax.rem(position, SIDE) - major + SIDE, SIDE)
    x = minor + core * (major - minor)
    y = major + core * (minor - major)
    return (x * SIDE + y) * 2 + core


def run_layers(
    eps,
    h_ref,
    value_ref,
    out_ref,
    gain_ref,
    codes_ref,
    scale_ref,
    hidden_ref,
    store_ref,
    w_value,
    w_out,
    gain_row,
    gain_own,
    gains,
    scale_row,
    products,
    normed,
    values,
    out1,
    in1,
    out2,
    in2,
    staged,
    own_sem,
    first_send,
    first_recv,
    late_send,
    near_send,
    near_recv,
    far_send,
    far_recv,
    side_send,
    side_recv,
    gain_send,
    gain_recv,
    sum1_send,
    sum1_recv,
    sum2_send,
    sum2_recv,
    stage_sem,
    code_send,
    code_recv,
):
    dp = lax.axis_index("dp")
    z = lax.axis_index("pipe")
    x, y, core = place(dp)
    sibling = dp + 1 - 2 * core
    zpair = (z + 1 - 2 * lax.rem(z, 2), 3 - z)
    rows, features = hidden_ref.shape
    head = value_ref.shape[-1]
    half = rows // 2
    quarter = rows // 8
    weights = (w_value, w_out)
    width = 4 * features

    def greet_all():
        barrier = pltpu.get_barrier_semaphore()

        def greet(j, carry):
            pl.semaphore_signal(
                barrier, inc=1, device_id=(lax.rem(dp + j, RANKS), z), device_id_type=MESH
            )
            return carry

        lax.fori_loop(1, RANKS, greet, 0)
        for j in range(1, 4):
            pl.semaphore_signal(
                barrier, inc=1, device_id=(dp, lax.rem(z + j, 4)), device_id_type=MESH
            )
        pl.semaphore_wait(barrier, RANKS + 2)

    def first_copy(kind, j):
        to = lax.rem(z + j, 4)
        if kind == 0:
            source = value_ref.at[to, x, y, core]
        else:
            source = out_ref.at[x, y, core, :, pl.ds(pl.multiple_of(to * features, features), features)]
        return pltpu.make_async_remote_copy(
            src_ref=source,
            dst_ref=weights[kind].at[4 - j, x, y, core],
            send_sem=first_send.at[kind, j - 1],
            recv_sem=first_recv.at[kind, 3 - j],
            device_id=(dp, to),
            device_id_type=MESH,
        )

    def first_arrival(kind, r):
        block = weights[kind].at[r, x, y, core]
        return pltpu.make_async_remote_copy(
            src_ref=block,
            dst_ref=block,
            send_sem=first_send.at[kind, r - 1],
            recv_sem=first_recv.at[kind, r - 1],
            device_id=(dp, lax.rem(z + r, 4)),
            device_id_type=MESH,
        )

    spot = (x, y)

    def near_copy(kind, r, j, arrival):
        there = lax.rem(spot[kind] + j, SIDE)
        at = there if arrival else spot[kind]
        block = w_value.at[r, at, y, core] if kind == 0 else w_out.at[r, x, at, core]
        chip = there * SIDE + y if kind == 0 else x * SIDE + there
        return pltpu.make_async_remote_copy(
            src_ref=block,
            dst_ref=block,
            send_sem=near_send.at[kind, r - 1, j],
            recv_sem=near_recv.at[kind, r - 1, at],
            device_id=(chip * 2 + core, z),
            device_id_type=MESH,
        )

    def far_copy(kind, r, j, arrival):
        there = lax.rem(spot[1 - kind] + j, SIDE)
        at = there if arrival else spot[1 - kind]
        block = w_value.at[r, :, at, core] if kind == 0 else w_out.at[r, at, :, core]
        chip = there * SIDE + y if kind == 1 else x * SIDE + there
        return pltpu.make_async_remote_copy(
            src_ref=block,
            dst_ref=block,
            send_sem=far_send.at[kind, r - 1, j],
            recv_sem=far_recv.at[kind, r - 1, at],
            device_id=(chip * 2 + core, z),
            device_id_type=MESH,
        )

    def late_copy(kind, j):
        to = lax.rem(z + j, 4)
        at = lax.rem(spot[1 - kind] + 2, SIDE)
        if kind == 0:
            source = value_ref.at[to, :, at, core]
            target = w_value.at[4 - j, :, at, core]
        else:
            source = out_ref.at[at, :, core, :, pl.ds(pl.multiple_of(to * features, features), features)]
            target = w_out.at[4 - j, at, :, core]
        return pltpu.make_async_remote_copy(
            src_ref=source,
            dst_ref=target,
            send_sem=late_send.at[kind, j - 1],
            recv_sem=far_recv.at[kind, 3 - j, at],
            device_id=(dp, to),
            device_id_type=MESH,
        )

    def gives_late(j):
        return jnp.logical_and(z >= 1, z < lax.rem(z + j, 4))

    def takes_late(k):
        return jnp.logical_and(k >= 1, k < z)

    def side_copy(kind, r, j, owner):
        at = lax.rem(spot[1 - kind] + j, SIDE)
        block = w_value.at[r, :, at, owner] if kind == 0 else w_out.at[r, at, :, owner]
        return pltpu.make_async_remote_copy(
            src_ref=block,
            dst_ref=block,
            send_sem=side_send.at[kind, r - 1, at],
            recv_sem=side_recv.at[kind, r - 1, at],
            device_id=(sibling, z),
            device_id_type=MESH,
        )

    def gain_copy(j):
        to = lax.rem(z + j, 4)
        return pltpu.make_async_remote_copy(
            src_ref=gain_own.at[to],
            dst_ref=gains.at[4 - j],
            send_sem=gain_send.at[j - 1],
            recv_sem=gain_recv.at[3 - j],
            device_id=(dp, to),
            device_id_type=MESH,
        )

    def own_copies():
        columns = pl.ds(pl.multiple_of(z * features, features), features)
        return (
            pltpu.make_async_copy(value_ref.at[z], w_value.at[0], own_sem.at[0]),
            pltpu.make_async_copy(out_ref.at[:, :, :, :, columns], w_out.at[0], own_sem.at[1]),
        )

    def stage_copy(d):
        columns = pl.ds(pl.multiple_of((d * 4 + z) * LANES, LANES), LANES)
        return pltpu.make_async_copy(codes_ref.at[:, columns], staged.at[d], stage_sem.at[d])

    def code_copy(d):
        return pltpu.make_async_remote_copy(
            src_ref=staged.at[d],
            dst_ref=store_ref.at[pl.ds(pl.multiple_of(dp * rows, rows), rows)],
            send_sem=code_send.at[d],
            recv_sem=code_recv.at[dp],
            device_id=(d, z),
            device_id_type=MESH,
        )

    def code_arrival(d):
        block = store_ref.at[pl.ds(pl.multiple_of(d * rows, rows), rows)]
        return pltpu.make_async_remote_copy(
            src_ref=block,
            dst_ref=block,
            send_sem=code_send.at[d],
            recv_sem=code_recv.at[d],
            device_id=(d, z),
            device_id_type=MESH,
        )

    def sum_copy(phase, layer, k, part):
        source, target, send, recv = (
            (out1, in1, sum1_send, sum1_recv),
            (out2, in2, sum2_send, sum2_recv),
        )[phase]
        return pltpu.make_async_remote_copy(
            src_ref=source.at[layer, k, part],
            dst_ref=target.at[layer, k, part],
            send_sem=send.at[layer, k, part],
            recv_sem=recv.at[layer, k, part],
            device_id=(dp, zpair[k ^ phase]),
            device_id_type=MESH,
        )

    small = (
        pltpu.make_async_copy(gain_ref, gain_row, own_sem.at[2]),
        pltpu.make_async_copy(scale_ref, scale_row, own_sem.at[3]),
        pltpu.make_async_copy(h_ref, hidden_ref, own_sem.at[4]),
    )
    for copy in small:
        copy.start()
    greet_all()
    for j in (1, 3, 2):
        first_copy(0, j).start()
        first_copy(1, j).start()
    for j in (1, 2):

        @pl.when(gives_late(j))
        def _():
            for kind in range(2):
                late_copy(kind, j).start()

    for copy in own_copies():
        copy.start()

    def fetch(d, carry):
        stage_copy(d).start()
        return carry

    lax.fori_loop(0, RANKS, fetch, 0)
    for copy in small:
        copy.wait()
    for part in range(4):
        for j in range(features // LANES):
            at = part * features + j * LANES
            gain_own[part, j : j + 1, :] = gain_row[:, at : at + LANES]
    for j in range(1, 4):
        gain_copy(j).start()
    gains[0] = gain_own[z]
    def turn(k):
        layer = k + jnp.where(k >= z, 1, 0)
        return lax.rem(layer - z + 4, 4)

    def spread_near(k, carry):
        r = turn(k)
        for kind in range(2):
            first_arrival(kind, r).wait_recv()
            for j in (1, 3, 2):
                near_copy(kind, r, j, False).start()
        return carry

    def spread_far(k):
        r = turn(k)
        for kind in range(2):
            for j in (1, 3, 2):
                near_copy(kind, r, j, True).wait_recv()
            for j in (1, 3):
                far_copy(kind, r, j, False).start()

            @pl.when(jnp.logical_not(takes_late(k)))
            def _():
                far_copy(kind, r, 2, False).start()

        for kind in range(2):
            side_copy(kind, r, 0, core).start()

    def serve(k):
        r = turn(k)
        for j in (1, 3, 2):
            for kind in range(2):
                far_copy(kind, r, j, True).wait_recv()
                side_copy(kind, r, j, core).start()

    lax.fori_loop(0, 3, spread_near, 0)
    def spread_all(k, carry):
        spread_far(k)
        return carry

    lax.fori_loop(0, 3, spread_all, 0)

    scale = jnp.broadcast_to(scale_row[...].astype(jnp.float32), (rows, LANES)).T

    def scale_codes(d, carry):
        stage_copy(d).wait()
        staged[d] = (staged[d].astype(jnp.float32) * scale).astype(jnp.bfloat16)
        return carry

    lax.fori_loop(0, RANKS, scale_codes, 0)
    store_ref[pl.ds(pl.multiple_of(dp * rows, rows), rows), :] = staged[dp]

    for copy in own_copies():
        copy.wait()
    for j in range(1, 4):
        gain_copy(j).wait()

    def send_codes(j, carry):
        code_copy(lax.rem(dp + j, RANKS)).start()
        return carry

    def layer_step(layer, carry):
        r = lax.rem(layer - z + 4, 4)

        @pl.when(layer != z)
        def _():
            for kind in range(2):
                for j in range(SIDE):
                    side_copy(kind, r, j, 1 - core).wait_recv()

        gain = gains[r].astype(jnp.float32)
        squares = jnp.zeros((rows, LANES), jnp.float32)
        for j in range(features // LANES):
            columns = slice(j * LANES, (j + 1) * LANES)
            tile = hidden_ref[:, columns].astype(jnp.float32)
            squares += tile * tile
            normed[:, columns] = (tile * gain[j : j + 1, :]).astype(jnp.bfloat16)
        squares = jnp.broadcast_to(jnp.sum(squares, axis=1, keepdims=True), (rows, LANES))
        products[:, :head] = jnp.dot(
            normed[...], w_value[r].reshape(features, head), preferred_element_type=jnp.float32
        )
        products[:, head:] = squares
        lane = lax.broadcasted_iota(jnp.int32, (quarter, LANES), 1)

        def leave(phase, k, part):
            rows_in = slice(k * half + part * quarter, k * half + (part + 1) * quarter)
            buffer = (out1, out2)[phase]
            squares = products[rows_in, head:]
            high = squares.astype(jnp.bfloat16).astype(jnp.float32)
            buffer[layer, k, part, :, :head] = products[rows_in, :head].astype(jnp.bfloat16)
            buffer[layer, k, part, :, head:] = jnp.where(lane < LANES // 2, high, squares - high).astype(
                jnp.bfloat16
            )
            sum_copy(phase, layer, k, part).start()

        def arrive(phase, k, part):
            rows_in = slice(k * half + part * quarter, k * half + (part + 1) * quarter)
            buffer = (in1, in2)[phase]
            sum_copy(phase, layer, k, part).wait_recv()
            marks = buffer[layer, k, part, :, head:].astype(jnp.float32)
            so_far = products[rows_in, :head] + buffer[layer, k, part, :, :head].astype(jnp.float32)
            return rows_in, so_far, products[rows_in, head:] + marks + pltpu.roll(marks, LANES // 2, 1)

        order = [(k, part) for part in range(4) for k in range(2)]
        for k, part in order:
            leave(0, k, part)

        @pl.when(layer == 2)
        def _():
            lax.fori_loop(1, CHIPS, send_codes, 0)

        for k, part in order:
            rows_in, so_far, squares = arrive(0, k, part)
            products[rows_in, :head] = so_far
            products[rows_in, head:] = squares
            leave(1, k, part)

        @pl.when(layer + 1 < z)
        def _():
            serve(layer + 1)

        @pl.when(jnp.logical_and(layer >= z, layer < 3))
        def _():
            serve(layer)

        @pl.when(layer == 2)
        def _():
            lax.fori_loop(CHIPS, RANKS, send_codes, 0)

        for k, part in order:
            rows_in, so_far, squares = arrive(1, k, part)
            scale = lax.rsqrt(squares * (1.0 / width) + eps)
            for j in range(head // LANES):
                columns = slice(j * LANES, (j + 1) * LANES)
                values[rows_in, columns] = (so_far[:, columns] * scale).astype(jnp.bfloat16)
        for n in range(features // 512):
            columns = slice(n * 512, (n + 1) * 512)
            branch = jnp.dot(
                values[...],
                w_out[r, :, :, :, :, columns].reshape(head, 512),
                preferred_element_type=jnp.float32,
            )
            hidden_ref[:, columns] = (hidden_ref[:, columns].astype(jnp.float32) + branch).astype(
                jnp.bfloat16
            )
        return carry

    @pl.when(z > 0)
    def _():
        serve(0)

    lax.fori_loop(0, 4, layer_step, 0)

    def sends_out():
        for kind in range(2):
            for j in range(1, 4):
                first_copy(kind, j).wait_send()
                for r in range(1, 4):
                    near_copy(kind, r, j, False).wait_send()
                    if j != 2:
                        far_copy(kind, r, j, False).wait_send()
            for j in (1, 2):

                @pl.when(gives_late(j))
                def _():
                    late_copy(kind, j).wait_send()

            for k in range(3):

                @pl.when(jnp.logical_not(takes_late(k)))
                def _():
                    far_copy(kind, turn(k), 2, False).wait_send()

            for r in range(1, 4):
                for j in range(SIDE):
                    side_copy(kind, r, j, core).wait_send()
        for layer in range(4):
            for k in range(2):
                for part in range(4):
                    for phase in range(2):
                        sum_copy(phase, layer, k, part).wait_send()

    def codes_in():
        def arrive(j, carry):
            code_arrival(lax.rem(dp + j, RANKS)).wait_recv()
            return carry

        lax.fori_loop(1, RANKS, arrive, 0)

    def codes_out():
        def leave(j, carry):
            code_copy(lax.rem(dp + j, RANKS)).wait_send()
            return carry

        lax.fori_loop(1, RANKS, leave, 0)

    return codes_in, codes_out, sends_out


def run_wide(
    inv_root,
    share,
    codes_in,
    codes_out,
    sends_out,
    store_ref,
    perm_ref,
    proj_ref,
    grad_ref,
    loss_ref,
    held,
    squares,
    total,
    rounded,
    rounded_sem,
    y_own,
    y_keep,
    out1,
    in1,
    out2,
    in2,
    rows_g,
    store,
    aim,
    losses,
    ring_send,
    ring_recv,
    side_send,
    side_recv,
    sum1_send,
    sum1_recv,
    sum2_send,
    sum2_recv,
    rows1_send,
    rows1_recv,
    rows2_send,
    rows2_recv,
    loss_send,
    loss_recv,
):
    dp = lax.axis_index("dp")
    z = lax.axis_index("pipe")
    x, y, core = place(dp)
    here = cycle_position(x, y, core)
    after = cycle_device(lax.rem(here + 1, CHIPS), core)
    before = cycle_device(lax.rem(here + CHIPS - 1, CHIPS), core)
    sibling = dp + 1 - 2 * core
    za = z + 1 - 2 * lax.rem(z, 2)
    zb = 3 - z
    steps = CHIPS
    part = held.shape[1] // 4
    block = 4 * part
    half = block // 2
    zpair = (za, zb)
    ring = (after, before)

    sizes = (4, SIDE, 2 * SIDE)
    spots = (z, y, 2 * x + core)

    def peer(group, j):
        spot = lax.rem(spots[group] + j, sizes[group])
        if group == 0:
            return dp, spot
        if group == 1:
            return (x * SIDE + spot) * 2 + core, z
        return ((spot // 2) * SIDE + y) * 2 + lax.rem(spot, 2), z

    mine = pl.multiple_of(core * 2 * part, 2 * part)
    theirs = pl.multiple_of((1 - core) * 2 * part, 2 * part)

    def ring_copy(s, way, sub, later):
        start = mine + way * part + sub * (part // 4)
        rows = pl.ds(pl.multiple_of(start, part // 4), part // 4)
        return pltpu.make_async_remote_copy(
            src_ref=held.at[s, rows],
            dst_ref=held.at[s + later, rows],
            send_sem=ring_send.at[s, way, sub],
            recv_sem=ring_recv.at[s + later, way, sub],
            device_id=(ring[way], z),
            device_id_type=MESH,
        )

    def side_copy(s, start):
        rows = pl.ds(start, 2 * part)
        return pltpu.make_async_remote_copy(
            src_ref=held.at[s, rows],
            dst_ref=held.at[s, rows],
            send_sem=side_send.at[s],
            recv_sem=side_recv.at[s],
            device_id=(sibling, z),
            device_id_type=MESH,
        )

    def sum1_copy(s, k):
        return pltpu.make_async_remote_copy(
            src_ref=out1.at[s, k],
            dst_ref=in1.at[s, k],
            send_sem=sum1_send.at[s, k],
            recv_sem=sum1_recv.at[s, k],
            device_id=(dp, zpair[k]),
            device_id_type=MESH,
        )

    def sum2_copy(s, k):
        return pltpu.make_async_remote_copy(
            src_ref=out2.at[s, k],
            dst_ref=in2.at[s, k],
            send_sem=sum2_send.at[s, k],
            recv_sem=sum2_recv.at[s, k],
            device_id=(dp, zpair[1 - k]),
            device_id_type=MESH,
        )

    def rows1_copy(s, k, quarter):
        return pltpu.make_async_remote_copy(
            src_ref=rows_g.at[s, quarter],
            dst_ref=rows_g.at[s, quarter],
            send_sem=rows1_send.at[s, k],
            recv_sem=rows1_recv.at[s, k],
            device_id=(dp, zpair[k]),
            device_id_type=MESH,
        )

    def rows2_copy(s, k, quarter):
        rows = pl.ds(k * half, half)
        return pltpu.make_async_remote_copy(
            src_ref=rows_g.at[s, quarter, rows],
            dst_ref=rows_g.at[s, quarter, rows],
            send_sem=rows2_send.at[s, k],
            recv_sem=rows2_recv.at[s, k],
            device_id=(dp, zpair[k]),
            device_id_type=MESH,
        )

    def loss_copy(group, j, arrival):
        spot = lax.rem(spots[group] + j, sizes[group]) if arrival else spots[group]
        return pltpu.make_async_remote_copy(
            src_ref=losses.at[group, spot],
            dst_ref=losses.at[group, spot],
            send_sem=loss_send.at[group, j],
            recv_sem=loss_recv.at[group, spot],
            device_id=peer(group, j),
            device_id_type=MESH,
        )

    def loss_out(group):
        losses[group, spots[group]] = squares[...]
        for j in range(1, sizes[group]):
            loss_copy(group, j, False).start()

    def loss_in(group):
        for j in range(1, sizes[group]):
            loss_copy(group, j, True).wait_recv()
        squares[...] = functools.reduce(
            jnp.add, [losses[group, spot] for spot in range(sizes[group])]
        )

    squares[...] = jnp.zeros_like(squares)
    total[...] = jnp.zeros_like(total)

    def pass_on(i, sub):
        @pl.when(jnp.logical_and(i > 0, i < steps))
        def _():
            for way in range(2):
                ring_copy(i, way, sub, 0).wait_recv()

        @pl.when(i < steps - 1)
        def _():
            for way in range(2):
                ring_copy(i, way, sub, 1).start()

    def body(i, carry):
        pass_on(i, 0)

        @pl.when(jnp.logical_and(i >= 1, i < steps + 1))
        def _():
            s = i - 1
            slot = lax.rem(s, 2)
            side_copy(s, theirs).wait_recv()
            for n in range(2):
                part_y = jnp.dot(
                    held[s], proj_ref[:, n * 256 : (n + 1) * 256], preferred_element_type=jnp.float32
                )
                y_own[slot, 2 * n] = part_y[:, :128]
                y_own[slot, 2 * n + 1] = part_y[:, 128:]
            for k in range(2):
                rows = pl.ds(k * half, half)
                other = 3 - zpair[k] if k == 0 else zpair[k] + 1 - 2 * lax.rem(zpair[k], 2)
                out1[s, k, 0] = y_own[slot, zpair[k], rows, :].astype(jnp.bfloat16)
                out1[s, k, 1] = y_own[slot, other, rows, :].astype(jnp.bfloat16)
                sum1_copy(s, k).start()

        pass_on(i, 1)

        @pl.when(i == 4)
        def _():
            codes_in()
            store[...] = store_ref[...].astype(jnp.float32)

        @pl.when(jnp.logical_and(i >= 4, i < steps + 4))
        def _():
            s = i - 4
            slot = lax.rem(s, 2)
            for k in range(2):
                sum2_copy(s, k).wait_recv()
            for chunk in range(4):
                ring_core, way = chunk // 2, chunk % 2
                at = cycle_position(x, y, ring_core)
                origin = cycle_device(lax.rem(at + (CHIPS - s if way == 0 else s), CHIPS), ring_core)
                token = pl.multiple_of((origin * 2 + way) * part, part)
                rows = pl.ds(chunk * part, part)
                inside = pl.ds((chunk % 2) * part, part)

                def seek(group, carry):
                    for j in range(8):
                        at_row = group * 8 + j
                        aim[pl.ds(chunk * part + at_row, 1), :] = store[
                            pl.ds(perm_ref[token + at_row], 1), :
                        ]
                    return carry

                lax.fori_loop(0, part // 8, seek, 0)
                diff = (
                    y_keep[slot, rows, :]
                    + in2[s, chunk // 2, inside, :].astype(jnp.float32)
                    - aim[rows, :]
                )
                rows_g[s, z, rows, :] = (diff * inv_root).astype(jnp.bfloat16)
                squares[...] += jnp.sum((diff * diff).reshape(part // 8, 8, diff.shape[1]), axis=0)
            for k in range(2):
                rows1_copy(s, k, z).start()

        pass_on(i, 2)

        @pl.when(jnp.logical_and(i >= 2, i < steps + 2))
        def _():
            s = i - 2
            slot = lax.rem(s, 2)
            for k in range(2):
                rows = pl.ds(k * half, half)
                sum1_copy(s, k).wait_recv()
                passed = y_own[slot, zpair[1 - k], rows, :] + in1[s, k, 1].astype(jnp.float32)
                out2[s, k] = passed.astype(jnp.bfloat16)
                sum2_copy(s, k).start()
                y_keep[slot, rows, :] = y_own[slot, z, rows, :] + in1[s, k, 0].astype(jnp.float32)

        @pl.when(jnp.logical_and(i >= 5, i < steps + 5))
        def _():
            s = i - 5
            for k in range(2):
                rows1_copy(s, k, zpair[k]).wait_recv()
            for k in range(2):
                rows2_copy(s, k, zpair[1 - k]).start()

        pass_on(i, 3)

        @pl.when(i < steps)
        def _():
            side_copy(i, mine).start()

        @pl.when(i == steps + 3)
        def _():
            loss_out(0)

        @pl.when(i == steps + 4)
        def _():
            loss_in(0)
            loss_out(1)

        @pl.when(i == steps + 5)
        def _():
            loss_in(1)
            loss_out(2)

        @pl.when(i >= 6)
        def _():
            s = i - 6
            for k in range(2):
                rows2_copy(s, k, 3 - zpair[k] if k == 0 else zpair[k] + 1 - 2 * lax.rem(zpair[k], 2)).wait_recv()
            rows = jnp.concatenate([rows_g[s, q] for q in range(4)], axis=1)
            for f in range(8):
                features = slice(f * 256, (f + 1) * 256)
                total[features, :] += lax.dot_general(
                    held[s, :, features], rows, (((0,), (0,)), ((), ())), preferred_element_type=jnp.float32
                )

            @pl.when(s < steps - 1)
            def _():
                for way in range(2):
                    for sub in range(4):
                        ring_copy(s, way, sub, 1).wait_send()

            side_copy(s, mine).wait_send()
            for k in range(2):
                sum1_copy(s, k).wait_send()
                sum2_copy(s, k).wait_send()
                rows1_copy(s, k, z).wait_send()
                rows2_copy(s, k, zpair[1 - k]).wait_send()

        @pl.when(i == 8)
        def _():
            sends_out()

        @pl.when(i == 10)
        def _():
            codes_out()

        return carry

    lax.fori_loop(0, steps + 6, body, 0)

    def piece_out(f):
        rows = pl.ds(f * 256, 256)
        return pltpu.make_async_copy(rounded.at[rows], grad_ref.at[rows], rounded_sem.at[f])

    for f in range(8):
        rounded[f * 256 : (f + 1) * 256, :] = total[f * 256 : (f + 1) * 256, :].astype(jnp.bfloat16)
        piece_out(f).start()
    loss_in(2)
    for group in range(3):
        for j in range(1, sizes[group]):
            loss_copy(group, j, False).wait_send()
    loss_ref[0, 0] = jnp.sum(squares[...]) * share
    for f in range(8):
        piece_out(f).wait()


LAYER_SCRATCH = 33


def kernel(
    eps,
    inv_root,
    share,
    h_ref,
    value_ref,
    out_ref,
    gain_ref,
    proj_ref,
    codes_ref,
    scale_ref,
    perm_ref,
    grad_ref,
    loss_ref,
    held,
    store_ref,
    proj,
    proj_sem,
    *scratch,
):
    core = lax.rem(lax.axis_index("dp"), 2)
    rows = held.shape[1] // 2
    fetch_proj = pltpu.make_async_copy(proj_ref, proj, proj_sem)
    fetch_proj.start()
    codes_in, codes_out, sends_out = run_layers(
        eps,
        h_ref,
        value_ref,
        out_ref,
        gain_ref,
        codes_ref,
        scale_ref,
        held.at[0, pl.ds(pl.multiple_of(core * rows, rows), rows)],
        store_ref,
        *scratch[:LAYER_SCRATCH],
    )
    fetch_proj.wait()
    run_wide(
        inv_root,
        share,
        codes_in,
        codes_out,
        sends_out,
        store_ref,
        perm_ref,
        proj,
        grad_ref,
        loss_ref,
        held,
        *scratch[LAYER_SCRATCH:],
    )


def distill(hidden, value_weight, folded_out, gain, proj, codes, scales, perm):
    rows, features = hidden.shape
    head = value_weight.shape[1]
    columns = proj.shape[1]
    quarter = columns // 4
    tokens = rows * RANKS
    block = 2 * rows
    wide_half = block // 2
    grid = (4, SIDE, SIDE, 2)
    value_weight = value_weight.reshape(*grid, features // RANKS, head)
    folded_out = folded_out.reshape(*grid[1:], head // RANKS, 4 * features)
    bf16, f32 = jnp.bfloat16, jnp.float32
    dma = pltpu.SemaphoreType.DMA
    message = pltpu.VMEM((4, 2, 4, rows // 8, head + LANES), bf16)
    lanes = (features // LANES, LANES)
    layer_scratch = [
        pltpu.VMEM((*grid, features // RANKS, head), bf16),
        pltpu.VMEM((*grid, head // RANKS, features), bf16),
        pltpu.VMEM(gain.shape, bf16),
        pltpu.VMEM((4, *lanes), bf16),
        pltpu.VMEM((4, *lanes), bf16),
        pltpu.VMEM(scales.shape, bf16),
        pltpu.VMEM((rows, head + LANES), f32),
        pltpu.VMEM((rows, features), bf16),
        pltpu.VMEM((rows, head), bf16),
        message,
        message,
        message,
        message,
        pltpu.VMEM((RANKS, rows, LANES), bf16),
        dma((5,)),
        *[dma((2, 3))] * 3,
        *[dma((2, 3, SIDE))] * 6,
        dma((3,)),
        dma((3,)),
        *[dma((4, 2, 4))] * 4,
        *[dma((RANKS,))] * 3,
    ]
    wide_scratch = [
        pltpu.VMEM((8, quarter), f32),
        pltpu.VMEM((features, columns), f32),
        pltpu.VMEM((features, columns), bf16),
        dma((8,)),
        pltpu.VMEM((2, 4, block, quarter), f32),
        pltpu.VMEM((2, block, quarter), f32),
        pltpu.VMEM((CHIPS, 2, 2, wide_half, quarter), bf16),
        pltpu.VMEM((CHIPS, 2, 2, wide_half, quarter), bf16),
        pltpu.VMEM((CHIPS, 2, wide_half, quarter), bf16),
        pltpu.VMEM((CHIPS, 2, wide_half, quarter), bf16),
        pltpu.VMEM((CHIPS, 4, block, quarter), bf16),
        pltpu.VMEM((tokens, LANES), f32),
        pltpu.VMEM((block, quarter), f32),
        pltpu.VMEM((3, 2 * SIDE, 8, quarter), f32),
        dma((CHIPS, 2, 4)),
        dma((CHIPS, 2, 4)),
        dma((CHIPS,)),
        dma((CHIPS,)),
        dma((CHIPS, 2)),
        dma((CHIPS, 2)),
        dma((CHIPS, 2)),
        dma((CHIPS, 2)),
        dma((CHIPS, 2)),
        dma((CHIPS, 2)),
        dma((CHIPS, 2)),
        dma((CHIPS, 2)),
        dma((3, 2 * SIDE)),
        dma((3, 2 * SIDE)),
    ]
    smem = pl.BlockSpec(memory_space=pltpu.SMEM)
    anywhere = pl.BlockSpec(memory_space=pl.ANY)
    return pl.pallas_call(
        functools.partial(kernel, 1e-5, 1.0 / math.sqrt(tokens), 0.5 / (tokens * columns * RANKS)),
        out_shape=(
            jax.ShapeDtypeStruct((features, columns), bf16),
            jax.ShapeDtypeStruct((1, 1), f32),
        ),
        in_specs=[anywhere] * 7 + [smem],
        out_specs=(anywhere, smem),
        scratch_shapes=[
            pltpu.VMEM((CHIPS, block, features), bf16),
            pltpu.VMEM((tokens, LANES), bf16),
            pltpu.VMEM(proj.shape, bf16),
            dma,
        ]
        + layer_scratch
        + wide_scratch,
        compiler_params=pltpu.CompilerParams(
            collective_id=0, has_side_effects=True, vmem_limit_bytes=63 * 1024 * 1024
        ),
    )(hidden, value_weight, folded_out, gain, proj, codes, scales, perm)


def shards(
    student_in, value_weight, folded_out, norm_gain, proj, teacher_codes, teacher_scales, perm
):
    grad_proj, loss = distill(
        student_in,
        value_weight[0],
        folded_out[0],
        norm_gain,
        proj,
        teacher_codes,
        teacher_scales[None, :],
        perm,
    )
    return (grad_proj, loss[0, 0])


def solution(mesh):
    return jax.shard_map(
        shards,
        mesh=mesh,
        in_specs=(
            P("dp", "pipe"),
            P("pipe", None, None),
            P("pipe", None, None),
            P("pipe", None),
            P("pipe", "dp"),
            P("dp", None),
            P("dp"),
            P(),
        ),
        out_specs=(P("pipe", "dp"), P()),
        check_vma=False,
    )
```
